32 devices in a mesh: row: 2 (over y), seq: 4 (over x, core), tp: 4 (over z).
Axes of the slice: x: 2, y: 2, z: 4, core: 2. Of those that a mesh axis runs over, the one named last changes fastest.
Arguments:
- block_in: float32 [2, 4096, 1536], P('row', ('seq', 'tp')), may hold values from -6 to 6
- block_grad: float32 [2, 4096, 1536], P('row', ('seq', 'tp')), may hold values from -6 to 6
- norm_gains: float32 [4, 1536], replicated, may hold values from 0.5 to 1.5
- mixer_in: bfloat16 [1536, 2, 3072], P(None, None, 'tp'), may hold values from -0.15625 to 0.15625
- conv_taps: float32 [4, 3072], P(None, 'tp'), may hold values from -3 to 3
- conv_bias: float32 [3072], P('tp'), may hold values from -3 to 3
- state_proj: bfloat16 [3072, 128], P('tp'), may hold values from -0.109375 to 0.109375
- step_proj: bfloat16 [96, 3072], P(None, 'tp'), may hold values from -0.625 to 0.625
- step_bias: float32 [3072], P('tp'), may hold values from -4 to -1
- decay_log: float32 [16, 3072], P(None, 'tp'), may hold values from -4.6 to 2.8
- skip_gain: float32 [3072], P('tp'), may hold values from 0.5 to 1.5
- mixer_out: bfloat16 [3072, 1536], P('tp'), may hold values from -0.3125 to 0.3125
- first_in: bfloat16 [1536, 2, 4096], P(None, None, 'tp'), may hold values from -0.15625 to 0.15625
- first_out: bfloat16 [4096, 1536], P('tp'), may hold values from -0.1875 to 0.1875
- attend_in: bfloat16 [1536, 3, 1536], P(None, None, 'tp'), may hold values from -0.15625 to 0.15625
- attend_out: bfloat16 [1536, 1536], P('tp'), may hold values from -1.25 to 1.25
- second_in: bfloat16 [1536, 2, 4096], P(None, None, 'tp'), may hold values from -0.15625 to 0.15625
- second_out: bfloat16 [4096, 1536], P('tp'), may hold values from -0.1875 to 0.1875
- row_counts: int32 [2], P('row'), may hold values from 1 to 4096, as said below
- doc_starts: int32 [2, 8], P('row'), may hold values from 0 to 4095, as said below
- row_mask: int32 [2], P('row'), may hold values from 0 to 1, as said below
Outputs:
- block_out: float32 [2, 4096, 1536], P('row', ('seq', 'tp'))
- grad_in: float32 [2, 4096, 1536], P('row', ('seq', 'tp'))
- grad_norm_gains: float32 [4, 1536], replicated
- grad_mixer_in: float32 [1536, 2, 3072], P(('row', 'seq'), None, 'tp')
- grad_conv_taps: float32 [4, 3072], P(None, 'tp')
- grad_conv_bias: float32 [3072], P('tp')
- grad_state_proj: float32 [3072, 128], P('tp')
- grad_step_proj: float32 [96, 3072], P(None, 'tp')
- grad_step_bias: float32 [3072], P('tp')
- grad_decay_log: float32 [16, 3072], P(None, 'tp')
- grad_skip_gain: float32 [3072], P('tp')
- grad_mixer_out: float32 [3072, 1536], P('tp', ('row', 'seq'))
- grad_first_in: float32 [1536, 2, 4096], P(('row', 'seq'), None, 'tp')
- grad_first_out: float32 [4096, 1536], P('tp', ('row', 'seq'))
- grad_attend_in: float32 [1536, 3, 1536], P(('row', 'seq'), None, 'tp')
- grad_attend_out: float32 [1536, 1536], P('tp', ('row', 'seq'))
- grad_second_in: float32 [1536, 2, 4096], P(('row', 'seq'), None, 'tp')
- grad_second_out: float32 [4096, 1536], P('tp', ('row', 'seq'))
The draws below stay inside these ranges and needn't reach their ends.
Inputs may be any that keep to these rules, and one draw needn't show every extreme that they name: `row_counts`: in each aligned block of 1 row one row, drawn from the seed, has a count above 3072; some row has the count 4096. `doc_starts`: each row's starts are non-decreasing and begin with 0; equal starts make empty documents. In the row chosen for row_counts the second document starts within the first 1024 positions and ends after position 3072, and the last start is 4095. `row_mask`: the row chosen for row_counts in each aligned block is real; where 1 >= 2 some other row is padding.
All inputs are finite; a program needn't handle non-finite values.
Results may differ from the reference program's by a relative error of at most 0.02.
Values may be sent and summed in bfloat16 or wider, within the bound.
No kernel may reach another device: no remote copies, remote signals or barrier semaphores. Data moves between devices by JAX's collectives and lax.ppermute only.
A program may use at most 448 MiB of HBM per device.

```python
import jax
import jax.numpy as jnp
from jax import lax

D = 1536
INNER = 3072
STATE = 16
CONV = 4
RANK = 96
FF = 4096
HEADS = 12
HDIM = 128
WINDOW = 2048
ROW_LEN = 4096
ROW_DEV = 1
DOCS = 8
MBLOCK = 64
ROWS = 2
SHARD = 1024


def pick_rows(key):
    key = jax.random.fold_in(key, 11)
    which = jax.random.randint(key, (ROWS // ROW_DEV,), 0, ROW_DEV)
    place = jnp.arange(ROWS, dtype=jnp.int32) % ROW_DEV
    return (place == jnp.repeat(which, ROW_DEV)).astype(jnp.int32)


def draw_row_counts(key, part):
    chosen = pick_rows(key)
    key = jax.random.fold_in(key, 1)
    loose_key, tight_key, top_key = jax.random.split(key, 3)
    loose = jax.random.randint(loose_key, (ROWS,), 1, ROW_LEN + 1)
    tight = jax.random.randint(tight_key, (ROWS,), ROW_LEN - SHARD + 1, ROW_LEN + 1)
    counts = jnp.where(chosen == 1, tight, loose)
    top = jax.random.randint(top_key, (), 0, ROWS)
    return jnp.where(jnp.arange(ROWS) == top, ROW_LEN, counts).astype(jnp.int32)


def draw_doc_starts(key, part):
    chosen = pick_rows(key)
    key = jax.random.fold_in(key, 2)
    streams = jax.random.split(key, 4)
    loose = jnp.sort(jax.random.randint(streams[0], (ROWS, DOCS - 1), 1, ROW_LEN), axis=1)
    opening = jax.random.randint(streams[1], (ROWS, 1), 1, SHARD)
    closing = jax.random.randint(streams[2], (ROWS, 1), ROW_LEN - SHARD + 1, ROW_LEN)
    rest = jnp.sort(jnp.maximum(jax.random.randint(streams[3], (ROWS, DOCS - 3), ROW_LEN - SHARD + 1, ROW_LEN), closing), axis=1)
    tight = jnp.concatenate([opening, closing, rest], axis=1)
    tight = tight.at[:, -1].set(ROW_LEN - 1)
    starts = jnp.where(chosen[:, None] == 1, tight, loose)
    return jnp.concatenate([jnp.zeros((ROWS, 1), jnp.int32), starts], axis=1).astype(jnp.int32)


def draw_row_mask(key, part):
    chosen = pick_rows(key)
    key = jax.random.fold_in(key, 3)
    coin_key, pick_key = jax.random.split(key)
    coins = jax.random.randint(coin_key, (ROWS,), 0, 2)
    score = jnp.where(chosen == 1, -1, jax.random.randint(pick_key, (ROWS,), 0, 1 << 20))
    dropped = jnp.argmax(score).astype(jnp.int32)
    place = jnp.arange(ROWS, dtype=jnp.int32)
    mask = jnp.where((place == dropped) & (chosen == 0), 0, coins)
    return jnp.where(chosen == 1, 1, mask).astype(jnp.int32)


def steps_of(key, shape, cuts, least, top_value):
    factor_of, own = 1.0, jax.random.fold_in(key, 6)
    for dim, shards_of in cuts:
        steps = jnp.exp(jax.random.uniform(jax.random.fold_in(own, dim), (shards_of,), jnp.float32, least / len(cuts), top_value / len(cuts)))
        factor_of = factor_of * jnp.repeat(steps, shape[dim] // shards_of).reshape([-1 if axis == dim else 1 for axis in range(len(shape))])
    return factor_of


def centred(own_key, shape, spread, limit, shards=(), kind=jnp.bfloat16):
    values = jax.random.normal(own_key, shape, jnp.float32) * spread
    if len(shards) > 0:
        values = steps_of(own_key, shape, shards, -0.22, 0.18) * values
    return jnp.clip(values, min=-limit, max=limit).astype(kind)


def setup_inputs(seed: int = 0) -> dict:
    key_list = jax.random.split(jax.random.key(seed), 22)
    return {
        "block_in": centred(key_list[0], (ROWS, ROW_LEN, D), 1.0, 6.0, ((0, 2), (1, 16)), jnp.float32),
        "block_grad": centred(key_list[1], (ROWS, ROW_LEN, D), 1.0, 6.0, ((0, 2), (1, 16)), jnp.float32),
        "norm_gains": jnp.clip(1.0 + 0.1 * jax.random.normal(key_list[2], (4, D), jnp.float32), 0.5, 1.5),
        "mixer_in": centred(key_list[3], (D, 2, INNER), D ** -0.5, 0.15625, ((2, 4),)),
        "conv_taps": centred(key_list[4], (CONV, INNER), 0.5, 3.0, ((1, 4),), jnp.float32),
        "conv_bias": centred(key_list[5], (INNER,), 0.5, 3.0, ((0, 4),), jnp.float32),
        "state_proj": centred(key_list[6], (INNER, RANK + 2 * STATE), INNER ** -0.5, 0.109375, ((0, 4),)),
        "step_proj": centred(key_list[7], (RANK, INNER), RANK ** -0.5, 0.625, ((1, 4),)),
        "step_bias": jnp.clip(-4.0 + 3.0 * jax.random.uniform(key_list[8], (INNER,), jnp.float32) ** steps_of(key_list[8], (INNER,), ((0, 4),), -0.2, 0.2), -4.0, -1.0),
        "decay_log": jnp.clip(-4.6 + 7.3999998569488525 * jax.random.uniform(key_list[9], (STATE, INNER), jnp.float32) ** steps_of(key_list[9], (STATE, INNER), ((1, 4),), -0.2, 0.2), -4.6, 2.8),
        "skip_gain": jnp.clip(0.5 + 1.0 * jax.random.uniform(key_list[10], (INNER,), jnp.float32) ** steps_of(key_list[10], (INNER,), ((0, 4),), -0.2, 0.2), 0.5, 1.5),
        "mixer_out": centred(key_list[11], (INNER, D), (INNER // 8) ** -0.5, 0.3125, ((0, 4),)),
        "first_in": centred(key_list[12], (D, 2, FF), D ** -0.5, 0.15625, ((2, 4),)),
        "first_out": centred(key_list[13], (FF, D), (FF // 4) ** -0.5, 0.1875, ((0, 4),)),
        "attend_in": centred(key_list[14], (D, 3, HEADS * HDIM), D ** -0.5, 0.15625, ((2, 4),)),
        "attend_out": centred(key_list[15], (HEADS * HDIM, D), (D // 64) ** -0.5, 1.25, ((0, 4),)),
        "second_in": centred(key_list[16], (D, 2, FF), D ** -0.5, 0.15625, ((2, 4),)),
        "second_out": centred(key_list[17], (FF, D), (FF // 4) ** -0.5, 0.1875, ((0, 4),)),
        "row_counts": draw_row_counts(jax.random.fold_in(key_list[21], 71), 0),
        "doc_starts": draw_doc_starts(jax.random.fold_in(key_list[21], 71), 0),
        "row_mask": draw_row_mask(jax.random.fold_in(key_list[21], 71), 0),
    }


@jax.custom_vjp
def low(v):
    return lax.optimization_barrier(v.astype(jnp.bfloat16)).astype(jnp.float32)

@jax.custom_vjp
def low_back(v):
    return v

def low_keep(v):
    return (low(v), None)

def low_pass(kept, grad):
    return (grad,)

def back_keep(v):
    return (v, None)

def back_low(kept, grad):
    return (low(grad),)
low.defvjp(low_keep, low_pass)
low_back.defvjp(back_keep, back_low)
epsilon = 1e-05
masked_score = -1e+30
highest = lax.Precision.HIGHEST

def product(left, right):
    return jnp.dot(left, right, preferred_element_type=jnp.float32, precision=highest)

def doc_index(positions, starts):
    return lax.optimization_barrier(jnp.sum((starts[None, :] <= positions[:, None]).astype(jnp.int32), axis=1))

def rms_norm(stream, gain):
    return stream * lax.rsqrt(lax.optimization_barrier(jnp.mean(stream * stream, axis=-1, keepdims=True)) + epsilon) * gain

def state_scan(step, write_in, read_out, source, keep, rate):

    def block_run(state, items):

        def token(held, item):
            step_now, write_now, read_now, source_now, keep_now = item
            held = jnp.exp(step_now[None, :] * rate) * keep_now * held + step_now[None, :] * write_now[:, None] * source_now[None, :]
            return (held, lax.optimization_barrier(jnp.sum(read_now[:, None] * held, axis=0)))
        return lax.scan(token, state, items)
    count = ROW_LEN // MBLOCK
    items = tuple((value.reshape((count, MBLOCK) + value.shape[1:]) for value in (step, write_in, read_out, source, keep)))
    _, outputs = lax.scan(jax.checkpoint(block_run), jnp.zeros((STATE, INNER), jnp.float32), items)
    return outputs.reshape(ROW_LEN, INNER)

def mixer(normed, weights, starts, documents, keep):
    mixer_in, conv_taps, conv_bias, state_proj, step_proj, step_bias, decay_log, skip_gain, mixer_out = weights
    signal = low_back(low(product(normed, mixer_in[:, 0, :])))
    gate = low_back(product(normed, mixer_in[:, 1, :]))
    positions = jnp.arange(ROW_LEN, dtype=jnp.int32)
    padded = jnp.concatenate([jnp.zeros((CONV - 1, INNER), jnp.float32), signal], axis=0)
    conv_sum = conv_bias[None, :] + jnp.zeros_like(gate)
    for tap in range(CONV):
        anchor = positions - (CONV - 1 - tap)
        same = ((anchor >= 0) & (doc_index(anchor, starts) == documents)).astype(jnp.float32)
        conv_sum = conv_sum + conv_taps[tap][None, :] * padded[tap:tap + ROW_LEN] * same[:, None]
    inner = low(jax.nn.silu(conv_sum))
    mixed = low_back(product(inner, state_proj))
    step_low = low(mixed[:, :RANK])
    write_in = mixed[:, RANK:RANK + STATE]
    read_out = mixed[:, RANK + STATE:]
    step_raw = low_back(product(step_low, step_proj) + step_bias[None, :])
    step = jax.nn.softplus(step_raw)
    rate = -jnp.exp(decay_log)
    result = state_scan(step, write_in, read_out, inner, keep, rate) + skip_gain[None, :] * inner
    gated = low(result * jax.nn.silu(gate))
    return low_back(product(gated, mixer_out))

def feed_forward(normed, weights):
    dense_in, dense_out = weights
    gate = low_back(product(normed, dense_in[:, 0, :]))
    upper = low_back(product(normed, dense_in[:, 1, :]))
    hidden = low(jax.nn.silu(gate) * upper)
    return low_back(product(hidden, dense_out))

def attention(normed, weights, documents):
    attend_in, attend_out = weights
    projected = low_back(low(product(normed, attend_in.reshape(D, 3 * HEADS * HDIM))))
    split = projected.reshape(ROW_LEN, 3, HEADS, HDIM)
    query, keys, values = (split[:, 0], split[:, 1], split[:, 2])
    keys_padded = jnp.concatenate([jnp.zeros((WINDOW, HEADS, HDIM), jnp.float32), keys], axis=0)
    values_padded = jnp.concatenate([jnp.zeros((WINDOW, HEADS, HDIM), jnp.float32), values], axis=0)
    docs_padded = jnp.concatenate([jnp.zeros((WINDOW,), jnp.int32), documents], axis=0)
    block = min(512, ROW_LEN)

    def one_block(first):
        query_blk = lax.dynamic_slice_in_dim(query, first, block, 0)
        keys_blk = lax.dynamic_slice_in_dim(keys_padded, first, block + WINDOW, 0)
        values_blk = lax.dynamic_slice_in_dim(values_padded, first, block + WINDOW, 0)
        query_place = first + jnp.arange(block, dtype=jnp.int32)
        key_place = first - WINDOW + jnp.arange(block + WINDOW, dtype=jnp.int32)
        query_doc = lax.dynamic_slice_in_dim(documents, first, block, 0)
        key_doc = lax.dynamic_slice_in_dim(docs_padded, first, block + WINDOW, 0)
        scores = low_back(jnp.einsum('qhd,khd->hqk', query_blk, keys_blk, precision=highest) * HDIM ** (-0.5))
        mask = (key_place[None, :] <= query_place[:, None]) & (query_place[:, None] - key_place[None, :] < WINDOW) & (key_place[None, :] >= 0) & (query_doc[:, None] == key_doc[None, :])
        soft = jax.nn.softmax(jnp.where(mask[None], scores, masked_score), axis=-1)
        return jnp.einsum('hqk,khd->qhd', low(soft), values_blk, precision=highest)
    firsts = jnp.arange(ROW_LEN // block, dtype=jnp.int32) * block
    attended = lax.map(jax.checkpoint(one_block), firsts).reshape(ROW_LEN, HEADS * HDIM)
    attended = low_back(low(attended))
    return low_back(product(attended, attend_out))

def layer(weights_all, stream, starts, count, alive):
    gains, mixer_weights, first_weights, attend_weights, second_weights = weights_all
    positions = jnp.arange(ROW_LEN, dtype=jnp.int32)
    documents = doc_index(positions, starts)
    keep = 1.0 - jnp.any(starts[None, :] == positions[:, None], axis=1).astype(jnp.float32)
    stream = stream + mixer(low(rms_norm(stream, gains[0])), mixer_weights, starts, documents, keep)
    stream = stream + feed_forward(low(rms_norm(stream, gains[1])), first_weights)
    stream = stream + attention(low(rms_norm(stream, gains[2])), attend_weights, documents)
    stream = stream + feed_forward(low(rms_norm(stream, gains[3])), second_weights)
    valid = ((positions < count) & (alive == 1)).astype(jnp.float32)
    return stream * valid[:, None]

def reference(block_in, block_grad, norm_gains, mixer_in, conv_taps, conv_bias, state_proj, step_proj, step_bias, decay_log, skip_gain, mixer_out, first_in, first_out, attend_in, attend_out, second_in, second_out, row_counts, doc_starts, row_mask):

    def widen(value):
        return value.astype(jnp.float32)
    weights_all = (widen(norm_gains), tuple((widen(value) for value in (mixer_in, conv_taps, conv_bias, state_proj, step_proj, step_bias, decay_log, skip_gain, mixer_out))), (widen(first_in), widen(first_out)), (widen(attend_in), widen(attend_out)), (widen(second_in), widen(second_out)))

    def per_row(total, item):
        stream, cotangent, starts, count, alive = item

        def forward(weights_now, stream_now):
            return layer(weights_now, stream_now, starts, count, alive)
        output, pullback = jax.vjp(forward, weights_all, stream)
        grad_weights, grad_stream = pullback(cotangent)
        return (jax.tree.map(lambda held, fresh: held + fresh, total, grad_weights), (output, grad_stream))
    zeros = jax.tree.map(jnp.zeros_like, weights_all)
    total, (outputs, grad_input) = lax.scan(per_row, zeros, (widen(block_in), widen(block_grad), doc_starts, row_counts, row_mask))
    gains, mixer_grads, first_grads, attend_grads, second_grads = total
    return (outputs, grad_input, gains, mixer_grads[0], mixer_grads[1], mixer_grads[2], mixer_grads[3], mixer_grads[4], mixer_grads[5], mixer_grads[6], mixer_grads[7], mixer_grads[8], first_grads[0], first_grads[1], attend_grads[0], attend_grads[1], second_grads[0], second_grads[1])
```

```python
import jax
import jax.numpy as jnp
from jax import lax
from jax.experimental import pallas as pl
from jax.experimental.pallas import tpu as pltpu
from jax.sharding import PartitionSpec as P

HDIM = 128
WINDOW = 2048
f32 = jnp.float32
LOG2E = 1.4426950408889634
FAR = 1e30


epsilon = 1e-05
masked_score = -1e30


def carried_in(value, axis, join, neutral, backward):
    count, mine = (lax.axis_size(axis), lax.axis_index(axis))
    pieces = jax.tree.map(lambda part: lax.all_gather(part, axis), value)
    if backward:
        pieces = jax.tree.map(lambda part: part[::-1], pieces)
        mine = count - 1 - mine
    total = jax.tree.map(
        lambda part, zero: jnp.full_like(part, 0) + jnp.asarray(zero, part.dtype), value, neutral
    )

    def lap(position, total):
        longer = join(total, jax.tree.map(lambda part: part[position], pieces))
        return jax.tree.map(lambda new, old: jnp.where(position < mine, new, old), longer, total)

    return lax.fori_loop(0, count - 1, lap, total)


def from_behind(x, axis, by):
    peers = lax.axis_size(axis)
    pairs = [(i, i + by) for i in range(peers) if 0 <= i + by < peers]
    return lax.ppermute(x, axis, pairs)


def chain_pair(earlier, later):
    return (earlier[0] * later[0], later[0] * earlier[1] + later[1])


def gather_rows(local):
    return lax.all_gather(local, "tp", axis=1, tiled=True)


def reduce_rows(partial_value):
    low = partial_value.astype(jnp.bfloat16)
    return lax.psum_scatter(low, "tp", scatter_dimension=1, tiled=True).astype(jnp.float32)


def channel_total(partial_value):
    return lax.psum(partial_value, "tp")


def carry_across(pair, backward):
    identity = (jnp.ones_like(pair[0]), jnp.zeros_like(pair[1]))
    return carried_in(pair, "seq", chain_pair, identity, backward)


def settle(pending, grad_weight_in, grad_weight_out):
    return pending + [(grad_weight_in, grad_weight_out)]


def doc_numbers(positions, starts):
    return jnp.sum((starts[:, None, :] <= positions[None, :, None]).astype(jnp.int32), axis=-1)


def norm_forward(stream, gain):
    scale = lax.rsqrt(jnp.mean(stream * stream, axis=-1, keepdims=True) + epsilon)
    return (stream * scale * gain, scale)


def norm_backward(stream, scale, gain, grad_normed):
    unit = stream * scale
    scaled = grad_normed * gain
    grad_gain = jnp.sum(grad_normed * unit, axis=(0, 1))
    grad_stream = scale * (scaled - unit * jnp.mean(scaled * unit, axis=-1, keepdims=True))
    return (grad_stream, grad_gain)


def silu_slope(value):
    logistic = jax.nn.sigmoid(value)
    return logistic * (1.0 + value * (1.0 - logistic))


TB = 128
VM = 48 * 1024 * 1024

def params():
    return pltpu.CompilerParams(vmem_limit_bytes=VM, dimension_semantics=("arbitrary",))

def turned(ref, b, base, tb):
    return pltpu.roll(ref[b], lax.rem(tb - base, tb), axis=1)

def ends_kernel(step_ref, push_ref, write_ref, rate_ref, end_ref):
    rows, tb = step_ref.shape[0], step_ref.shape[1]
    @pl.when(pl.program_id(0) == 0)
    def _():
        end_ref[...] = jnp.zeros_like(end_ref)
    def group(j, held):
        base = pl.multiple_of(j * 8, 8)
        held = list(held)
        for b in range(rows):
            steps = step_ref[b, pl.ds(base, 8), :]
            pushes = push_ref[b, pl.ds(base, 8), :]
            writes = turned(write_ref, b, base, tb)
            for k in range(8):
                factor = jnp.exp2(steps[k:k+1] * rate_ref[...])
                held[b] = factor * held[b] + writes[:, k:k+1] * pushes[k:k+1]
        return tuple(held)
    held = lax.fori_loop(0, tb // 8, group, tuple(end_ref[b] for b in range(rows)))
    for b in range(rows):
        end_ref[b] = held[b]

def scan_ends(step, push, write, rate):
    rows, length, chans = step.shape
    states = rate.shape[0]
    tb = min(TB, length)
    big = pl.BlockSpec((rows, tb, chans), lambda i: (0, i, 0))
    thin = pl.BlockSpec((rows, states, tb), lambda i: (0, 0, i))
    return pl.pallas_call(ends_kernel, grid=(length // tb,),
        in_specs=[big, big, thin, pl.BlockSpec((states, chans), lambda i: (0, 0))],
        out_specs=pl.BlockSpec((rows, states, chans), lambda i: (0, 0, 0)),
        out_shape=jax.ShapeDtypeStruct((rows, states, chans), f32),
        compiler_params=params())(step, push, write, rate)

def outputs_kernel(step_ref, push_ref, write_ref, read_ref, rate_ref, first_ref, out_ref, start_ref, held_ref):
    rows, tb = step_ref.shape[0], step_ref.shape[1]
    @pl.when(pl.program_id(0) == 0)
    def _():
        held_ref[...] = first_ref[...]
    start_ref[:, 0] = held_ref[...]
    def group(j, held):
        base = pl.multiple_of(j * 8, 8)
        held = list(held)
        for b in range(rows):
            steps = step_ref[b, pl.ds(base, 8), :]
            pushes = push_ref[b, pl.ds(base, 8), :]
            writes = turned(write_ref, b, base, tb)
            reads = turned(read_ref, b, base, tb)
            lines = []
            for k in range(8):
                factor = jnp.exp2(steps[k:k+1] * rate_ref[...])
                held[b] = factor * held[b] + writes[:, k:k+1] * pushes[k:k+1]
                lines.append(jnp.sum(held[b] * reads[:, k:k+1], axis=0, keepdims=True))
            out_ref[b, pl.ds(base, 8), :] = jnp.concatenate(lines, axis=0)
        return tuple(held)
    held = lax.fori_loop(0, tb // 8, group, tuple(held_ref[b] for b in range(rows)))
    for b in range(rows):
        held_ref[b] = held[b]

def scan_outputs(step, push, write, read, rate, first):
    rows, length, chans = step.shape
    states = rate.shape[0]
    tb = min(TB, length)
    big = pl.BlockSpec((rows, tb, chans), lambda i: (0, i, 0))
    thin = pl.BlockSpec((rows, states, tb), lambda i: (0, 0, i))
    whole = pl.BlockSpec((rows, states, chans), lambda i: (0, 0, 0))
    return pl.pallas_call(outputs_kernel, grid=(length // tb,),
        in_specs=[big, big, thin, thin, pl.BlockSpec((states, chans), lambda i: (0, 0)), whole],
        out_specs=[big, pl.BlockSpec((rows, 1, states, chans), lambda i: (0, i, 0, 0))],
        out_shape=[jax.ShapeDtypeStruct((rows, length, chans), f32),
                   jax.ShapeDtypeStruct((rows, length // tb, states, chans), f32)],
        scratch_shapes=[pltpu.VMEM((rows, states, chans), f32)],
        compiler_params=params())(step, push, write, read, rate, first)

def tail_kernel(step_ref, grad_ref, read_ref, rate_ref, end_ref):
    rows, tb = step_ref.shape[0], step_ref.shape[1]
    @pl.when(pl.program_id(0) == 0)
    def _():
        end_ref[...] = jnp.zeros_like(end_ref)
    def group(j, held):
        base = pl.multiple_of(tb - 8 - j * 8, 8)
        held = list(held)
        for b in range(rows):
            steps = step_ref[b, pl.ds(base, 8), :]
            grads = grad_ref[b, pl.ds(base, 8), :]
            reads = turned(read_ref, b, base, tb)
            for k in range(7, -1, -1):
                factor = jnp.exp2(steps[k:k+1] * rate_ref[...])
                held[b] = factor * (held[b] + reads[:, k:k+1] * grads[k:k+1])
        return tuple(held)
    held = lax.fori_loop(0, tb // 8, group, tuple(end_ref[b] for b in range(rows)))
    for b in range(rows):
        end_ref[b] = held[b]

def scan_tail(step, grad, read, rate):
    rows, length, chans = step.shape
    states = rate.shape[0]
    tb = min(TB, length)
    n = length // tb
    big = pl.BlockSpec((rows, tb, chans), lambda i: (0, n - 1 - i, 0))
    thin = pl.BlockSpec((rows, states, tb), lambda i: (0, 0, n - 1 - i))
    return pl.pallas_call(tail_kernel, grid=(n,),
        in_specs=[big, big, thin, pl.BlockSpec((states, chans), lambda i: (0, 0))],
        out_specs=pl.BlockSpec((rows, states, chans), lambda i: (0, 0, 0)),
        out_shape=jax.ShapeDtypeStruct((rows, states, chans), f32),
        compiler_params=params())(step, grad, read, rate)

def back_kernel(step_ref, push_ref, grad_ref, write_ref, read_ref, rate_ref, start_ref, later_ref,
                decay_ref, weight_ref, gwrite_ref, gread_ref, grate_ref, carry_ref, factor_sc, kept_sc):
    rows, tb = step_ref.shape[0], step_ref.shape[1]
    @pl.when(pl.program_id(0) == 0)
    def _():
        carry_ref[...] = later_ref[...]
        grate_ref[...] = jnp.zeros_like(grate_ref)
    def redo(j, held):
        base = pl.multiple_of(j * 8, 8)
        held = list(held)
        for b in range(rows):
            steps = step_ref[b, pl.ds(base, 8), :]
            pushes = push_ref[b, pl.ds(base, 8), :]
            writes = turned(write_ref, b, base, tb)
            for k in range(8):
                factor = jnp.exp2(steps[k:k+1] * rate_ref[...])
                kept = factor * held[b]
                factor_sc[b, base + k] = factor
                kept_sc[b, base + k] = kept
                held[b] = kept + writes[:, k:k+1] * pushes[k:k+1]
        return tuple(held)
    lax.fori_loop(0, tb // 8, redo, tuple(start_ref[b, 0] for b in range(rows)))
    lanes = lax.broadcasted_iota(jnp.int32, (1, tb), 1)
    def group(j, carried):
        base = pl.multiple_of(tb - 8 - j * 8, 8)
        carry, total = list(carried[0]), carried[1]
        for b in range(rows):
            steps = step_ref[b, pl.ds(base, 8), :]
            pushes = push_ref[b, pl.ds(base, 8), :]
            grads = grad_ref[b, pl.ds(base, 8), :]
            writes = turned(write_ref, b, base, tb)
            reads = turned(read_ref, b, base, tb)
            gwrite, gread = gwrite_ref[b], gread_ref[b]
            decays, weights = [None] * 8, [None] * 8
            for k in range(7, -1, -1):
                kept = kept_sc[b, base + k]
                adjoint = reads[:, k:k+1] * grads[k:k+1] + carry[b]
                weighted = adjoint * kept
                decays[k] = jnp.sum(weighted * rate_ref[...], axis=0, keepdims=True)
                weights[k] = jnp.sum(adjoint * writes[:, k:k+1], axis=0, keepdims=True)
                here = lanes == base + k
                gwrite = jnp.where(here, jnp.sum(adjoint * pushes[k:k+1], axis=1, keepdims=True), gwrite)
                gread = jnp.where(here, jnp.sum(kept * grads[k:k+1], axis=1, keepdims=True), gread)
                total = total + weighted * steps[k:k+1]
                carry[b] = factor_sc[b, base + k] * adjoint
            gwrite_ref[b], gread_ref[b] = gwrite, gread
            decay_ref[b, pl.ds(base, 8), :] = jnp.concatenate(decays, axis=0)
            weight_ref[b, pl.ds(base, 8), :] = jnp.concatenate(weights, axis=0)
        return (tuple(carry), total)
    gwrite_ref[...] = jnp.zeros_like(gwrite_ref)
    gread_ref[...] = jnp.zeros_like(gread_ref)
    carry, total = lax.fori_loop(0, tb // 8, group, (tuple(carry_ref[b] for b in range(rows)), grate_ref[...]))
    grate_ref[...] = total
    for b in range(rows):
        carry_ref[b] = carry[b]

def scan_back(step, push, grad, write, read, rate, starts, later):
    rows, length, chans = step.shape
    states = rate.shape[0]
    tb = min(TB, length)
    n = length // tb
    big = pl.BlockSpec((rows, tb, chans), lambda i: (0, n - 1 - i, 0))
    thin = pl.BlockSpec((rows, states, tb), lambda i: (0, 0, n - 1 - i))
    whole = pl.BlockSpec((rows, states, chans), lambda i: (0, 0, 0))
    flat = pl.BlockSpec((states, chans), lambda i: (0, 0))
    return pl.pallas_call(back_kernel, grid=(n,),
        in_specs=[big, big, big, thin, thin, flat, pl.BlockSpec((rows, 1, states, chans), lambda i: (0, n - 1 - i, 0, 0)), whole],
        out_specs=[big, big, thin, thin, flat],
        out_shape=[jax.ShapeDtypeStruct((rows, length, chans), f32)] * 2
                 + [jax.ShapeDtypeStruct((rows, states, length), f32)] * 2
                 + [jax.ShapeDtypeStruct((states, chans), f32)],
        scratch_shapes=[pltpu.VMEM((rows, states, chans), f32),
                        pltpu.VMEM((rows, tb, states, chans), f32),
                        pltpu.VMEM((rows, tb, states, chans), f32)],
        compiler_params=params())(step, push, grad, write, read, rate, starts, later)


def mixer_forward(normed, weights, same, flags):
    (
        mixer_in,
        conv_taps,
        conv_bias,
        state_proj,
        step_proj,
        step_bias,
        decay_log,
        skip_gain,
        mixer_out,
    ) = weights
    both = jnp.einsum("rtd,dce->rtce", normed, mixer_in, preferred_element_type=jnp.float32)
    signal = both[:, :, 0].astype(jnp.bfloat16)
    gate = both[:, :, 1]
    taps = conv_taps.shape[0]
    length = signal.shape[1]
    rows = signal.shape[0]
    tail = from_behind(signal[:, length - (taps - 1) :], "seq", 1)
    widened = jnp.concatenate([tail, signal], axis=1).astype(jnp.float32)
    conv_sum = conv_bias + jnp.zeros_like(gate)
    for tap in range(taps):
        conv_sum = (
            conv_sum + conv_taps[tap] * widened[:, tap : tap + length] * same[:, :, tap : tap + 1]
        )
    inner = jax.nn.silu(conv_sum).astype(jnp.bfloat16)
    source = inner.astype(jnp.float32)
    mixed = channel_total(
        jnp.einsum("rte,ec->rtc", inner, state_proj, preferred_element_type=jnp.float32)
    )
    rank = step_proj.shape[0]
    states = decay_log.shape[0]
    step_low = mixed[:, :, :rank].astype(jnp.bfloat16)
    write_in = mixed[:, :, rank : rank + states]
    read_out = mixed[:, :, rank + states :]
    step_raw = (
        jnp.einsum("rtk,ke->rte", step_low, step_proj, preferred_element_type=jnp.float32)
        + step_bias
    )
    step = jax.nn.softplus(step_raw)
    rate = -jnp.exp(decay_log)
    step_far = jnp.where(flags[:, :, None] > 0, FAR, step)
    push = step * source
    write_cols = jnp.swapaxes(write_in, 1, 2)
    read_cols = jnp.swapaxes(read_out, 1, 2)
    ends = scan_ends(step_far, push, write_cols, rate * LOG2E)
    kept = 1.0 - jnp.max(flags, axis=1)
    factors = jnp.exp(rate[None] * jnp.sum(step, axis=1)[:, None, :]) * kept[:, None, None]
    incoming = carry_across((factors, ends), False)[1]
    scanned, firsts = scan_outputs(step_far, push, write_cols, read_cols, rate * LOG2E, incoming)
    result = scanned + skip_gain * source
    gated = (result * jax.nn.silu(gate)).astype(jnp.bfloat16)
    partial_value = jnp.einsum("rte,ed->rtd", gated, mixer_out, preferred_element_type=jnp.float32)
    cache = (
        normed,
        widened,
        gate,
        conv_sum,
        inner,
        source,
        step_low,
        step_raw,
        step,
        step_far,
        push,
        write_in,
        write_cols,
        read_cols,
        result,
        gated,
        firsts,
        factors,
    )
    return (partial_value, cache)


def mixer_backward(grad_branch, cache, weights, same, flags):
    (
        mixer_in,
        conv_taps,
        conv_bias,
        state_proj,
        step_proj,
        step_bias,
        decay_log,
        skip_gain,
        mixer_out,
    ) = weights
    (
        normed,
        widened,
        gate,
        conv_sum,
        inner,
        source,
        step_low,
        step_raw,
        step,
        step_far,
        push,
        write_in,
        write_cols,
        read_cols,
        result,
        gated,
        firsts,
        factors,
    ) = cache
    grad_gated = jnp.einsum(
        "rtd,ed->rte", grad_branch, mixer_out, preferred_element_type=jnp.float32
    )
    grad_mixer_out = jnp.einsum(
        "rte,rtd->ed", gated, grad_branch, preferred_element_type=jnp.float32
    )
    grad_result = grad_gated * jax.nn.silu(gate)
    grad_gate = grad_gated * result * silu_slope(gate)
    grad_skip = jnp.sum(grad_result * source, axis=(0, 1))
    rate = -jnp.exp(decay_log)
    tail = scan_tail(step_far, grad_result, read_cols, rate * LOG2E)
    later = carry_across((factors, tail), True)[1]
    decays, weights_back, write_back, read_back, grad_rate = scan_back(
        step_far, push, grad_result, write_cols, read_cols, rate * LOG2E, firsts, later
    )
    grad_step = decays * (1.0 / LOG2E) + weights_back * source
    grad_source = weights_back * step
    grad_write = jnp.swapaxes(write_back, 1, 2)
    grad_read = jnp.swapaxes(read_back, 1, 2) + write_in * jnp.sum(
        push * grad_result, axis=2, keepdims=True
    )
    grad_source = grad_source + skip_gain * grad_result
    grad_step_raw = (grad_step * jax.nn.sigmoid(step_raw)).astype(jnp.bfloat16)
    grad_step_bias = jnp.sum(grad_step_raw.astype(jnp.float32), axis=(0, 1))
    grad_step_proj = jnp.einsum(
        "rtk,rte->ke", step_low, grad_step_raw, preferred_element_type=jnp.float32
    )
    grad_low = jnp.einsum(
        "rte,ke->rtk", grad_step_raw, step_proj, preferred_element_type=jnp.float32
    )
    grad_mixed = channel_total(jnp.concatenate([grad_low, grad_write, grad_read], axis=-1)).astype(
        jnp.bfloat16
    )
    grad_state_proj = jnp.einsum(
        "rte,rtc->ec", inner, grad_mixed, preferred_element_type=jnp.float32
    )
    grad_source = grad_source + jnp.einsum(
        "rtc,ec->rte", grad_mixed, state_proj, preferred_element_type=jnp.float32
    )
    grad_conv = grad_source * silu_slope(conv_sum)
    length = grad_conv.shape[1]
    taps = conv_taps.shape[0]
    grad_widened = jnp.zeros(widened.shape, jnp.float32)
    grad_taps = []
    for tap in range(taps):
        term = grad_conv * same[:, :, tap : tap + 1]
        grad_widened = grad_widened.at[:, tap : tap + length].add(conv_taps[tap] * term)
        grad_taps.append(jnp.sum(widened[:, tap : tap + length] * term, axis=(0, 1)))
    grad_conv_bias = jnp.sum(grad_conv, axis=(0, 1))
    returned = from_behind(grad_widened[:, : taps - 1], "seq", -1)
    grad_signal = grad_widened[:, taps - 1 :] + jnp.pad(
        returned, ((0, 0), (length - taps + 1, 0), (0, 0))
    )
    grad_both = jnp.stack([grad_signal, grad_gate], axis=2).astype(jnp.bfloat16)
    grad_mixer_in = jnp.einsum(
        "rtd,rtce->dce", normed, grad_both, preferred_element_type=jnp.float32
    )
    grad_normed = jnp.einsum(
        "rtce,dce->rtd", grad_both, mixer_in, preferred_element_type=jnp.float32
    )
    small = (
        jnp.stack(grad_taps),
        grad_conv_bias,
        grad_state_proj,
        grad_step_proj,
        grad_step_bias,
        grad_rate * rate,
        grad_skip,
    )
    return (grad_normed, grad_mixer_in, grad_mixer_out, small)


def dense_forward(normed, dense_in, dense_out):
    both = jnp.einsum("rtd,dcf->rtcf", normed, dense_in, preferred_element_type=jnp.float32)
    gate = both[:, :, 0]
    upper = both[:, :, 1]
    hidden = (jax.nn.silu(gate) * upper).astype(jnp.bfloat16)
    partial_value = jnp.einsum("rtf,fd->rtd", hidden, dense_out, preferred_element_type=jnp.float32)
    return (partial_value, (normed, gate, upper, hidden))


def dense_backward(grad_branch, cache, dense_in, dense_out):
    normed, gate, upper, hidden = cache
    grad_hidden = jnp.einsum(
        "rtd,fd->rtf", grad_branch, dense_out, preferred_element_type=jnp.float32
    )
    grad_dense_out = jnp.einsum(
        "rtf,rtd->fd", hidden, grad_branch, preferred_element_type=jnp.float32
    )
    grad_gate = grad_hidden * upper * silu_slope(gate)
    grad_upper = grad_hidden * jax.nn.silu(gate)
    grad_both = jnp.stack([grad_gate, grad_upper], axis=2).astype(jnp.bfloat16)
    grad_dense_in = jnp.einsum(
        "rtd,rtcf->dcf", normed, grad_both, preferred_element_type=jnp.float32
    )
    grad_normed = jnp.einsum(
        "rtcf,dcf->rtd", grad_both, dense_in, preferred_element_type=jnp.float32
    )
    return (grad_normed, grad_dense_in, grad_dense_out)


def window_mask(positions, documents, key_place, key_docs, first, block, span):
    query_place = positions[first : first + block]
    near = key_place[first : first + span]
    allowed = (
        (near[None, :] <= query_place[:, None])
        & (query_place[:, None] - near[None, :] < WINDOW)
        & (near[None, :] >= 0)
    )
    alike = documents[:, first : first + block, None] == key_docs[:, None, first : first + span]
    return (allowed[None] & alike)[:, None]


def block_scores(query, keys_wide, mask, first, block, span):
    scores = jnp.einsum(
        "rqhd,rkhd->rhqk",
        query[:, first : first + block],
        keys_wide[:, first : first + span],
        preferred_element_type=jnp.float32,
    ) * HDIM ** (-0.5)
    return jnp.where(mask, scores, masked_score)


def attention_forward(normed, attend_in, attend_out, positions, documents, key_place, key_docs):
    projected = jnp.einsum(
        "rtd,dch->rtch", normed, attend_in, preferred_element_type=jnp.float32
    ).astype(jnp.bfloat16)
    rows, length = (projected.shape[0], projected.shape[1])
    heads = projected.shape[3] // HDIM
    split = projected.reshape(rows, length, 3, heads, HDIM)
    query, keys, values = (split[:, :, 0], split[:, :, 1], split[:, :, 2])
    reach = key_place.shape[0] // length - 1
    fetched = []
    for back in range(1, reach + 1):
        fetched.append(from_behind((keys, values), "seq", back))
    keys_wide = jnp.concatenate([piece[0] for piece in fetched[::-1]] + [keys], axis=1)
    values_wide = jnp.concatenate([piece[1] for piece in fetched[::-1]] + [values], axis=1)
    block = min(512, length)
    span = reach * length + block
    outputs = []
    totals = []
    for first in range(0, length, block):
        mask = window_mask(positions, documents, key_place, key_docs, first, block, span)
        scores = block_scores(query, keys_wide, mask, first, block, span)
        top = jnp.max(scores, axis=-1, keepdims=True)
        log_total = top + jnp.log(jnp.sum(jnp.exp(scores - top), axis=-1, keepdims=True))
        soft = jnp.exp(scores - log_total).astype(jnp.bfloat16)
        outputs.append(
            jnp.einsum(
                "rhqk,rkhd->rqhd",
                soft,
                values_wide[:, first : first + span],
                preferred_element_type=jnp.float32,
            ).astype(jnp.bfloat16)
        )
        totals.append(log_total)
    attended = jnp.concatenate(outputs, axis=1).reshape(rows, length, heads * HDIM)
    partial_value = jnp.einsum(
        "rth,hd->rtd", attended, attend_out, preferred_element_type=jnp.float32
    )
    return (partial_value, (normed, query, keys_wide, values_wide, attended, totals))


def attention_backward(
    grad_branch, cache, attend_in, attend_out, positions, documents, key_place, key_docs
):
    normed, query, keys_wide, values_wide, attended, totals = cache
    rows, length, heads = (query.shape[0], query.shape[1], query.shape[2])
    grad_attended = (
        jnp.einsum("rtd,hd->rth", grad_branch, attend_out, preferred_element_type=jnp.float32)
        .astype(jnp.bfloat16)
        .reshape(rows, length, heads, HDIM)
    )
    grad_attend_out = jnp.einsum(
        "rth,rtd->hd", attended, grad_branch, preferred_element_type=jnp.float32
    )
    reach = keys_wide.shape[1] // length - 1
    block = min(512, length)
    span = reach * length + block
    grad_keys = jnp.zeros(keys_wide.shape, jnp.float32)
    grad_values = jnp.zeros(values_wide.shape, jnp.float32)
    query_parts = []
    for index, first in enumerate(range(0, length, block)):
        mask = window_mask(positions, documents, key_place, key_docs, first, block, span)
        scores = block_scores(query, keys_wide, mask, first, block, span)
        soft = jnp.exp(scores - totals[index])
        soft_low = soft.astype(jnp.bfloat16)
        grad_slice = grad_attended[:, first : first + block]
        grad_soft = jnp.einsum(
            "rqhd,rkhd->rhqk",
            grad_slice,
            values_wide[:, first : first + span],
            preferred_element_type=jnp.float32,
        )
        grad_values = grad_values.at[:, first : first + span].add(
            jnp.einsum("rhqk,rqhd->rkhd", soft_low, grad_slice, preferred_element_type=jnp.float32)
        )
        grad_scores = (
            soft * (grad_soft - jnp.sum(soft * grad_soft, axis=-1, keepdims=True))
        ).astype(jnp.bfloat16)
        query_parts.append(
            jnp.einsum(
                "rhqk,rkhd->rqhd",
                grad_scores,
                keys_wide[:, first : first + span],
                preferred_element_type=jnp.float32,
            )
            * HDIM ** (-0.5)
        )
        grad_keys = grad_keys.at[:, first : first + span].add(
            jnp.einsum(
                "rhqk,rqhd->rkhd",
                grad_scores,
                query[:, first : first + block],
                preferred_element_type=jnp.float32,
            )
            * HDIM ** (-0.5)
        )
    own_keys = grad_keys[:, reach * length :]
    own_values = grad_values[:, reach * length :]
    for back in range(1, reach + 1):
        start = (reach - back) * length
        returned = (
            from_behind(
                grad_keys[:, start : start + length].astype(jnp.bfloat16), "seq", -back
            ).astype(jnp.float32),
            from_behind(
                grad_values[:, start : start + length].astype(jnp.bfloat16), "seq", -back
            ).astype(jnp.float32),
        )
        own_keys = own_keys + returned[0]
        own_values = own_values + returned[1]
    grad_projected = (
        jnp.stack([jnp.concatenate(query_parts, axis=1), own_keys, own_values], axis=2)
        .astype(jnp.bfloat16)
        .reshape(rows, length, 3, heads * HDIM)
    )
    grad_attend_in = jnp.einsum(
        "rtd,rtch->dch", normed, grad_projected, preferred_element_type=jnp.float32
    )
    grad_normed = jnp.einsum(
        "rtch,dch->rtd", grad_projected, attend_in, preferred_element_type=jnp.float32
    )
    return (grad_normed, grad_attend_in, grad_attend_out)


def shards(
    block_in,
    block_grad,
    norm_gains,
    mixer_in,
    conv_taps,
    conv_bias,
    state_proj,
    step_proj,
    step_bias,
    decay_log,
    skip_gain,
    mixer_out,
    first_in,
    first_out,
    attend_in,
    attend_out,
    second_in,
    second_out,
    row_counts,
    doc_starts,
    row_mask,
):
    local_len = block_in.shape[1]
    length = local_len * lax.axis_size("tp")
    anchor = lax.axis_index("seq") * length
    positions = anchor + jnp.arange(length, dtype=jnp.int32)
    own_place = anchor + lax.axis_index("tp") * local_len + jnp.arange(local_len, dtype=jnp.int32)
    valid = ((own_place[None, :] < row_counts[:, None]) & (row_mask[:, None] == 1)).astype(
        jnp.float32
    )[:, :, None]
    documents = doc_numbers(positions, doc_starts)
    flags = jnp.any(doc_starts[:, None, :] == positions[None, :, None], axis=-1).astype(jnp.float32)
    taps = conv_taps.shape[0]
    same = jnp.stack(
        [
            (
                (positions - (taps - 1 - tap) >= 0)[None, :]
                & (doc_numbers(positions - (taps - 1 - tap), doc_starts) == documents)
            ).astype(jnp.float32)
            for tap in range(taps)
        ],
        axis=-1,
    )
    reach = -(-WINDOW // length)
    key_place = anchor - reach * length + jnp.arange((reach + 1) * length, dtype=jnp.int32)
    key_docs = doc_numbers(key_place, doc_starts)
    mixer_weights = (
        mixer_in,
        conv_taps,
        conv_bias,
        state_proj,
        step_proj,
        step_bias,
        decay_log,
        skip_gain,
        mixer_out,
    )
    normed_mix, scale_mix = norm_forward(block_in, norm_gains[0])
    partial_value, cache_mix = mixer_forward(
        gather_rows(normed_mix.astype(jnp.bfloat16)), mixer_weights, same, flags
    )
    stream_mix = block_in + reduce_rows(partial_value)
    normed_first, scale_first = norm_forward(stream_mix, norm_gains[1])
    partial_value, cache_first = dense_forward(
        gather_rows(normed_first.astype(jnp.bfloat16)), first_in, first_out
    )
    stream_first = stream_mix + reduce_rows(partial_value)
    normed_attend, scale_attend = norm_forward(stream_first, norm_gains[2])
    partial_value, cache_attend = attention_forward(
        gather_rows(normed_attend.astype(jnp.bfloat16)),
        attend_in,
        attend_out,
        positions,
        documents,
        key_place,
        key_docs,
    )
    stream_attend = stream_first + reduce_rows(partial_value)
    normed_second, scale_second = norm_forward(stream_attend, norm_gains[3])
    partial_value, cache_second = dense_forward(
        gather_rows(normed_second.astype(jnp.bfloat16)), second_in, second_out
    )
    stream_out = stream_attend + reduce_rows(partial_value)
    block_out = stream_out * valid
    grad_stream = block_grad * valid
    grad_normed, grad_second_in, grad_second_out = dense_backward(
        gather_rows(grad_stream.astype(jnp.bfloat16)), cache_second, second_in, second_out
    )
    pending = settle([], grad_second_in, grad_second_out)
    grad_back, gain_four = norm_backward(
        stream_attend, scale_second, norm_gains[3], reduce_rows(grad_normed)
    )
    grad_stream = grad_stream + grad_back
    grad_normed, grad_attend_in, grad_attend_out = attention_backward(
        gather_rows(grad_stream.astype(jnp.bfloat16)),
        cache_attend,
        attend_in,
        attend_out,
        positions,
        documents,
        key_place,
        key_docs,
    )
    pending = settle(pending, grad_attend_in, grad_attend_out)
    grad_back, gain_three = norm_backward(
        stream_first, scale_attend, norm_gains[2], reduce_rows(grad_normed)
    )
    grad_stream = grad_stream + grad_back
    grad_normed, grad_first_in, grad_first_out = dense_backward(
        gather_rows(grad_stream.astype(jnp.bfloat16)), cache_first, first_in, first_out
    )
    pending = settle(pending, grad_first_in, grad_first_out)
    grad_back, gain_two = norm_backward(
        stream_mix, scale_first, norm_gains[1], reduce_rows(grad_normed)
    )
    grad_stream = grad_stream + grad_back
    grad_normed, grad_mixer_in, grad_mixer_out, small = mixer_backward(
        gather_rows(grad_stream.astype(jnp.bfloat16)), cache_mix, mixer_weights, same, flags
    )
    pending = settle(pending, grad_mixer_in, grad_mixer_out)
    grad_back, gain_one = norm_backward(
        block_in, scale_mix, norm_gains[0], reduce_rows(grad_normed)
    )
    grad_stream = grad_stream + grad_back
    ordered = [pending[3], pending[2], pending[1], pending[0]]
    flat = tuple((member for pair in ordered for member in pair))
    flat = (
        lax.psum_scatter(
            flat[0].astype(jnp.bfloat16), ("row", "seq"), scatter_dimension=0, tiled=True
        ).astype(jnp.float32),
        lax.psum_scatter(
            flat[1].astype(jnp.bfloat16), ("row", "seq"), scatter_dimension=1, tiled=True
        ).astype(jnp.float32),
        lax.psum_scatter(
            flat[2].astype(jnp.bfloat16), ("row", "seq"), scatter_dimension=0, tiled=True
        ).astype(jnp.float32),
        lax.psum_scatter(
            flat[3].astype(jnp.bfloat16), ("row", "seq"), scatter_dimension=1, tiled=True
        ).astype(jnp.float32),
        lax.psum_scatter(
            flat[4].astype(jnp.bfloat16), ("row", "seq"), scatter_dimension=0, tiled=True
        ).astype(jnp.float32),
        lax.psum_scatter(
            flat[5].astype(jnp.bfloat16), ("row", "seq"), scatter_dimension=1, tiled=True
        ).astype(jnp.float32),
        lax.psum_scatter(
            flat[6].astype(jnp.bfloat16), ("row", "seq"), scatter_dimension=0, tiled=True
        ).astype(jnp.float32),
        lax.psum_scatter(
            flat[7].astype(jnp.bfloat16), ("row", "seq"), scatter_dimension=1, tiled=True
        ).astype(jnp.float32),
    )
    small = (
        lax.psum(small[0].astype(jnp.bfloat16), ("row", "seq")).astype(jnp.float32),
        lax.psum(small[1].astype(jnp.bfloat16), ("row", "seq")).astype(jnp.float32),
        lax.psum(small[2].astype(jnp.bfloat16), ("row", "seq")).astype(jnp.float32),
        lax.psum(small[3].astype(jnp.bfloat16), ("row", "seq")).astype(jnp.float32),
        lax.psum(small[4].astype(jnp.bfloat16), ("row", "seq")).astype(jnp.float32),
        lax.psum(small[5].astype(jnp.bfloat16), ("row", "seq")).astype(jnp.float32),
        lax.psum(small[6].astype(jnp.bfloat16), ("row", "seq")).astype(jnp.float32),
    )
    gains = lax.psum(jnp.stack([gain_one, gain_two, gain_three, gain_four]), ("row", "seq", "tp"))
    return (
        block_out,
        grad_stream,
        gains,
        flat[0],
        small[0],
        small[1],
        small[2],
        small[3],
        small[4],
        small[5],
        small[6],
        flat[1],
        flat[2],
        flat[3],
        flat[4],
        flat[5],
        flat[6],
        flat[7],
    )


def solution(mesh):
    in_specs = (
        P("row", ("seq", "tp"), None),
        P("row", ("seq", "tp"), None),
        P(),
        P(None, None, "tp"),
        P(None, "tp"),
        P("tp"),
        P("tp", None),
        P(None, "tp"),
        P("tp"),
        P(None, "tp"),
        P("tp"),
        P("tp", None),
        P(None, None, "tp"),
        P("tp", None),
        P(None, None, "tp"),
        P("tp", None),
        P(None, None, "tp"),
        P("tp", None),
        P("row"),
        P("row", None),
        P("row"),
    )
    out_specs = (
        P("row", ("seq", "tp"), None),
        P("row", ("seq", "tp"), None),
        P(),
        P(("row", "seq"), None, "tp"),
        P(None, "tp"),
        P("tp"),
        P("tp", None),
        P(None, "tp"),
        P("tp"),
        P(None, "tp"),
        P("tp"),
        P("tp", ("row", "seq")),
        P(("row", "seq"), None, "tp"),
        P("tp", ("row", "seq")),
        P(("row", "seq"), None, "tp"),
        P("tp", ("row", "seq")),
        P(("row", "seq"), None, "tp"),
        P("tp", ("row", "seq")),
    )
    return jax.shard_map(shards, mesh=mesh, in_specs=in_specs, out_specs=out_specs, check_vma=False)
```

```python
import jax
import jax.numpy as jnp
from jax import lax
from jax.experimental import pallas as pl
from jax.experimental.pallas import tpu as pltpu
from jax.sharding import PartitionSpec as P

HDIM = 128
WINDOW = 2048
f32 = jnp.float32
LOG2E = 1.4426950408889634
FAR = 1e30
QBLOCK = 256


epsilon = 1e-05
masked_score = -1e30


def carried_in(state, span, rate, axis, backward):
    count, mine = (lax.axis_size(axis), lax.axis_index(axis))
    both = jnp.concatenate([state, span[:, None, :]], axis=1)
    pieces = lax.all_gather(both, axis)
    if backward:
        mine = count - 1 - mine
    total = jnp.zeros_like(state)
    for position in range(count - 1):
        piece = pieces[count - 1 - position if backward else position]
        longer = jnp.exp(rate[None] * piece[:, -1:, :]) * total + piece[:, :-1]
        total = jnp.where(position < mine, longer, total)
    return total


def from_behind(x, axis, by):
    peers = lax.axis_size(axis)
    pairs = [(i, i + by) for i in range(peers) if 0 <= i + by < peers]
    return lax.ppermute(x, axis, pairs)


def gather_rows(local):
    return lax.all_gather(local, "tp", axis=1, tiled=True)


def reduce_rows(partial_value, event=()):
    low = after(partial_value.astype(jnp.bfloat16), event)
    return lax.psum_scatter(low, "tp", scatter_dimension=1, tiled=True).astype(jnp.float32)


def after(value, *events):
    marks = [event[(0,) * event.ndim].astype(jnp.float32) for event in jax.tree.leaves(events)]
    if not marks:
        return value
    return value + (sum(marks) * 0.0).astype(value.dtype)


def spread_sum(value, axes, kind):
    for axis in axes:
        flip = 1
        while flip < lax.axis_size(axis):
            other = partner(value.astype(kind), axis, flip)
            value = value + other.astype(value.dtype)
            flip *= 2
    return value


def partner(x, axis, flip):
    return lax.ppermute(x, axis, [(i, i ^ flip) for i in range(lax.axis_size(axis))])


def channel_total(partial_value):
    rows, count = (partial_value.shape[0], lax.axis_size("tp"))
    low = partial_value.astype(jnp.bfloat16)
    parts = lax.all_to_all(low, "tp", split_axis=1, concat_axis=0, tiled=True)
    parts = parts.reshape((count, rows) + parts.shape[1:]).astype(jnp.float32)
    total = jnp.sum(parts, axis=0).astype(jnp.bfloat16)
    return lax.all_gather(total, "tp", axis=1, tiled=True)


def plane_first(grad):
    if lax.axis_size("row") != 2:
        return (grad.astype(jnp.bfloat16),)
    held = grad.reshape((2, 2, 2, grad.shape[0] // 8) + grad.shape[1:])
    place = lax.axis_index("seq") % 2
    given = lax.dynamic_slice_in_dim(held, 1 - place, 1, axis=2).astype(jnp.bfloat16)
    kept = lax.dynamic_slice_in_dim(held, place, 1, axis=2).astype(jnp.bfloat16)
    return (given, kept)


def joined(given, kept, name, flip):
    other = partner(given, name, flip).astype(jnp.float32)
    return kept.astype(jnp.float32) + other


def plane_second(given, kept=None):
    if kept is None:
        return lax.psum_scatter(given, ("row", "seq"), scatter_dimension=0, tiled=True)
    row = lax.axis_index("row")
    held = joined(given, kept, "seq", 1).astype(jnp.bfloat16)
    given = lax.dynamic_slice_in_dim(held, 1 - row, 1, axis=0)
    held = joined(given, lax.dynamic_slice_in_dim(held, row, 1, axis=0), "row", 1)
    return held.astype(jnp.bfloat16)


def plane_third(held, event=()):
    if lax.axis_size("row") != 2:
        return held.astype(jnp.float32)
    seq = lax.axis_index("seq")
    given = after(lax.dynamic_slice_in_dim(held, 1 - seq // 2, 1, axis=1), event)
    held = joined(given, lax.dynamic_slice_in_dim(held, seq // 2, 1, axis=1), "seq", 2)
    return held.reshape(held.shape[3:])


def doc_numbers(positions, starts):
    return jnp.sum((starts[:, None, :] <= positions[None, :, None]).astype(jnp.int32), axis=-1)


def norm_forward(stream, gain):
    scale = lax.rsqrt(jnp.mean(stream * stream, axis=-1, keepdims=True) + epsilon)
    return (stream * scale * gain, scale)


def norm_backward(stream, scale, gain, grad_normed):
    unit = stream * scale
    scaled = grad_normed * gain
    return scale * (scaled - unit * jnp.mean(scaled * unit, axis=-1, keepdims=True))


def gain_share(partial_value, normed, gain):
    product = partial_value.astype(jnp.float32) * normed.astype(jnp.float32)
    return jnp.sum(product, axis=(0, 1)) / gain


def silu_slope(value):
    logistic = jax.nn.sigmoid(value)
    return logistic * (1.0 + value * (1.0 - logistic))


TB = 128
UNROLL = 64
UNROLL_BACK = 32
VM = 48 * 1024 * 1024

def cost(microseconds):
    return pl.CostEstimate(
        flops=int(microseconds * 1e9), bytes_accessed=int(microseconds * 3e6), transcendentals=0
    )


def params():
    return pltpu.CompilerParams(vmem_limit_bytes=VM, dimension_semantics=("arbitrary",))

def turned(ref, b, base, tb):
    return pltpu.roll(ref[b], lax.rem(tb - base, tb), axis=1)

def ends_kernel(step_ref, push_ref, write_ref, rate_ref, end_ref):
    rows, tb = step_ref.shape[0], step_ref.shape[1]
    @pl.when(pl.program_id(0) == 0)
    def _():
        end_ref[...] = jnp.zeros_like(end_ref)
    def group(j, held):
        base = pl.multiple_of(j * UNROLL, UNROLL)
        held = list(held)
        for b in range(rows):
            steps = step_ref[b, pl.ds(base, UNROLL), :]
            pushes = push_ref[b, pl.ds(base, UNROLL), :]
            writes = turned(write_ref, b, base, tb)
            for k in range(UNROLL):
                factor = jnp.exp2(steps[k:k+1] * rate_ref[...])
                held[b] = factor * held[b] + writes[:, k:k+1] * pushes[k:k+1]
        return tuple(held)
    held = lax.fori_loop(0, tb // UNROLL, group, tuple(end_ref[b] for b in range(rows)))
    for b in range(rows):
        end_ref[b] = held[b]

def scan_ends(step, push, write, rate):
    rows, length, chans = step.shape
    states = rate.shape[0]
    tb = min(TB, length)
    big = pl.BlockSpec((rows, tb, chans), lambda i: (0, i, 0))
    thin = pl.BlockSpec((rows, states, tb), lambda i: (0, 0, i))
    return pl.pallas_call(ends_kernel, grid=(length // tb,),
        in_specs=[big, big, thin, pl.BlockSpec((states, chans), lambda i: (0, 0))],
        out_specs=pl.BlockSpec((rows, states, chans), lambda i: (0, 0, 0)),
        out_shape=jax.ShapeDtypeStruct((rows, states, chans), f32),
        cost_estimate=cost(12), compiler_params=params())(step, push, write, rate)

def picker(tb):
    row = lax.broadcasted_iota(jnp.int32, (tb, tb * 8), 0)
    column = lax.broadcasted_iota(jnp.int32, (tb, tb * 8), 1)
    inside = (column >= row * 8) & (column < row * 8 + 8)
    return jnp.where(inside, 1.0, 0.0).astype(jnp.bfloat16)


def folded(value):
    return sum(value[i : i + 8] for i in range(0, value.shape[0], 8))


def across(value):
    return sum(value[:, i : i + 128] for i in range(0, value.shape[1], 128))


def mat(left, right, dims):
    return lax.dot_general(left, right, (dims, ((), ())), preferred_element_type=f32)


def outputs_kernel(step_ref, push_ref, write_ref, read_ref, rate_ref, first_ref, out_ref, start_ref, held_ref, part_ref):
    rows, tb = step_ref.shape[0], step_ref.shape[1]
    @pl.when(pl.program_id(0) == 0)
    def _():
        held_ref[...] = first_ref[...]
    start_ref[:, 0] = held_ref[...]
    for b in range(rows):
        def group(j, held):
            base = pl.multiple_of(j * UNROLL, UNROLL)
            steps = step_ref[b, pl.ds(base, UNROLL), :]
            pushes = push_ref[b, pl.ds(base, UNROLL), :]
            writes = turned(write_ref, b, base, tb)
            reads = turned(read_ref, b, base, tb)
            for k in range(UNROLL):
                factor = jnp.exp2(steps[k:k+1] * rate_ref[...])
                held = factor * held + writes[:, k:k+1] * pushes[k:k+1]
                part_ref[pl.ds(pl.multiple_of((base + k) * 8, 8), 8), :] = folded(held * reads[:, k:k+1])
            return held
        held_ref[b] = lax.fori_loop(0, tb // UNROLL, group, held_ref[b])
        high = part_ref[...].astype(jnp.bfloat16)
        low = (part_ref[...] - high.astype(f32)).astype(jnp.bfloat16)
        out_ref[b] = mat(picker(tb), high, ((1,), (0,))) + mat(picker(tb), low, ((1,), (0,)))

def scan_outputs(step, push, write, read, rate, first):
    rows, length, chans = step.shape
    states = rate.shape[0]
    tb = min(TB, length)
    big = pl.BlockSpec((rows, tb, chans), lambda i: (0, i, 0))
    thin = pl.BlockSpec((rows, states, tb), lambda i: (0, 0, i))
    whole = pl.BlockSpec((rows, states, chans), lambda i: (0, 0, 0))
    return pl.pallas_call(outputs_kernel, grid=(length // tb,),
        in_specs=[big, big, thin, thin, pl.BlockSpec((states, chans), lambda i: (0, 0)), whole],
        out_specs=[big, pl.BlockSpec((rows, 1, states, chans), lambda i: (0, i, 0, 0))],
        out_shape=[jax.ShapeDtypeStruct((rows, length, chans), f32),
                   jax.ShapeDtypeStruct((rows, length // tb, states, chans), f32)],
        scratch_shapes=[pltpu.VMEM((rows, states, chans), f32), pltpu.VMEM((tb * 8, chans), f32)],
        cost_estimate=cost(21), compiler_params=params())(step, push, write, read, rate, first)

def tail_kernel(step_ref, grad_ref, read_ref, rate_ref, end_ref):
    rows, tb = step_ref.shape[0], step_ref.shape[1]
    @pl.when(pl.program_id(0) == 0)
    def _():
        end_ref[...] = jnp.zeros_like(end_ref)
    def group(j, held):
        base = pl.multiple_of(tb - UNROLL - j * UNROLL, UNROLL)
        held = list(held)
        for b in range(rows):
            steps = step_ref[b, pl.ds(base, UNROLL), :]
            grads = grad_ref[b, pl.ds(base, UNROLL), :]
            reads = turned(read_ref, b, base, tb)
            for k in range(UNROLL - 1, -1, -1):
                factor = jnp.exp2(steps[k:k+1] * rate_ref[...])
                held[b] = factor * (held[b] + reads[:, k:k+1] * grads[k:k+1])
        return tuple(held)
    held = lax.fori_loop(0, tb // UNROLL, group, tuple(end_ref[b] for b in range(rows)))
    for b in range(rows):
        end_ref[b] = held[b]

def scan_tail(step, grad, read, rate):
    rows, length, chans = step.shape
    states = rate.shape[0]
    tb = min(TB, length)
    n = length // tb
    big = pl.BlockSpec((rows, tb, chans), lambda i: (0, n - 1 - i, 0))
    thin = pl.BlockSpec((rows, states, tb), lambda i: (0, 0, n - 1 - i))
    return pl.pallas_call(tail_kernel, grid=(n,),
        in_specs=[big, big, thin, pl.BlockSpec((states, chans), lambda i: (0, 0))],
        out_specs=pl.BlockSpec((rows, states, chans), lambda i: (0, 0, 0)),
        out_shape=jax.ShapeDtypeStruct((rows, states, chans), f32),
        cost_estimate=cost(12), compiler_params=params())(step, grad, read, rate)

def back_kernel(step_ref, push_ref, grad_ref, write_ref, read_ref, rate_ref, start_ref, later_ref,
                decay_ref, weight_ref, gwrite_ref, gread_ref, grate_ref,
                carry_ref, factor_sc, kept_sc, decay_sc, weight_sc, gwrite_sc, gread_sc):
    rows, tb = step_ref.shape[0], step_ref.shape[1]
    states = rate_ref.shape[0]
    @pl.when(pl.program_id(0) == 0)
    def _():
        carry_ref[...] = later_ref[...]
        grate_ref[...] = jnp.zeros_like(grate_ref)
    for b in range(rows):
        def redo(j, held):
            base = pl.multiple_of(j * UNROLL, UNROLL)
            steps = step_ref[b, pl.ds(base, UNROLL), :]
            pushes = push_ref[b, pl.ds(base, UNROLL), :]
            writes = turned(write_ref, b, base, tb)
            for k in range(UNROLL):
                factor = jnp.exp2(steps[k:k+1] * rate_ref[...])
                kept = factor * held
                factor_sc[base + k] = factor
                kept_sc[base + k] = kept
                held = kept + writes[:, k:k+1] * pushes[k:k+1]
            return held
        lax.fori_loop(0, tb // UNROLL, redo, start_ref[b, 0])
        def group(j, carried):
            carry, total = carried
            base = pl.multiple_of(tb - UNROLL_BACK - j * UNROLL_BACK, UNROLL_BACK)
            steps = step_ref[b, pl.ds(base, UNROLL_BACK), :]
            pushes = push_ref[b, pl.ds(base, UNROLL_BACK), :]
            grads = grad_ref[b, pl.ds(base, UNROLL_BACK), :]
            writes = turned(write_ref, b, base, tb)
            reads = turned(read_ref, b, base, tb)
            for k in range(UNROLL_BACK - 1, -1, -1):
                kept = kept_sc[base + k]
                adjoint = reads[:, k:k+1] * grads[k:k+1] + carry
                carry = factor_sc[base + k] * adjoint
                weighted = adjoint * kept
                total = total + weighted * steps[k:k+1]
                eight = pl.ds(pl.multiple_of((base + k) * 8, 8), 8)
                decay_sc[eight, :] = folded(weighted * rate_ref[...])
                weight_sc[eight, :] = folded(adjoint * writes[:, k:k+1])
                wide = pl.ds(pl.multiple_of((base + k) * states, states), states)
                gwrite_sc[wide, :] = across(adjoint * pushes[k:k+1])
                gread_sc[wide, :] = across(kept * grads[k:k+1])
            return (carry, total)
        carry, total = lax.fori_loop(0, tb // UNROLL_BACK, group, (carry_ref[b], grate_ref[...]))
        grate_ref[...] = total
        carry_ref[b] = carry
        pick = picker(tb)
        decay_ref[b] = mat(pick, decay_sc[...].astype(jnp.bfloat16), ((1,), (0,)))
        weight_ref[b] = mat(pick, weight_sc[...].astype(jnp.bfloat16), ((1,), (0,)))
        ones = jnp.ones((8, 128), jnp.bfloat16)
        gwrite_ref[b] = mat(ones, gwrite_sc[...].astype(jnp.bfloat16), ((1,), (1,)))[:1]
        gread_ref[b] = mat(ones, gread_sc[...].astype(jnp.bfloat16), ((1,), (1,)))[:1]

def scan_back(step, push, grad, write, read, rate, starts, later):
    rows, length, chans = step.shape
    states = rate.shape[0]
    tb = min(TB, length)
    n = length // tb
    big = pl.BlockSpec((rows, tb, chans), lambda i: (0, n - 1 - i, 0))
    thin = pl.BlockSpec((rows, states, tb), lambda i: (0, 0, n - 1 - i))
    line = pl.BlockSpec((rows, 1, tb * states), lambda i: (0, 0, n - 1 - i))
    whole = pl.BlockSpec((rows, states, chans), lambda i: (0, 0, 0))
    flat = pl.BlockSpec((states, chans), lambda i: (0, 0))
    return pl.pallas_call(back_kernel, grid=(n,),
        in_specs=[big, big, big, thin, thin, flat, pl.BlockSpec((rows, 1, states, chans), lambda i: (0, n - 1 - i, 0, 0)), whole],
        out_specs=[big, big, line, line, flat],
        out_shape=[jax.ShapeDtypeStruct((rows, length, chans), f32)] * 2
                 + [jax.ShapeDtypeStruct((rows, 1, length * states), f32)] * 2
                 + [jax.ShapeDtypeStruct((states, chans), f32)],
        scratch_shapes=[pltpu.VMEM((rows, states, chans), f32),
                        pltpu.VMEM((tb, states, chans), f32),
                        pltpu.VMEM((tb, states, chans), f32),
                        pltpu.VMEM((tb * 8, chans), f32),
                        pltpu.VMEM((tb * 8, chans), f32),
                        pltpu.VMEM((tb * states, 128), f32),
                        pltpu.VMEM((tb * states, 128), f32)],
        cost_estimate=cost(46), compiler_params=params())(step, push, grad, write, read, rate, starts, later)


def mixer_forward(normed, weights, same, flags):
    (
        mixer_in,
        conv_taps,
        conv_bias,
        state_proj,
        step_proj,
        step_bias,
        decay_log,
        skip_gain,
        mixer_out,
    ) = weights
    both = jnp.einsum("rtd,dce->rtce", normed, mixer_in, preferred_element_type=jnp.float32)
    signal = both[:, :, 0].astype(jnp.bfloat16)
    gate = both[:, :, 1]
    taps = conv_taps.shape[0]
    length = signal.shape[1]
    rows = signal.shape[0]
    tail = from_behind(signal[:, length - (taps - 1) :], "seq", 1)
    widened = jnp.concatenate([tail, signal], axis=1).astype(jnp.float32)
    conv_sum = conv_bias + jnp.zeros_like(gate)
    for tap in range(taps):
        conv_sum = (
            conv_sum + conv_taps[tap] * widened[:, tap : tap + length] * same[:, :, tap : tap + 1]
        )
    inner = jax.nn.silu(conv_sum).astype(jnp.bfloat16)
    source = inner.astype(jnp.float32)
    mixed = channel_total(
        jnp.einsum("rte,ec->rtc", inner, state_proj, preferred_element_type=jnp.float32)
    )
    rank = step_proj.shape[0]
    states = decay_log.shape[0]
    step_low = mixed[:, :, :rank]
    write_in = mixed[:, :, rank : rank + states].astype(jnp.float32)
    read_out = mixed[:, :, rank + states :].astype(jnp.float32)
    step_raw = (
        jnp.einsum("rtk,ke->rte", step_low, step_proj, preferred_element_type=jnp.float32)
        + step_bias
    )
    step = jax.nn.softplus(step_raw)
    rate = -jnp.exp(decay_log)
    step_far = jnp.where(flags[:, :, None] > 0, FAR, step)
    push = step * source
    write_cols = jnp.swapaxes(write_in, 1, 2)
    read_cols = jnp.swapaxes(read_out, 1, 2)
    ends = scan_ends(step_far, push, write_cols, rate * LOG2E)
    span = jnp.where(jnp.max(flags, axis=1)[:, None] > 0, FAR, jnp.sum(step, axis=1))
    incoming = carried_in(ends, span, rate, "seq", False)
    scanned, firsts = scan_outputs(
        step_far, push, write_cols, read_cols, rate * LOG2E, incoming
    )
    result = scanned + skip_gain * source
    gated = (result * jax.nn.silu(gate)).astype(jnp.bfloat16)
    partial_value = jnp.einsum("rte,ed->rtd", gated, mixer_out, preferred_element_type=jnp.float32)
    cache = (
        normed,
        widened,
        gate,
        conv_sum,
        inner,
        source,
        step_low,
        step_raw,
        step,
        step_far,
        push,
        write_in,
        write_cols,
        read_cols,
        result,
        gated,
        firsts,
        span,
    )
    return (partial_value, cache)


def mixer_backward(grad_branch, cache, weights, same, flags, first):
    (
        mixer_in,
        conv_taps,
        conv_bias,
        state_proj,
        step_proj,
        step_bias,
        decay_log,
        skip_gain,
        mixer_out,
    ) = weights
    (
        normed,
        widened,
        gate,
        conv_sum,
        inner,
        source,
        step_low,
        step_raw,
        step,
        step_far,
        push,
        write_in,
        write_cols,
        read_cols,
        result,
        gated,
        firsts,
        span,
    ) = cache
    grad_gated = jnp.einsum(
        "rtd,ed->rte", grad_branch, mixer_out, preferred_element_type=jnp.float32
    )
    grad_mixer_out = jnp.einsum(
        "rtd,rte->de", grad_branch, gated, preferred_element_type=jnp.float32
    )
    first_out = plane_first(grad_mixer_out)
    grad_gated = after(grad_gated, first)
    grad_result = grad_gated * jax.nn.silu(gate)
    grad_gate = grad_gated * result * silu_slope(gate)
    grad_skip = jnp.sum(grad_result * source, axis=(0, 1))
    rate = -jnp.exp(decay_log)
    early = after(rate * LOG2E, first_out[0])
    tail = scan_tail(step_far, grad_result, read_cols, early)
    second_out = plane_second(*first_out)
    first = [plane_third(held, tail) for held in first]
    later = carried_in(tail, span, rate, "seq", True)
    early = after(rate * LOG2E, second_out)
    decays, weights_back, write_back, read_back, grad_rate = scan_back(
        step_far, push, grad_result, write_cols, read_cols, early, firsts, later
    )
    grad_mixer_out = plane_third(second_out, grad_rate)
    grad_step = decays * (1.0 / LOG2E) + weights_back * source
    grad_source = weights_back * step
    grad_write = write_back.reshape(write_in.shape)
    grad_read = read_back.reshape(write_in.shape) + write_in * jnp.sum(
        push * grad_result, axis=2, keepdims=True
    )
    grad_source = grad_source + skip_gain * grad_result
    grad_step_raw = (grad_step * jax.nn.sigmoid(step_raw)).astype(jnp.bfloat16)
    grad_step_bias = jnp.sum(grad_step_raw.astype(jnp.float32), axis=(0, 1))
    grad_step_proj = jnp.einsum(
        "rtk,rte->ke", step_low, grad_step_raw, preferred_element_type=jnp.float32
    )
    grad_low = jnp.einsum(
        "rte,ke->rtk", grad_step_raw, step_proj, preferred_element_type=jnp.float32
    )
    grad_mixed = channel_total(
        jnp.concatenate([after(grad_low, first), grad_write, grad_read], axis=-1)
    )
    grad_state_proj = jnp.einsum(
        "rte,rtc->ce", inner, grad_mixed, preferred_element_type=jnp.float32
    )
    grad_source = grad_source + jnp.einsum(
        "rtc,ec->rte", grad_mixed, state_proj, preferred_element_type=jnp.float32
    )
    grad_conv = grad_source * silu_slope(conv_sum)
    length = grad_conv.shape[1]
    taps = conv_taps.shape[0]
    reach = taps - 1
    terms = [grad_conv * same[:, :, tap : tap + 1] for tap in range(taps)]
    grad_taps = [
        jnp.sum(widened[:, tap : tap + length] * terms[tap], axis=(0, 1)) for tap in range(taps)
    ]
    grad_conv_bias = jnp.sum(grad_conv, axis=(0, 1))
    heads = [conv_taps[tap] * terms[tap][:, :reach] for tap in range(taps)]
    head = sum(
        jnp.pad(heads[tap][:, : reach - tap], ((0, 0), (tap, 0), (0, 0))) for tap in range(reach)
    )
    returned = from_behind(head, "seq", -1)
    grad_signal = jnp.pad(returned, ((0, 0), (length - reach, 0), (0, 0)))
    for tap in range(taps):
        shift = reach - tap
        grad_signal = grad_signal + conv_taps[tap] * jnp.pad(
            terms[tap][:, shift:], ((0, 0), (0, shift), (0, 0))
        )
    grad_both = jnp.stack([grad_signal, grad_gate], axis=2).astype(jnp.bfloat16)
    grad_mixer_in = jnp.einsum(
        "rtd,rtce->dce", normed, grad_both, preferred_element_type=jnp.float32
    )
    grad_normed = jnp.einsum(
        "rtce,dce->rtd", grad_both, mixer_in, preferred_element_type=jnp.float32
    )
    small = (
        jnp.stack(grad_taps),
        grad_conv_bias[None],
        grad_state_proj,
        grad_step_proj,
        grad_step_bias[None],
        grad_rate * rate,
        grad_skip[None],
    )
    return (grad_normed, grad_mixer_in, grad_mixer_out, small, first)


def dense_forward(normed, dense_in, dense_out):
    both = jnp.einsum("rtd,dcf->rtcf", normed, dense_in, preferred_element_type=jnp.float32)
    gate = both[:, :, 0]
    upper = both[:, :, 1]
    hidden = (jax.nn.silu(gate) * upper).astype(jnp.bfloat16)
    partial_value = jnp.einsum("rtf,fd->rtd", hidden, dense_out, preferred_element_type=jnp.float32)
    return (partial_value, (normed, gate, upper, hidden))


def dense_backward(grad_branch, cache, dense_in, dense_out, event=()):
    normed, gate, upper, hidden = cache
    grad_hidden = jnp.einsum(
        "rtd,fd->rtf", grad_branch, dense_out, preferred_element_type=jnp.float32
    )
    grad_hidden = after(grad_hidden, event)
    grad_gate = grad_hidden * upper * silu_slope(gate)
    grad_upper = grad_hidden * jax.nn.silu(gate)
    grad_both = jnp.stack([grad_gate, grad_upper], axis=2).astype(jnp.bfloat16)
    grad_normed = jnp.einsum(
        "rtcf,dcf->rtd", grad_both, dense_in, preferred_element_type=jnp.float32
    )
    grad_dense_out = jnp.einsum(
        "rtd,rtf->df", grad_branch, hidden, preferred_element_type=jnp.float32
    )
    grad_dense_in = jnp.einsum(
        "rtd,rtcf->dcf", normed, grad_both, preferred_element_type=jnp.float32
    )
    return (grad_normed, [plane_first(grad_dense_in), plane_first(grad_dense_out)])


def plan_of(length):
    block = min(QBLOCK, length)
    return (block, (WINDOW + block) // block)


def lower_edge(info_ref, row, first, block):
    lane = lax.broadcasted_iota(jnp.int32, (1, block), 1)
    place = info_ref[row, 0] + first + lane
    start = jnp.zeros((1, block), jnp.int32)
    for index in range(1, info_ref.shape[1]):
        entry = info_ref[row, index]
        start = jnp.maximum(start, jnp.where(entry <= place, entry, 0))
    return (jnp.maximum(lane + 1, start - (info_ref[row, 0] + first - WINDOW)), lane)


def piece_mask(low, lane, piece, block, pieces):
    index = piece * block + lax.broadcasted_iota(jnp.int32, (block, block), 0)
    allowed = index >= low
    if piece == pieces - 1:
        allowed = allowed & (index <= lane + WINDOW)
    return allowed


NT = (((1,), (1,)), ((), ()))
TN = (((0,), (0,)), ((), ()))
NN = (((1,), (0,)), ((), ()))


def dot(left, right, dims):
    return lax.dot_general(left, right, dims, preferred_element_type=f32)


def attend_kernel(heads, pieces, skip, info_ref, query_ref, key_ref, value_ref, out_ref, total_ref, held):
    block = query_ref.shape[1]
    first = pl.multiple_of(pl.program_id(1) * block, block)
    low, lane = lower_edge(info_ref, pl.program_id(0) // heads, first, block)
    query = query_ref[0]
    top = jnp.full((1, block), masked_score, f32)
    for piece in range(pieces):
        at = pl.ds(pl.multiple_of(first + skip + piece * block, block), block)
        scores = dot(key_ref[0, at, :], query, NT)
        scores = jnp.where(piece_mask(low, lane, piece, block, pieces), scores, masked_score)
        held[piece] = scores
        top = jnp.maximum(top, jnp.max(scores, axis=0, keepdims=True))
    slope = HDIM ** (-0.5) * LOG2E
    total = jnp.zeros((1, block), f32)
    summed = jnp.zeros((HDIM, block), f32)
    for piece in range(pieces):
        at = pl.ds(pl.multiple_of(first + skip + piece * block, block), block)
        soft = jnp.exp2((held[piece] - top) * slope)
        total = total + jnp.sum(soft, axis=0, keepdims=True)
        summed = summed + dot(value_ref[0, at, :], soft.astype(jnp.bfloat16), TN)
    out_ref[0] = (summed / total).T.astype(jnp.bfloat16)
    total_ref[0] = top * slope + jnp.log2(total)


def attend(info, query, wide, head):
    rows, length, reach = (query.shape[0], query.shape[1], wide.shape[1])
    block, pieces = plan_of(length)
    skip = reach - length - WINDOW
    body = lambda *refs: attend_kernel(1, pieces, skip, *refs)
    return pl.pallas_call(
        body,
        grid=(rows, length // block),
        in_specs=[
            pl.BlockSpec(memory_space=pltpu.SMEM),
            pl.BlockSpec((1, block, HDIM), lambda i, j: (i, j, head)),
            pl.BlockSpec((1, reach, HDIM), lambda i, j: (i, 0, 0)),
            pl.BlockSpec((1, reach, HDIM), lambda i, j: (i, 0, 1)),
        ],
        out_specs=[
            pl.BlockSpec((1, block, HDIM), lambda i, j: (i, j, 0)),
            pl.BlockSpec((1, 1, block), lambda i, j: (i, 0, j)),
        ],
        out_shape=[
            jax.ShapeDtypeStruct((rows, length, HDIM), jnp.bfloat16),
            jax.ShapeDtypeStruct((rows, 1, length), f32),
        ],
        scratch_shapes=[pltpu.VMEM((pieces, block, block), f32)],
        cost_estimate=cost(7),
        compiler_params=pltpu.CompilerParams(vmem_limit_bytes=VM),
    )(info, query, wide, wide)


def attend_back_kernel(
    heads, pieces, skip, info_ref, query_ref, grad_ref, key_ref, value_ref, total_ref, delta_ref,
    gquery_ref, gkey_ref, gvalue_ref,
):
    block = query_ref.shape[1]
    first = pl.multiple_of(pl.program_id(1) * block, block)
    low, lane = lower_edge(info_ref, pl.program_id(0) // heads, first, block)

    @pl.when(pl.program_id(1) == 0)
    def _():
        gkey_ref[...] = jnp.zeros_like(gkey_ref)
        gvalue_ref[...] = jnp.zeros_like(gvalue_ref)

    query, grad = (query_ref[0], grad_ref[0])
    total, delta = (total_ref[0], delta_ref[0])
    slope = HDIM ** (-0.5) * LOG2E
    summed = jnp.zeros((HDIM, block), f32)
    for piece in range(pieces):
        at = pl.ds(pl.multiple_of(first + skip + piece * block, block), block)
        keys = key_ref[0, at, :]
        scores = dot(keys, query, NT)
        allowed = piece_mask(low, lane, piece, block, pieces)
        soft = jnp.exp2(jnp.where(allowed, scores * slope - total, masked_score))
        gvalue_ref[0, at, :] += dot(soft.astype(jnp.bfloat16), grad, NN)
        spread = soft * (dot(value_ref[0, at, :], grad, NT) - delta)
        spread = spread.astype(jnp.bfloat16)
        gkey_ref[0, at, :] += dot(spread, query, NN)
        summed = summed + dot(keys, spread, TN)
    gquery_ref[0] = (summed * HDIM ** (-0.5)).T


def attend_back(info, query, grad, wide, total, delta, head):
    rows, length, reach = (query.shape[0], query.shape[1], wide.shape[1])
    block, pieces = plan_of(length)
    skip = reach - length - WINDOW
    body = lambda *refs: attend_back_kernel(1, pieces, skip, *refs)
    narrow = pl.BlockSpec((1, block, HDIM), lambda i, j: (i, j, head))
    line = pl.BlockSpec((1, 1, block), lambda i, j: (i, 0, j))
    tall = pl.BlockSpec((1, reach, HDIM), lambda i, j: (i, 0, 0))
    return pl.pallas_call(
        body,
        grid=(rows, length // block),
        in_specs=[
            pl.BlockSpec(memory_space=pltpu.SMEM),
            narrow,
            narrow,
            tall,
            pl.BlockSpec((1, reach, HDIM), lambda i, j: (i, 0, 1)),
            line,
            line,
        ],
        out_specs=[pl.BlockSpec((1, block, HDIM), lambda i, j: (i, j, 0)), tall, tall],
        out_shape=[
            jax.ShapeDtypeStruct((rows, length, HDIM), f32),
            jax.ShapeDtypeStruct((rows, reach, HDIM), f32),
            jax.ShapeDtypeStruct((rows, reach, HDIM), f32),
        ],
        cost_estimate=cost(12),
        compiler_params=pltpu.CompilerParams(vmem_limit_bytes=VM),
    )(info, query, grad, wide, wide, total, delta)


def by_head(attend_in):
    features, heads = (attend_in.shape[0], attend_in.shape[2] // HDIM)
    split = attend_in.reshape(features, 3, heads, HDIM)
    pairs = jnp.swapaxes(split[:, 1:], 1, 2).reshape(features, 2 * heads * HDIM)
    return (attend_in[:, 0], pairs)


def attention_forward(normed, attend_in, attend_out, info):
    heads = attend_in.shape[2] // HDIM
    weight_query, weight_pairs = by_head(attend_in)
    pairs = jnp.einsum(
        "rtd,dh->rth", normed, weight_pairs, preferred_element_type=jnp.float32
    ).astype(jnp.bfloat16)
    query = jnp.einsum(
        "rtd,dh->rth", normed, weight_query, preferred_element_type=jnp.float32
    ).astype(jnp.bfloat16)
    odd = lax.axis_index("seq") % 2 == 1
    wides, results = ([], [])
    for head in range(heads):
        own = pairs[:, :, 2 * head * HDIM : 2 * (head + 1) * HDIM]
        seconds = from_behind(own, "seq", 2)
        firsts = partner(jnp.where(odd, seconds, own), "seq", 1)
        wides.append(jnp.concatenate([seconds, firsts, own], axis=1))
        results.append(attend(info, query, wides[head], head))
    attended = jnp.concatenate([result[0] for result in results], axis=2)
    totals = [result[1] for result in results]
    partial_value = jnp.einsum(
        "rth,hd->rtd", attended, attend_out, preferred_element_type=jnp.float32
    )
    return (partial_value, (normed, query, wides, attended, totals, weight_query, weight_pairs))


def attention_backward(grad_branch, cache, attend_in, attend_out, info, event):
    normed, query, wides, attended, totals, weight_query, weight_pairs = cache
    rows, length = (query.shape[0], query.shape[1])
    heads = query.shape[2] // HDIM
    grad_attended = jnp.einsum(
        "rtd,hd->rth", grad_branch, attend_out, preferred_element_type=jnp.float32
    )
    grad_attended = after(grad_attended, event).astype(jnp.bfloat16)
    grad_attend_out = jnp.einsum(
        "rtd,rth->dh", grad_branch, attended, preferred_element_type=jnp.float32
    )
    both = grad_attended.astype(jnp.float32) * attended.astype(jnp.float32)
    delta = jnp.sum(both.reshape(rows, length, heads, HDIM), axis=-1)
    odd = lax.axis_index("seq") % 2 == 1
    queries, pairs, marks = ([], [], [[], []])
    for head in range(heads):
        grad_query, grad_keys, grad_values = attend_back(
            after(info, marks[head]),
            query,
            grad_attended,
            wides[head],
            totals[head],
            delta[:, :, head].reshape(rows, 1, length),
            head,
        )
        queries.append(grad_query)
        scaled = jnp.concatenate([grad_keys * HDIM ** (-0.5), grad_values], axis=2)
        seconds, firsts, own = (scaled[:, i * length : (i + 1) * length] for i in range(3))
        given = partner(firsts.astype(jnp.bfloat16), "seq", 1).astype(jnp.float32)
        sent = (seconds + jnp.where(odd, given, 0.0)).astype(jnp.bfloat16)
        marks.append(sent)
        back = from_behind(sent, "seq", -2)
        pairs.append(own + jnp.where(odd, 0.0, given) + back.astype(jnp.float32))
    grad_projected = jnp.concatenate(queries + pairs, axis=2).astype(jnp.bfloat16)
    grad_weight = jnp.einsum(
        "rtd,rth->dh", normed, grad_projected, preferred_element_type=jnp.float32
    )
    flat = jnp.concatenate([weight_query, weight_pairs], axis=1)
    grad_normed = jnp.einsum(
        "rth,dh->rtd", grad_projected, flat, preferred_element_type=jnp.float32
    )
    return (grad_normed, [plane_first(grad_weight), plane_first(grad_attend_out)])


def in_order(grad_weight, heads):
    features = grad_weight.shape[0]
    query = grad_weight[:, : heads * HDIM].reshape(features, 1, heads, HDIM)
    pairs = grad_weight[:, heads * HDIM :].reshape(features, heads, 2, HDIM)
    both = jnp.concatenate([query, jnp.swapaxes(pairs, 1, 2)], axis=1)
    return both.reshape(features, 3, heads * HDIM)


def shards(
    block_in,
    block_grad,
    norm_gains,
    mixer_in,
    conv_taps,
    conv_bias,
    state_proj,
    step_proj,
    step_bias,
    decay_log,
    skip_gain,
    mixer_out,
    first_in,
    first_out,
    attend_in,
    attend_out,
    second_in,
    second_out,
    row_counts,
    doc_starts,
    row_mask,
):
    local_len = block_in.shape[1]
    length = local_len * lax.axis_size("tp")
    anchor = lax.axis_index("seq") * length
    positions = anchor + jnp.arange(length, dtype=jnp.int32)
    own_place = anchor + lax.axis_index("tp") * local_len + jnp.arange(local_len, dtype=jnp.int32)
    valid = ((own_place[None, :] < row_counts[:, None]) & (row_mask[:, None] == 1)).astype(
        jnp.float32
    )[:, :, None]
    documents = doc_numbers(positions, doc_starts)
    flags = jnp.any(doc_starts[:, None, :] == positions[None, :, None], axis=-1).astype(jnp.float32)
    taps = conv_taps.shape[0]
    same = jnp.stack(
        [
            (
                (positions - (taps - 1 - tap) >= 0)[None, :]
                & (doc_numbers(positions - (taps - 1 - tap), doc_starts) == documents)
            ).astype(jnp.float32)
            for tap in range(taps)
        ],
        axis=-1,
    )
    here = jnp.broadcast_to(anchor, (doc_starts.shape[0], 1)).astype(jnp.int32)
    info = jnp.concatenate([here, doc_starts], axis=1)
    mixer_weights = (
        mixer_in,
        conv_taps,
        conv_bias,
        state_proj,
        step_proj,
        step_bias,
        decay_log,
        skip_gain,
        mixer_out,
    )
    normed_mix, scale_mix = norm_forward(block_in, norm_gains[0])
    partial_value, cache_mix = mixer_forward(
        gather_rows(normed_mix.astype(jnp.bfloat16)), mixer_weights, same, flags
    )
    stream_mix = block_in + reduce_rows(partial_value)
    normed_first, scale_first = norm_forward(stream_mix, norm_gains[1])
    partial_value, cache_first = dense_forward(
        gather_rows(normed_first.astype(jnp.bfloat16)), first_in, first_out
    )
    stream_first = stream_mix + reduce_rows(partial_value)
    grad_stream = block_grad * valid
    grad_second = gather_rows(grad_stream.astype(jnp.bfloat16))
    normed_attend, scale_attend = norm_forward(stream_first, norm_gains[2])
    partial_value, cache_attend = attention_forward(
        gather_rows(normed_attend.astype(jnp.bfloat16)), attend_in, attend_out, info
    )
    stream_attend = stream_first + reduce_rows(partial_value, grad_second)
    normed_second, scale_second = norm_forward(stream_attend, norm_gains[3])
    partial_out, cache_second = dense_forward(
        gather_rows(normed_second.astype(jnp.bfloat16)), second_in, second_out
    )
    partial_out = partial_out.astype(jnp.bfloat16)

    def gain_of(which, low, cache):
        return gain_share(low, cache[0], norm_gains[which])

    grad_normed, firsts = dense_backward(grad_second, cache_second, second_in, second_out)
    low = grad_normed.astype(jnp.bfloat16)
    gain_four = gain_of(3, low, cache_second)
    grad_back = norm_backward(
        stream_attend,
        scale_second,
        after(norm_gains[3], firsts[0][0], firsts[1][0], gain_four, partial_out),
        reduce_rows(low),
    )
    grad_stream = grad_stream + grad_back
    second = [plane_second(*pair) for pair in firsts]
    gathered = gather_rows(grad_stream.astype(jnp.bfloat16))
    stream_out = stream_attend + reduce_rows(partial_out, gathered)
    block_out = stream_out * valid
    grad_normed, firsts = attention_backward(
        gathered, cache_attend, attend_in, attend_out, info, second
    )
    low = grad_normed.astype(jnp.bfloat16)
    gain_three = gain_of(2, low, cache_attend)
    second = [plane_third(held, grad_normed) for held in second]
    grad_back = norm_backward(
        stream_first,
        scale_attend,
        after(norm_gains[2], firsts[0][0], firsts[1][0], second, gain_three),
        reduce_rows(low),
    )
    grad_stream = grad_stream + grad_back
    middle = [plane_second(*pair) for pair in firsts]
    grad_normed, firsts = dense_backward(
        gather_rows(grad_stream.astype(jnp.bfloat16)), cache_first, first_in, first_out, middle
    )
    middle = [plane_third(held) for held in middle]
    low = grad_normed.astype(jnp.bfloat16)
    gain_two = gain_of(1, low, cache_first)
    grad_back = norm_backward(
        stream_mix,
        scale_first,
        after(norm_gains[1], firsts[0][0], firsts[1][0], middle, gain_two),
        reduce_rows(low),
    )
    grad_stream = grad_stream + grad_back
    firsts = [plane_second(*pair) for pair in firsts]
    grad_normed, grad_mixer_in, grad_mixer_out, small, first = mixer_backward(
        gather_rows(grad_stream.astype(jnp.bfloat16)),
        cache_mix,
        mixer_weights,
        same,
        flags,
        firsts,
    )
    low = grad_normed.astype(jnp.bfloat16)
    gains = jnp.stack([gain_of(0, low, cache_mix), gain_two, gain_three, gain_four])
    grad_mixer_in = plane_third(plane_second(*plane_first(grad_mixer_in)))
    grad_normed = reduce_rows(low)
    wide = small[0].shape[1]
    small = small + (gains.reshape(-1, wide),)
    counts = [member.shape[0] for member in small]
    packed = spread_sum(jnp.concatenate(small), ("seq", "row"), jnp.bfloat16)
    small, place = ([], 0)
    for count in counts:
        small.append(packed[place : place + count])
        place += count
    gains = jnp.sum(lax.all_gather(small.pop(), "tp"), axis=0).reshape(gains.shape)
    grad_back = norm_backward(
        block_in, scale_mix, norm_gains[0], grad_normed
    )
    grad_stream = grad_stream + grad_back
    middle[0] = in_order(middle[0], attend_in.shape[2] // HDIM)
    pairs = ((grad_mixer_in, grad_mixer_out), first, middle, second)
    flat = [member for pair in pairs for member in (pair[0], pair[1].T)]
    return (
        block_out,
        grad_stream,
        gains,
        flat[0],
        small[0],
        small[1][0],
        small[2].T,
        small[3],
        small[4][0],
        small[5],
        small[6][0],
        flat[1],
        flat[2],
        flat[3],
        flat[4],
        flat[5],
        flat[6],
        flat[7],
    )


def solution(mesh):
    in_specs = (
        P("row", ("seq", "tp"), None),
        P("row", ("seq", "tp"), None),
        P(),
        P(None, None, "tp"),
        P(None, "tp"),
        P("tp"),
        P("tp", None),
        P(None, "tp"),
        P("tp"),
        P(None, "tp"),
        P("tp"),
        P("tp", None),
        P(None, None, "tp"),
        P("tp", None),
        P(None, None, "tp"),
        P("tp", None),
        P(None, None, "tp"),
        P("tp", None),
        P("row"),
        P("row", None),
        P("row"),
    )
    out_specs = (
        P("row", ("seq", "tp"), None),
        P("row", ("seq", "tp"), None),
        P(),
        P(("row", "seq"), None, "tp"),
        P(None, "tp"),
        P("tp"),
        P("tp", None),
        P(None, "tp"),
        P("tp"),
        P(None, "tp"),
        P("tp"),
        P("tp", ("row", "seq")),
        P(("row", "seq"), None, "tp"),
        P("tp", ("row", "seq")),
        P(("row", "seq"), None, "tp"),
        P("tp", ("row", "seq")),
        P(("row", "seq"), None, "tp"),
        P("tp", ("row", "seq")),
    )
    return jax.shard_map(shards, mesh=mesh, in_specs=in_specs, out_specs=out_specs, check_vma=False)
```

```python
import jax
import jax.numpy as jnp
from jax import lax
from jax.experimental import pallas as pl
from jax.experimental.layout import Layout, with_layout_constraint
from jax.experimental.pallas import tpu as pltpu
from jax.sharding import PartitionSpec as P

HDIM = 128
WINDOW = 2048
f32 = jnp.float32
LOG2E = 1.4426950408889634
FAR = 1e30
QBLOCK = 256


epsilon = 1e-05
masked_score = -1e30


def carried_in(state, span, rate, axis, backward):
    count, mine = (lax.axis_size(axis), lax.axis_index(axis))
    both = jnp.concatenate([state, span[:, None, :]], axis=1)
    pieces = lax.all_gather(both, axis)
    if backward:
        mine = count - 1 - mine
    total = jnp.zeros_like(state)
    for position in range(count - 1):
        piece = pieces[count - 1 - position if backward else position]
        longer = jnp.exp(rate[None] * piece[:, -1:, :]) * total + piece[:, :-1]
        total = jnp.where(position < mine, longer, total)
    return total


def from_behind(x, axis, by):
    peers = lax.axis_size(axis)
    pairs = [(i, i + by) for i in range(peers) if 0 <= i + by < peers]
    return lax.ppermute(x, axis, pairs)


def gather_rows(local):
    return lax.all_gather(local, "tp", axis=1, tiled=True)


def reduce_rows(partial_value, event=()):
    low = after(partial_value.astype(jnp.bfloat16), event)
    return lax.psum_scatter(low, "tp", scatter_dimension=1, tiled=True)


def after(value, *events):
    marks = [event[(0,) * event.ndim].astype(jnp.float32) for event in jax.tree.leaves(events)]
    if not marks:
        return value
    return value + (sum(marks) * 0.0).astype(value.dtype)


def rowwise(value):
    return with_layout_constraint(value, Layout(tuple(range(value.ndim))))


def spread_sum(value, axes, kind):
    for axis in axes:
        flip = 1
        while flip < lax.axis_size(axis):
            other = partner(value.astype(kind), axis, flip)
            value = value + other.astype(value.dtype)
            flip *= 2
    return value


def partner(x, axis, flip):
    return lax.ppermute(x, axis, [(i, i ^ flip) for i in range(lax.axis_size(axis))])


def channel_total(partial_value):
    low = partial_value.astype(jnp.bfloat16).astype(jnp.float32)
    flip = 1
    while flip < lax.axis_size("tp"):
        other = partner(low.astype(jnp.bfloat16), "tp", flip)
        low = (low + other.astype(jnp.float32)).astype(jnp.bfloat16).astype(jnp.float32)
        flip *= 2
    return low.astype(jnp.bfloat16)


def plane_first(grad):
    if lax.axis_size("row") != 2:
        return (grad.astype(jnp.bfloat16),)
    held = grad.reshape((2, 2, 2, grad.shape[0] // 8) + grad.shape[1:])
    place = lax.axis_index("seq") % 2
    given = lax.dynamic_slice_in_dim(held, 1 - place, 1, axis=2).astype(jnp.bfloat16)
    kept = lax.dynamic_slice_in_dim(held, place, 1, axis=2).astype(jnp.bfloat16)
    return (given, kept)


def joined(given, kept, name, flip):
    other = partner(given, name, flip).astype(jnp.float32)
    return kept.astype(jnp.float32) + other


def plane_second(given, kept=None):
    if kept is None:
        return lax.psum_scatter(given, ("row", "seq"), scatter_dimension=0, tiled=True)
    row = lax.axis_index("row")
    held = joined(given, kept, "seq", 1).astype(jnp.bfloat16)
    given = lax.dynamic_slice_in_dim(held, 1 - row, 1, axis=0)
    held = joined(given, lax.dynamic_slice_in_dim(held, row, 1, axis=0), "row", 1)
    return held.astype(jnp.bfloat16)


def plane_third(held, event=()):
    if lax.axis_size("row") != 2:
        return held.astype(jnp.float32)
    seq = lax.axis_index("seq")
    given = after(lax.dynamic_slice_in_dim(held, 1 - seq // 2, 1, axis=1), event)
    held = joined(given, lax.dynamic_slice_in_dim(held, seq // 2, 1, axis=1), "seq", 2)
    return held.reshape(held.shape[3:])


def doc_numbers(positions, starts):
    return jnp.sum((starts[:, None, :] <= positions[None, :, None]).astype(jnp.int32), axis=-1)


def norm_kernel(stream_ref, part_ref, gain_ref, out_ref, normed_ref):
    stream = stream_ref[0] + part_ref[0].astype(f32)
    scale = lax.rsqrt(jnp.mean(stream * stream, axis=-1, keepdims=True) + epsilon)
    out_ref[0] = stream
    normed_ref[0] = (stream * scale * gain_ref[...]).astype(jnp.bfloat16)


def norm_specs(stream):
    rows, length, features = stream.shape
    block = min(128, length)
    tile = pl.BlockSpec((1, block, features), lambda i, j: (i, j, 0))
    return ((rows, length // block), tile, pl.BlockSpec((1, features), lambda i, j: (0, 0)))


def norm_forward(stream, part, gain):
    grid, tile, line = norm_specs(stream)
    return pl.pallas_call(
        norm_kernel,
        grid=grid,
        in_specs=[tile, tile, line],
        out_specs=[tile, tile],
        out_shape=[
            jax.ShapeDtypeStruct(stream.shape, f32),
            jax.ShapeDtypeStruct(stream.shape, jnp.bfloat16),
        ],
        cost_estimate=cost(2),
    )(stream, part, gain[None])


def norm_back_kernel(stream_ref, grad_ref, part_ref, gain_ref, out_ref, low_ref):
    stream = stream_ref[0]
    scale = lax.rsqrt(jnp.mean(stream * stream, axis=-1, keepdims=True) + epsilon)
    unit = stream * scale
    scaled = part_ref[0].astype(f32) * gain_ref[...]
    mean = jnp.mean(scaled * unit, axis=-1, keepdims=True)
    grad = grad_ref[0] + scale * (scaled - unit * mean)
    out_ref[0] = grad
    low_ref[0] = grad.astype(jnp.bfloat16)


def norm_backward(stream, grad, part, gain):
    grid, tile, line = norm_specs(stream)
    return pl.pallas_call(
        norm_back_kernel,
        grid=grid,
        in_specs=[tile, tile, tile, line],
        out_specs=[tile, tile],
        out_shape=[
            jax.ShapeDtypeStruct(stream.shape, f32),
            jax.ShapeDtypeStruct(stream.shape, jnp.bfloat16),
        ],
        cost_estimate=cost(2),
    )(stream, grad, part, gain[None])


def gain_share(partial_value, normed, gain):
    product = partial_value.astype(jnp.float32) * normed.astype(jnp.float32)
    return jnp.sum(product, axis=(0, 1)) / gain


def silu_slope(value):
    logistic = jax.nn.sigmoid(value)
    return logistic * (1.0 + value * (1.0 - logistic))


TB = 128
UNROLL = 64
UNROLL_BACK = 32
VM = 48 * 1024 * 1024

def cost(microseconds):
    return pl.CostEstimate(
        flops=int(microseconds * 1e9), bytes_accessed=int(microseconds * 3e6), transcendentals=0
    )


def params():
    return pltpu.CompilerParams(vmem_limit_bytes=VM, dimension_semantics=("arbitrary",))

def turned(ref, b, base, tb):
    return pltpu.roll(ref[b], lax.rem(tb - base, tb), axis=1)

def ends_kernel(step_ref, push_ref, write_ref, rate_ref, end_ref):
    rows, tb = step_ref.shape[0], step_ref.shape[1]
    @pl.when(pl.program_id(0) == 0)
    def _():
        end_ref[...] = jnp.zeros_like(end_ref)
    def group(j, held):
        base = pl.multiple_of(j * UNROLL, UNROLL)
        held = list(held)
        for b in range(rows):
            steps = step_ref[b, pl.ds(base, UNROLL), :]
            pushes = push_ref[b, pl.ds(base, UNROLL), :]
            writes = turned(write_ref, b, base, tb)
            for k in range(UNROLL):
                factor = jnp.exp2(steps[k:k+1] * rate_ref[...])
                held[b] = factor * held[b] + writes[:, k:k+1] * pushes[k:k+1]
        return tuple(held)
    held = lax.fori_loop(0, tb // UNROLL, group, tuple(end_ref[b] for b in range(rows)))
    for b in range(rows):
        end_ref[b] = held[b]

def scan_ends(step, push, write, rate):
    rows, length, chans = step.shape
    states = rate.shape[0]
    tb = min(TB, length)
    big = pl.BlockSpec((rows, tb, chans), lambda i: (0, i, 0))
    thin = pl.BlockSpec((rows, states, tb), lambda i: (0, 0, i))
    return pl.pallas_call(ends_kernel, grid=(length // tb,),
        in_specs=[big, big, thin, pl.BlockSpec((states, chans), lambda i: (0, 0))],
        out_specs=pl.BlockSpec((rows, states, chans), lambda i: (0, 0, 0)),
        out_shape=jax.ShapeDtypeStruct((rows, states, chans), f32),
        cost_estimate=cost(12), compiler_params=params())(step, push, write, rate)

def picker(tb):
    row = lax.broadcasted_iota(jnp.int32, (tb, tb * 8), 0)
    column = lax.broadcasted_iota(jnp.int32, (tb, tb * 8), 1)
    inside = (column >= row * 8) & (column < row * 8 + 8)
    return jnp.where(inside, 1.0, 0.0).astype(jnp.bfloat16)


def folded(value):
    return sum(value[i : i + 8] for i in range(0, value.shape[0], 8))


def across(value):
    return sum(value[:, i : i + 128] for i in range(0, value.shape[1], 128))


def mat(left, right, dims):
    return lax.dot_general(left, right, (dims, ((), ())), preferred_element_type=f32)


def outputs_kernel(step_ref, push_ref, write_ref, read_ref, rate_ref, first_ref, out_ref, start_ref, held_ref, part_ref):
    rows, tb = step_ref.shape[0], step_ref.shape[1]
    @pl.when(pl.program_id(0) == 0)
    def _():
        held_ref[...] = first_ref[...]
    start_ref[:, 0] = held_ref[...]
    for b in range(rows):
        def group(j, held):
            base = pl.multiple_of(j * UNROLL, UNROLL)
            steps = step_ref[b, pl.ds(base, UNROLL), :]
            pushes = push_ref[b, pl.ds(base, UNROLL), :]
            writes = turned(write_ref, b, base, tb)
            reads = turned(read_ref, b, base, tb)
            for k in range(UNROLL):
                factor = jnp.exp2(steps[k:k+1] * rate_ref[...])
                held = factor * held + writes[:, k:k+1] * pushes[k:k+1]
                part_ref[pl.ds(pl.multiple_of((base + k) * 8, 8), 8), :] = folded(held * reads[:, k:k+1])
            return held
        held_ref[b] = lax.fori_loop(0, tb // UNROLL, group, held_ref[b])
        high = part_ref[...].astype(jnp.bfloat16)
        low = (part_ref[...] - high.astype(f32)).astype(jnp.bfloat16)
        out_ref[b] = mat(picker(tb), high, ((1,), (0,))) + mat(picker(tb), low, ((1,), (0,)))

def scan_outputs(step, push, write, read, rate, first):
    rows, length, chans = step.shape
    states = rate.shape[0]
    tb = min(TB, length)
    big = pl.BlockSpec((rows, tb, chans), lambda i: (0, i, 0))
    thin = pl.BlockSpec((rows, states, tb), lambda i: (0, 0, i))
    whole = pl.BlockSpec((rows, states, chans), lambda i: (0, 0, 0))
    return pl.pallas_call(outputs_kernel, grid=(length // tb,),
        in_specs=[big, big, thin, thin, pl.BlockSpec((states, chans), lambda i: (0, 0)), whole],
        out_specs=[big, pl.BlockSpec((rows, 1, states, chans), lambda i: (0, i, 0, 0))],
        out_shape=[jax.ShapeDtypeStruct((rows, length, chans), f32),
                   jax.ShapeDtypeStruct((rows, length // tb, states, chans), f32)],
        scratch_shapes=[pltpu.VMEM((rows, states, chans), f32), pltpu.VMEM((tb * 8, chans), f32)],
        cost_estimate=cost(21), compiler_params=params())(step, push, write, read, rate, first)

def tail_kernel(step_ref, grad_ref, read_ref, rate_ref, end_ref):
    rows, tb = step_ref.shape[0], step_ref.shape[1]
    @pl.when(pl.program_id(0) == 0)
    def _():
        end_ref[...] = jnp.zeros_like(end_ref)
    def group(j, held):
        base = pl.multiple_of(tb - UNROLL - j * UNROLL, UNROLL)
        held = list(held)
        for b in range(rows):
            steps = step_ref[b, pl.ds(base, UNROLL), :]
            grads = grad_ref[b, pl.ds(base, UNROLL), :]
            reads = turned(read_ref, b, base, tb)
            for k in range(UNROLL - 1, -1, -1):
                factor = jnp.exp2(steps[k:k+1] * rate_ref[...])
                held[b] = factor * (held[b] + reads[:, k:k+1] * grads[k:k+1])
        return tuple(held)
    held = lax.fori_loop(0, tb // UNROLL, group, tuple(end_ref[b] for b in range(rows)))
    for b in range(rows):
        end_ref[b] = held[b]

def scan_tail(step, grad, read, rate):
    rows, length, chans = step.shape
    states = rate.shape[0]
    tb = min(TB, length)
    n = length // tb
    big = pl.BlockSpec((rows, tb, chans), lambda i: (0, n - 1 - i, 0))
    thin = pl.BlockSpec((rows, states, tb), lambda i: (0, 0, n - 1 - i))
    return pl.pallas_call(tail_kernel, grid=(n,),
        in_specs=[big, big, thin, pl.BlockSpec((states, chans), lambda i: (0, 0))],
        out_specs=pl.BlockSpec((rows, states, chans), lambda i: (0, 0, 0)),
        out_shape=jax.ShapeDtypeStruct((rows, states, chans), f32),
        cost_estimate=cost(12), compiler_params=params())(step, grad, read, rate)

def back_kernel(step_ref, push_ref, grad_ref, write_ref, read_ref, rate_ref, start_ref, later_ref,
                decay_ref, weight_ref, gwrite_ref, gread_ref, grate_ref,
                carry_ref, factor_sc, kept_sc, decay_sc, weight_sc, gwrite_sc, gread_sc):
    rows, tb = step_ref.shape[0], step_ref.shape[1]
    states = rate_ref.shape[0]
    @pl.when(pl.program_id(0) == 0)
    def _():
        carry_ref[...] = later_ref[...]
        grate_ref[...] = jnp.zeros_like(grate_ref)
    for b in range(rows):
        def redo(j, held):
            base = pl.multiple_of(j * UNROLL, UNROLL)
            steps = step_ref[b, pl.ds(base, UNROLL), :]
            pushes = push_ref[b, pl.ds(base, UNROLL), :]
            writes = turned(write_ref, b, base, tb)
            for k in range(UNROLL):
                factor = jnp.exp2(steps[k:k+1] * rate_ref[...])
                kept = factor * held
                factor_sc[base + k] = factor
                kept_sc[base + k] = kept
                held = kept + writes[:, k:k+1] * pushes[k:k+1]
            return held
        lax.fori_loop(0, tb // UNROLL, redo, start_ref[b, 0])
        def group(j, carried):
            carry, total = carried
            base = pl.multiple_of(tb - UNROLL_BACK - j * UNROLL_BACK, UNROLL_BACK)
            steps = step_ref[b, pl.ds(base, UNROLL_BACK), :]
            pushes = push_ref[b, pl.ds(base, UNROLL_BACK), :]
            grads = grad_ref[b, pl.ds(base, UNROLL_BACK), :]
            writes = turned(write_ref, b, base, tb)
            reads = turned(read_ref, b, base, tb)
            for k in range(UNROLL_BACK - 1, -1, -1):
                kept = kept_sc[base + k]
                adjoint = reads[:, k:k+1] * grads[k:k+1] + carry
                carry = factor_sc[base + k] * adjoint
                weighted = adjoint * kept
                total = total + weighted * steps[k:k+1]
                eight = pl.ds(pl.multiple_of((base + k) * 8, 8), 8)
                decay_sc[eight, :] = folded(weighted * rate_ref[...])
                weight_sc[eight, :] = folded(adjoint * writes[:, k:k+1])
                wide = pl.ds(pl.multiple_of((base + k) * states, states), states)
                gwrite_sc[wide, :] = across(adjoint * pushes[k:k+1])
                gread_sc[wide, :] = across(kept * grads[k:k+1])
            return (carry, total)
        carry, total = lax.fori_loop(0, tb // UNROLL_BACK, group, (carry_ref[b], grate_ref[...]))
        grate_ref[...] = total
        carry_ref[b] = carry
        pick = picker(tb)
        decay_ref[b] = mat(pick, decay_sc[...].astype(jnp.bfloat16), ((1,), (0,)))
        weight_ref[b] = mat(pick, weight_sc[...].astype(jnp.bfloat16), ((1,), (0,)))
        ones = jnp.ones((8, 128), jnp.bfloat16)
        gwrite_ref[b] = mat(ones, gwrite_sc[...].astype(jnp.bfloat16), ((1,), (1,)))[:1]
        gread_ref[b] = mat(ones, gread_sc[...].astype(jnp.bfloat16), ((1,), (1,)))[:1]

def scan_back(step, push, grad, write, read, rate, starts, later):
    rows, length, chans = step.shape
    states = rate.shape[0]
    tb = min(TB, length)
    n = length // tb
    big = pl.BlockSpec((rows, tb, chans), lambda i: (0, n - 1 - i, 0))
    thin = pl.BlockSpec((rows, states, tb), lambda i: (0, 0, n - 1 - i))
    line = pl.BlockSpec((rows, 1, tb * states), lambda i: (0, 0, n - 1 - i))
    whole = pl.BlockSpec((rows, states, chans), lambda i: (0, 0, 0))
    flat = pl.BlockSpec((states, chans), lambda i: (0, 0))
    return pl.pallas_call(back_kernel, grid=(n,),
        in_specs=[big, big, big, thin, thin, flat, pl.BlockSpec((rows, 1, states, chans), lambda i: (0, n - 1 - i, 0, 0)), whole],
        out_specs=[big, big, line, line, flat],
        out_shape=[jax.ShapeDtypeStruct((rows, length, chans), f32)] * 2
                 + [jax.ShapeDtypeStruct((rows, 1, length * states), f32)] * 2
                 + [jax.ShapeDtypeStruct((states, chans), f32)],
        scratch_shapes=[pltpu.VMEM((rows, states, chans), f32),
                        pltpu.VMEM((tb, states, chans), f32),
                        pltpu.VMEM((tb, states, chans), f32),
                        pltpu.VMEM((tb * 8, chans), f32),
                        pltpu.VMEM((tb * 8, chans), f32),
                        pltpu.VMEM((tb * states, 128), f32),
                        pltpu.VMEM((tb * states, 128), f32)],
        cost_estimate=cost(46), compiler_params=params())(step, push, grad, write, read, rate, starts, later)


def mixer_forward(normed, weights, same, flags, late):
    (
        mixer_in,
        conv_taps,
        conv_bias,
        state_proj,
        step_proj,
        step_bias,
        decay_log,
        skip_gain,
        mixer_out,
    ) = weights
    both = jnp.einsum("rtd,dce->rtce", normed, mixer_in, preferred_element_type=jnp.float32)
    signal = both[:, :, 0].astype(jnp.bfloat16)
    gate = both[:, :, 1]
    taps = conv_taps.shape[0]
    length = signal.shape[1]
    rows = signal.shape[0]
    tail = from_behind(signal[:, length - (taps - 1) :], "seq", 1)
    widened = jnp.concatenate([tail, signal], axis=1).astype(jnp.float32)
    conv_sum = conv_bias + jnp.zeros_like(gate)
    for tap in range(taps):
        conv_sum = (
            conv_sum + conv_taps[tap] * widened[:, tap : tap + length] * same[:, :, tap : tap + 1]
        )
    inner = jax.nn.silu(conv_sum).astype(jnp.bfloat16)
    source = inner.astype(jnp.float32)
    mixed = channel_total(
        jnp.einsum("rte,ec->rtc", inner, state_proj, preferred_element_type=jnp.float32)
    )
    late = gather_rows(after(late, mixed))
    rank = step_proj.shape[0]
    states = decay_log.shape[0]
    step_low = mixed[:, :, :rank]
    write_in = mixed[:, :, rank : rank + states].astype(jnp.float32)
    read_out = mixed[:, :, rank + states :].astype(jnp.float32)
    step_raw = (
        jnp.einsum("rtk,ke->rte", step_low, step_proj, preferred_element_type=jnp.float32)
        + step_bias
    )
    step = jax.nn.softplus(step_raw)
    rate = -jnp.exp(decay_log)
    step_far = jnp.where(flags[:, :, None] > 0, FAR, step)
    push = step * source
    write_cols = jnp.swapaxes(write_in, 1, 2)
    read_cols = jnp.swapaxes(read_out, 1, 2)
    ends = scan_ends(step_far, push, write_cols, rate * LOG2E)
    span = jnp.where(jnp.max(flags, axis=1)[:, None] > 0, FAR, jnp.sum(step, axis=1))
    incoming = carried_in(ends, span, rate, "seq", False)
    scanned, firsts = scan_outputs(
        step_far, push, write_cols, read_cols, rate * LOG2E, incoming
    )
    result = scanned + skip_gain * source
    gated = (result * jax.nn.silu(gate)).astype(jnp.bfloat16)
    partial_value = jnp.einsum("rte,ed->rtd", gated, mixer_out, preferred_element_type=jnp.float32)
    cache = (
        normed,
        widened,
        gate,
        conv_sum,
        inner,
        source,
        step_low,
        step_raw,
        step,
        step_far,
        push,
        write_in,
        write_cols,
        read_cols,
        result,
        gated,
        firsts,
        span,
    )
    return (partial_value, cache, late)


def mixer_backward(grad_branch, cache, weights, same, flags, first, branch):
    (
        mixer_in,
        conv_taps,
        conv_bias,
        state_proj,
        step_proj,
        step_bias,
        decay_log,
        skip_gain,
        mixer_out,
    ) = weights
    (
        normed,
        widened,
        gate,
        conv_sum,
        inner,
        source,
        step_low,
        step_raw,
        step,
        step_far,
        push,
        write_in,
        write_cols,
        read_cols,
        result,
        gated,
        firsts,
        span,
    ) = cache
    grad_gated = jnp.einsum(
        "rtd,ed->rte", grad_branch, mixer_out, preferred_element_type=jnp.float32
    )
    grad_mixer_out = jnp.einsum(
        "rtd,rte->de", grad_branch, gated, preferred_element_type=jnp.float32
    )
    first_out = plane_first(grad_mixer_out)
    grad_gated = after(grad_gated, first)
    grad_result = grad_gated * jax.nn.silu(gate)
    grad_gate = grad_gated * result * silu_slope(gate)
    grad_skip = jnp.sum(grad_result * source, axis=(0, 1))
    rate = -jnp.exp(decay_log)
    early = after(rate * LOG2E, first_out[0])
    tail = scan_tail(step_far, grad_result, read_cols, early)
    second_out = plane_second(*first_out)
    first = [plane_third(held, tail) for held in first]
    later = carried_in(tail, span, rate, "seq", True)
    early = after(rate * LOG2E, second_out)
    decays, weights_back, write_back, read_back, grad_rate = scan_back(
        step_far, push, grad_result, write_cols, read_cols, early, firsts, later
    )
    grad_mixer_out = plane_third(second_out, grad_rate)
    grad_step = decays * (1.0 / LOG2E) + weights_back * source
    grad_source = weights_back * step
    grad_write = write_back.reshape(write_in.shape)
    grad_read = read_back.reshape(write_in.shape) + write_in * jnp.sum(
        push * grad_result, axis=2, keepdims=True
    )
    grad_source = grad_source + skip_gain * grad_result
    grad_step_raw = (grad_step * jax.nn.sigmoid(step_raw)).astype(jnp.bfloat16)
    grad_step_bias = jnp.sum(grad_step_raw.astype(jnp.float32), axis=(0, 1))
    grad_step_proj = jnp.einsum(
        "rtk,rte->ke", step_low, grad_step_raw, preferred_element_type=jnp.float32
    )
    grad_low = jnp.einsum(
        "rte,ke->rtk", grad_step_raw, step_proj, preferred_element_type=jnp.float32
    )
    grad_mixed = channel_total(
        jnp.concatenate([after(grad_low, first, branch), grad_write, grad_read], axis=-1)
    )
    grad_state_proj = jnp.einsum(
        "rte,rtc->ce", inner, grad_mixed, preferred_element_type=jnp.float32
    )
    grad_source = grad_source + jnp.einsum(
        "rtc,ec->rte", grad_mixed, state_proj, preferred_element_type=jnp.float32
    )
    grad_conv = grad_source * silu_slope(conv_sum)
    length = grad_conv.shape[1]
    taps = conv_taps.shape[0]
    reach = taps - 1
    terms = [grad_conv * same[:, :, tap : tap + 1] for tap in range(taps)]
    grad_taps = [
        jnp.sum(widened[:, tap : tap + length] * terms[tap], axis=(0, 1)) for tap in range(taps)
    ]
    grad_conv_bias = jnp.sum(grad_conv, axis=(0, 1))
    heads = [conv_taps[tap] * terms[tap][:, :reach] for tap in range(taps)]
    head = sum(
        jnp.pad(heads[tap][:, : reach - tap], ((0, 0), (tap, 0), (0, 0))) for tap in range(reach)
    )
    returned = from_behind(head, "seq", -1)
    grad_signal = jnp.pad(returned, ((0, 0), (length - reach, 0), (0, 0)))
    for tap in range(taps):
        shift = reach - tap
        grad_signal = grad_signal + conv_taps[tap] * jnp.pad(
            terms[tap][:, shift:], ((0, 0), (0, shift), (0, 0))
        )
    grad_both = jnp.stack([grad_signal, grad_gate], axis=2).astype(jnp.bfloat16)
    grad_mixer_in = jnp.einsum(
        "rtd,rtce->dce", normed, grad_both, preferred_element_type=jnp.float32
    )
    grad_normed = jnp.einsum(
        "rtce,dce->rtd", grad_both, mixer_in, preferred_element_type=jnp.float32
    )
    small = (
        jnp.stack(grad_taps),
        grad_conv_bias[None],
        grad_state_proj,
        grad_step_proj,
        grad_step_bias[None],
        grad_rate * rate,
        grad_skip[None],
    )
    return (grad_normed, grad_mixer_in, grad_mixer_out, small, first)


def dense_forward(normed, dense_in, dense_out):
    both = jnp.einsum("rtd,dcf->rtcf", normed, dense_in, preferred_element_type=jnp.float32)
    gate = both[:, :, 0]
    upper = both[:, :, 1]
    hidden = (jax.nn.silu(gate) * upper).astype(jnp.bfloat16)
    partial_value = jnp.einsum("rtf,fd->rtd", hidden, dense_out, preferred_element_type=jnp.float32)
    return (partial_value, (normed, gate, upper, hidden))


def dense_backward(grad_branch, cache, dense_in, dense_out, event=()):
    normed, gate, upper, hidden = cache
    grad_hidden = jnp.einsum(
        "rtd,fd->rtf", grad_branch, dense_out, preferred_element_type=jnp.float32
    )
    grad_hidden = after(grad_hidden, event)
    grad_gate = grad_hidden * upper * silu_slope(gate)
    grad_upper = grad_hidden * jax.nn.silu(gate)
    grad_both = jnp.stack([grad_gate, grad_upper], axis=2).astype(jnp.bfloat16)
    grad_normed = jnp.einsum(
        "rtcf,dcf->rtd", grad_both, dense_in, preferred_element_type=jnp.float32
    )
    grad_dense_out = jnp.einsum(
        "rtd,rtf->df", grad_branch, hidden, preferred_element_type=jnp.float32
    )
    grad_dense_in = jnp.einsum(
        "rtd,rtcf->dcf", normed, grad_both, preferred_element_type=jnp.float32
    )
    return (grad_normed, [plane_first(grad_dense_in), plane_first(grad_dense_out)])


def plan_of(length):
    block = min(QBLOCK, length)
    return (block, (WINDOW + block) // block)


def lower_edge(info_ref, row, first, block):
    lane = lax.broadcasted_iota(jnp.int32, (1, block), 1)
    place = info_ref[row, 0] + first + lane
    start = jnp.zeros((1, block), jnp.int32)
    for index in range(1, info_ref.shape[1]):
        entry = info_ref[row, index]
        start = jnp.maximum(start, jnp.where(entry <= place, entry, 0))
    return (jnp.maximum(lane + 1, start - (info_ref[row, 0] + first - WINDOW)), lane)


def piece_mask(low, lane, piece, block, pieces):
    index = piece * block + lax.broadcasted_iota(jnp.int32, (block, block), 0)
    allowed = index >= low
    if piece == pieces - 1:
        allowed = allowed & (index <= lane + WINDOW)
    return allowed


NT = (((1,), (1,)), ((), ()))
TN = (((0,), (0,)), ((), ()))
NN = (((1,), (0,)), ((), ()))


def dot(left, right, dims):
    return lax.dot_general(left, right, dims, preferred_element_type=f32)


def gathered_pieces(refs, wide):
    length = refs[0].shape[1]
    for index, ref in enumerate(refs):
        wide[pl.ds(index * length, length), :] = ref[0]


def attend_kernel(
    pieces, skip, info_ref, query_ref, second_ref, first_ref, own_ref, out_ref, total_ref, wide, held
):
    block = query_ref.shape[1]

    @pl.when(pl.program_id(1) == 0)
    def _():
        gathered_pieces((second_ref, first_ref, own_ref), wide)

    first = pl.multiple_of(pl.program_id(1) * block, block)
    low, lane = lower_edge(info_ref, pl.program_id(0), first, block)
    query = query_ref[0]
    top = jnp.full((1, block), masked_score, f32)
    for piece in range(pieces):
        at = pl.ds(pl.multiple_of(first + skip + piece * block, block), block)
        scores = dot(wide[at, :HDIM], query, NT)
        scores = jnp.where(piece_mask(low, lane, piece, block, pieces), scores, masked_score)
        held[piece] = scores
        top = jnp.maximum(top, jnp.max(scores, axis=0, keepdims=True))
    slope = HDIM ** (-0.5) * LOG2E
    total = jnp.zeros((1, block), f32)
    summed = jnp.zeros((HDIM, block), f32)
    for piece in range(pieces):
        at = pl.ds(pl.multiple_of(first + skip + piece * block, block), block)
        soft = jnp.exp2((held[piece] - top) * slope)
        total = total + jnp.sum(soft, axis=0, keepdims=True)
        summed = summed + dot(wide[at, HDIM:], soft.astype(jnp.bfloat16), TN)
    out_ref[0] = (summed / total).T.astype(jnp.bfloat16)
    total_ref[0] = top * slope + jnp.log2(total)


def head_specs(query, head):
    rows, length = (query.shape[0], query.shape[1])
    block, pieces = plan_of(length)
    halo = pl.BlockSpec((1, length, 2 * HDIM), lambda i, j: (i, 0, 0))
    own = pl.BlockSpec((1, length, 2 * HDIM), lambda i, j: (i, 0, head))
    narrow = pl.BlockSpec((1, block, HDIM), lambda i, j: (i, j, head))
    plain = pl.BlockSpec((1, block, HDIM), lambda i, j: (i, j, 0))
    line = pl.BlockSpec((1, 1, block), lambda i, j: (i, 0, j))
    skip = 2 * length - WINDOW
    return (rows, length, block, pieces, skip, halo, own, narrow, plain, line)


def attend(info, query, seconds, firsts, pairs, head):
    rows, length, block, pieces, skip, halo, own, narrow, plain, line = head_specs(query, head)
    body = lambda *refs: attend_kernel(pieces, skip, *refs)
    return pl.pallas_call(
        body,
        grid=(rows, length // block),
        in_specs=[pl.BlockSpec(memory_space=pltpu.SMEM), narrow, halo, halo, own],
        out_specs=[plain, line],
        out_shape=[
            jax.ShapeDtypeStruct((rows, length, HDIM), jnp.bfloat16),
            jax.ShapeDtypeStruct((rows, 1, length), f32),
        ],
        scratch_shapes=[
            pltpu.VMEM((3 * length, 2 * HDIM), jnp.bfloat16),
            pltpu.VMEM((pieces, block, block), f32),
        ],
        cost_estimate=cost(7),
        compiler_params=pltpu.CompilerParams(vmem_limit_bytes=VM),
    )(info, query, seconds, firsts, pairs)


def attend_back_kernel(
    pieces, skip, info_ref, query_ref, grad_ref, second_ref, first_ref, own_ref, total_ref, delta_ref,
    gquery_ref, gsecond_ref, gfirst_ref, gown_ref, wide, gkeys, gvalues,
):
    block, length = (query_ref.shape[1], own_ref.shape[1])
    first = pl.multiple_of(pl.program_id(1) * block, block)
    low, lane = lower_edge(info_ref, pl.program_id(0), first, block)

    @pl.when(pl.program_id(1) == 0)
    def _():
        gathered_pieces((second_ref, first_ref, own_ref), wide)
        gkeys[...] = jnp.zeros_like(gkeys)
        gvalues[...] = jnp.zeros_like(gvalues)

    query, grad = (query_ref[0], grad_ref[0])
    total, delta = (total_ref[0], delta_ref[0])
    slope = HDIM ** (-0.5) * LOG2E
    summed = jnp.zeros((HDIM, block), f32)
    for piece in range(pieces):
        at = pl.ds(pl.multiple_of(first + skip + piece * block, block), block)
        keys = wide[at, :HDIM]
        scores = dot(keys, query, NT)
        allowed = piece_mask(low, lane, piece, block, pieces)
        soft = jnp.exp2(jnp.where(allowed, scores * slope - total, masked_score))
        gvalues[at, :] += dot(soft.astype(jnp.bfloat16), grad, NN)
        spread = soft * (dot(wide[at, HDIM:], grad, NT) - delta)
        spread = spread.astype(jnp.bfloat16)
        gkeys[at, :] += dot(spread, query, NN)
        summed = summed + dot(keys, spread, TN)
    gquery_ref[0] = (summed * HDIM ** (-0.5)).T.astype(jnp.bfloat16)

    @pl.when(pl.program_id(1) == pl.num_programs(1) - 1)
    def _():
        for index, ref in enumerate((gsecond_ref, gfirst_ref, gown_ref)):
            at = pl.ds(index * length, length)
            ref[0, :, :HDIM] = (gkeys[at, :] * HDIM ** (-0.5)).astype(ref.dtype)
            ref[0, :, HDIM:] = gvalues[at, :].astype(ref.dtype)


def attend_back(info, query, grad, seconds, firsts, pairs, total, delta, head):
    rows, length, block, pieces, skip, halo, own, narrow, plain, line = head_specs(query, head)
    body = lambda *refs: attend_back_kernel(pieces, skip, *refs)
    double = (rows, length, 2 * HDIM)
    return pl.pallas_call(
        body,
        grid=(rows, length // block),
        in_specs=[
            pl.BlockSpec(memory_space=pltpu.SMEM),
            narrow,
            narrow,
            halo,
            halo,
            own,
            line,
            line,
        ],
        out_specs=[plain, halo, halo, halo],
        out_shape=[
            jax.ShapeDtypeStruct((rows, length, HDIM), jnp.bfloat16),
            jax.ShapeDtypeStruct(double, f32),
            jax.ShapeDtypeStruct(double, jnp.bfloat16),
            jax.ShapeDtypeStruct(double, f32),
        ],
        scratch_shapes=[
            pltpu.VMEM((3 * length, 2 * HDIM), jnp.bfloat16),
            pltpu.VMEM((3 * length, HDIM), f32),
            pltpu.VMEM((3 * length, HDIM), f32),
        ],
        cost_estimate=cost(12),
        compiler_params=pltpu.CompilerParams(vmem_limit_bytes=VM),
    )(info, query, grad, seconds, firsts, pairs, total, delta)


def by_head(attend_in):
    features, heads = (attend_in.shape[0], attend_in.shape[2] // HDIM)
    split = attend_in.reshape(features, 3, heads, HDIM)
    pairs = jnp.swapaxes(split[:, 1:], 1, 2).reshape(features, 2 * heads * HDIM)
    return (attend_in[:, 0], pairs)


def attention_forward(normed, attend_in, attend_out, info):
    heads = attend_in.shape[2] // HDIM
    weight_query, weight_pairs = by_head(attend_in)
    pairs = rowwise(
        jnp.einsum(
            "rtd,dh->rth", normed, weight_pairs, preferred_element_type=jnp.float32
        ).astype(jnp.bfloat16)
    )
    query = rowwise(
        jnp.einsum(
            "rtd,dh->rth", normed, weight_query, preferred_element_type=jnp.float32
        ).astype(jnp.bfloat16)
    )
    odd = lax.axis_index("seq") % 2 == 1
    halos, results = ([], [])
    for head in range(heads):
        own = rowwise(pairs[:, :, 2 * head * HDIM : 2 * (head + 1) * HDIM])
        seconds = rowwise(from_behind(own, "seq", 2))
        firsts = rowwise(partner(rowwise(jnp.where(odd, seconds, own)), "seq", 1))
        halos.append((seconds, firsts))
        results.append(attend(info, query, seconds, firsts, pairs, head))
    attended = jnp.concatenate([result[0] for result in results], axis=2)
    totals = [result[1] for result in results]
    partial_value = jnp.einsum(
        "rth,hd->rtd", attended, attend_out, preferred_element_type=jnp.float32
    )
    return (partial_value, (normed, query, pairs, halos, attended, totals, weight_query, weight_pairs))


def attention_backward(grad_branch, cache, attend_in, attend_out, info, event):
    normed, query, own_pairs, halos, attended, totals, weight_query, weight_pairs = cache
    rows, length = (query.shape[0], query.shape[1])
    heads = query.shape[2] // HDIM
    grad_attended = jnp.einsum(
        "rtd,hd->rth", grad_branch, attend_out, preferred_element_type=jnp.float32
    )
    grad_attended = rowwise(after(grad_attended, event).astype(jnp.bfloat16))
    grad_attend_out = jnp.einsum(
        "rtd,rth->dh", grad_branch, attended, preferred_element_type=jnp.float32
    )
    both = grad_attended.astype(jnp.float32) * attended.astype(jnp.float32)
    delta = jnp.sum(both.reshape(rows, length, heads, HDIM), axis=-1)
    odd = lax.axis_index("seq") % 2 == 1
    queries, pairs, marks = ([], [], [[], []])
    for head in range(heads):
        grad_query, second, given, own = attend_back(
            after(info, marks[head]),
            query,
            grad_attended,
            *halos[head],
            own_pairs,
            totals[head],
            delta[:, :, head].reshape(rows, 1, length),
            head,
        )
        queries.append(grad_query)
        given = rowwise(partner(given, "seq", 1)).astype(jnp.float32)
        sent = rowwise((second + jnp.where(odd, given, 0.0)).astype(jnp.bfloat16))
        marks.append(sent)
        back = rowwise(from_behind(sent, "seq", -2))
        pairs.append((own + jnp.where(odd, 0.0, given) + back.astype(jnp.float32)).astype(jnp.bfloat16))
    grad_projected = rowwise(jnp.concatenate(queries + pairs, axis=2))
    grad_weight = jnp.einsum(
        "rtd,rth->dh", normed, grad_projected, preferred_element_type=jnp.float32
    )
    flat = jnp.concatenate([weight_query, weight_pairs], axis=1)
    grad_normed = jnp.einsum(
        "rth,dh->rtd", grad_projected, flat, preferred_element_type=jnp.float32
    )
    return (grad_normed, [plane_first(grad_weight), plane_first(grad_attend_out)])


def in_order(grad_weight, heads):
    features = grad_weight.shape[0]
    query = grad_weight[:, : heads * HDIM].reshape(features, 1, heads, HDIM)
    pairs = grad_weight[:, heads * HDIM :].reshape(features, heads, 2, HDIM)
    both = jnp.concatenate([query, jnp.swapaxes(pairs, 1, 2)], axis=1)
    return both.reshape(features, 3, heads * HDIM)


def shards(
    block_in,
    block_grad,
    norm_gains,
    mixer_in,
    conv_taps,
    conv_bias,
    state_proj,
    step_proj,
    step_bias,
    decay_log,
    skip_gain,
    mixer_out,
    first_in,
    first_out,
    attend_in,
    attend_out,
    second_in,
    second_out,
    row_counts,
    doc_starts,
    row_mask,
):
    local_len = block_in.shape[1]
    length = local_len * lax.axis_size("tp")
    anchor = lax.axis_index("seq") * length
    positions = anchor + jnp.arange(length, dtype=jnp.int32)
    own_place = anchor + lax.axis_index("tp") * local_len + jnp.arange(local_len, dtype=jnp.int32)
    valid = ((own_place[None, :] < row_counts[:, None]) & (row_mask[:, None] == 1)).astype(
        jnp.float32
    )[:, :, None]
    documents = doc_numbers(positions, doc_starts)
    flags = jnp.any(doc_starts[:, None, :] == positions[None, :, None], axis=-1).astype(jnp.float32)
    taps = conv_taps.shape[0]
    same = jnp.stack(
        [
            (
                (positions - (taps - 1 - tap) >= 0)[None, :]
                & (doc_numbers(positions - (taps - 1 - tap), doc_starts) == documents)
            ).astype(jnp.float32)
            for tap in range(taps)
        ],
        axis=-1,
    )
    here = jnp.broadcast_to(anchor, (doc_starts.shape[0], 1)).astype(jnp.int32)
    info = jnp.concatenate([here, doc_starts], axis=1)
    mixer_weights = (
        mixer_in,
        conv_taps,
        conv_bias,
        state_proj,
        step_proj,
        step_bias,
        decay_log,
        skip_gain,
        mixer_out,
    )
    grad_stream = rowwise(block_grad * valid)
    unit = block_in * lax.rsqrt(jnp.mean(block_in * block_in, axis=-1, keepdims=True) + epsilon)
    normed = (unit * norm_gains[0]).astype(jnp.bfloat16)
    gathered = gather_rows(normed)
    partial_value, cache_mix, grad_second = mixer_forward(
        gathered, mixer_weights, same, flags, grad_stream.astype(jnp.bfloat16)
    )
    stream_mix, normed = norm_forward(
        block_in, reduce_rows(partial_value, grad_second), norm_gains[1]
    )
    partial_value, cache_first = dense_forward(gather_rows(normed), first_in, first_out)
    stream_first, normed = norm_forward(stream_mix, reduce_rows(partial_value), norm_gains[2])
    partial_value, cache_attend = attention_forward(
        gather_rows(normed), attend_in, attend_out, info
    )
    stream_attend, normed = norm_forward(stream_first, reduce_rows(partial_value), norm_gains[3])
    partial_out, cache_second = dense_forward(
        gather_rows(normed), second_in, second_out
    )
    partial_out = partial_out.astype(jnp.bfloat16)

    def gain_of(which, low, cache):
        return gain_share(low, cache[0], norm_gains[which])

    grad_normed, firsts = dense_backward(grad_second, cache_second, second_in, second_out)
    low = grad_normed.astype(jnp.bfloat16)
    gain_four = gain_of(3, low, cache_second)
    grad_stream, grad_low = norm_backward(
        stream_attend,
        grad_stream,
        reduce_rows(low),
        after(norm_gains[3], firsts[0][0], firsts[1][0], gain_four, partial_out),
    )
    second = [plane_second(*pair) for pair in firsts]
    gathered = gather_rows(grad_low)
    grad_normed, firsts = attention_backward(
        gathered, cache_attend, attend_in, attend_out, info, second
    )
    low = grad_normed.astype(jnp.bfloat16)
    gain_three = gain_of(2, low, cache_attend)
    second = [plane_third(held, grad_normed) for held in second]
    grad_stream, grad_low = norm_backward(
        stream_first,
        grad_stream,
        reduce_rows(low),
        after(norm_gains[2], firsts[0][0], firsts[1][0], second[0], second[1], gain_three),
    )
    middle = [plane_second(*pair) for pair in firsts]
    grad_normed, firsts = dense_backward(
        gather_rows(grad_low), cache_first, first_in, first_out, middle
    )
    middle = [plane_third(held) for held in middle]
    low = grad_normed.astype(jnp.bfloat16)
    gain_two = gain_of(1, low, cache_first)
    grad_stream, grad_low = norm_backward(
        stream_mix,
        grad_stream,
        reduce_rows(low),
        after(norm_gains[1], firsts[0][0], firsts[1][0], middle[0], middle[1], gain_two),
    )
    firsts = [plane_second(*pair) for pair in firsts]
    gathered = gather_rows(grad_low)
    branch = reduce_rows(partial_out, gathered)
    block_out = (stream_attend + branch.astype(jnp.float32)) * valid
    grad_normed, grad_mixer_in, grad_mixer_out, small, first = mixer_backward(
        gathered,
        cache_mix,
        mixer_weights,
        same,
        flags,
        firsts,
        branch,
    )
    low = grad_normed.astype(jnp.bfloat16)
    gains = jnp.stack([gain_of(0, low, cache_mix), gain_two, gain_three, gain_four])
    parted = plane_first(grad_mixer_in)
    grad_normed = reduce_rows(low)
    wide = small[0].shape[1]
    small = small + (gains.reshape(-1, wide),)
    counts = [member.shape[0] for member in small]
    packed = spread_sum(jnp.concatenate(small), ("seq", "row"), jnp.bfloat16)
    parted = (after(parted[0], packed),) + parted[1:]
    grad_mixer_in = plane_third(plane_second(*parted))
    small, place = ([], 0)
    for count in counts:
        small.append(packed[place : place + count])
        place += count
    gains = spread_sum(small.pop(), ("tp",), jnp.float32).reshape(gains.shape)
    grad_stream, _ = norm_backward(block_in, grad_stream, grad_normed, norm_gains[0])
    middle[0] = in_order(middle[0], attend_in.shape[2] // HDIM)
    pairs = ((grad_mixer_in, grad_mixer_out), first, middle, second)
    flat = [member for pair in pairs for member in (pair[0], pair[1].T)]
    return (
        block_out,
        grad_stream,
        gains,
        flat[0],
        small[0],
        small[1][0],
        small[2].T,
        small[3],
        small[4][0],
        small[5],
        small[6][0],
        flat[1],
        flat[2],
        flat[3],
        flat[4],
        flat[5],
        flat[6],
        flat[7],
    )


def solution(mesh):
    in_specs = (
        P("row", ("seq", "tp"), None),
        P("row", ("seq", "tp"), None),
        P(),
        P(None, None, "tp"),
        P(None, "tp"),
        P("tp"),
        P("tp", None),
        P(None, "tp"),
        P("tp"),
        P(None, "tp"),
        P("tp"),
        P("tp", None),
        P(None, None, "tp"),
        P("tp", None),
        P(None, None, "tp"),
        P("tp", None),
        P(None, None, "tp"),
        P("tp", None),
        P("row"),
        P("row", None),
        P("row"),
    )
    out_specs = (
        P("row", ("seq", "tp"), None),
        P("row", ("seq", "tp"), None),
        P(),
        P(("row", "seq"), None, "tp"),
        P(None, "tp"),
        P("tp"),
        P("tp", None),
        P(None, "tp"),
        P("tp"),
        P(None, "tp"),
        P("tp"),
        P("tp", ("row", "seq")),
        P(("row", "seq"), None, "tp"),
        P("tp", ("row", "seq")),
        P(("row", "seq"), None, "tp"),
        P("tp", ("row", "seq")),
        P(("row", "seq"), None, "tp"),
        P("tp", ("row", "seq")),
    )
    return jax.shard_map(shards, mesh=mesh, in_specs=in_specs, out_specs=out_specs, check_vma=False)
```

```python
import jax
import jax.numpy as jnp
from jax import lax
from jax.experimental import pallas as pl
from jax.experimental.layout import Layout, with_layout_constraint
from jax.experimental.pallas import tpu as pltpu
from jax.sharding import PartitionSpec as P

HDIM = 128
WINDOW = 2048
f32 = jnp.float32
LOG2E = 1.4426950408889634
FAR = 1e30
QBLOCK = 256


epsilon = 1e-05
masked_score = -1e30


def carried_in(state, span, rate, axis, backward):
    count, mine = (lax.axis_size(axis), lax.axis_index(axis))
    both = jnp.concatenate([state, span[:, None, :]], axis=1)
    pieces = lax.all_gather(both, axis)
    if backward:
        mine = count - 1 - mine
    total = jnp.zeros_like(state)
    for position in range(count - 1):
        piece = pieces[count - 1 - position if backward else position]
        longer = jnp.exp(rate[None] * piece[:, -1:, :]) * total + piece[:, :-1]
        total = jnp.where(position < mine, longer, total)
    return total


def from_behind(x, axis, by):
    peers = lax.axis_size(axis)
    pairs = [(i, i + by) for i in range(peers) if 0 <= i + by < peers]
    return lax.ppermute(x, axis, pairs)


def gather_rows(local):
    return lax.all_gather(local, "tp", axis=1, tiled=True)


def reduce_rows(partial_value, event=()):
    low = partial_value.astype(jnp.bfloat16)
    if jax.tree.leaves(event):
        low = nudged(low, event)
    return lax.psum_scatter(low, "tp", scatter_dimension=1, tiled=True)


def nudged(value, *events):
    corner = lax.slice(value, (0,) * value.ndim, (1,) * value.ndim)
    return lax.dynamic_update_slice(value, after(corner, *events), (0,) * value.ndim)


def after(value, *events):
    marks = [event[(0,) * event.ndim].astype(jnp.float32) for event in jax.tree.leaves(events)]
    if not marks:
        return value
    return value + (sum(marks) * 0.0).astype(value.dtype)


def rowwise(value):
    return with_layout_constraint(value, Layout(tuple(range(value.ndim))))


def spread_sum(value, axes, kind):
    for axis in axes:
        flip = 1
        while flip < lax.axis_size(axis):
            other = partner(value.astype(kind), axis, flip)
            value = value + other.astype(value.dtype)
            flip *= 2
    return value


def partner(x, axis, flip):
    return lax.ppermute(x, axis, [(i, i ^ flip) for i in range(lax.axis_size(axis))])


def channel_total(partial_value):
    low = partial_value.astype(jnp.bfloat16).astype(jnp.float32)
    flip, hops = (1, [])
    while flip < lax.axis_size("tp"):
        hops.append(partner(low.astype(jnp.bfloat16), "tp", flip))
        low = (low + hops[-1].astype(jnp.float32)).astype(jnp.bfloat16).astype(jnp.float32)
        flip *= 2
    return (low.astype(jnp.bfloat16), hops[0])


def plane_first(grad):
    if lax.axis_size("row") != 2:
        return (grad.astype(jnp.bfloat16),)
    held = grad.reshape((2, 2, 2, grad.shape[0] // 8) + grad.shape[1:])
    place = lax.axis_index("seq") % 2
    given = lax.dynamic_slice_in_dim(held, 1 - place, 1, axis=2).astype(jnp.bfloat16)
    kept = lax.dynamic_slice_in_dim(held, place, 1, axis=2).astype(jnp.bfloat16)
    return (given, kept)


def joined(given, kept, name, flip):
    other = partner(given, name, flip).astype(jnp.float32)
    return kept.astype(jnp.float32) + other


def plane_second(given, kept=None):
    if kept is None:
        return lax.psum_scatter(given, ("row", "seq"), scatter_dimension=0, tiled=True)
    row = lax.axis_index("row")
    held = joined(given, kept, "seq", 1).astype(jnp.bfloat16)
    given = lax.dynamic_slice_in_dim(held, 1 - row, 1, axis=0)
    held = joined(given, lax.dynamic_slice_in_dim(held, row, 1, axis=0), "row", 1)
    return held.astype(jnp.bfloat16)


def plane_third(held, event=()):
    if lax.axis_size("row") != 2:
        return (held.astype(jnp.float32), held)
    seq = lax.axis_index("seq")
    given = after(lax.dynamic_slice_in_dim(held, 1 - seq // 2, 1, axis=1), event)
    kept = lax.dynamic_slice_in_dim(held, seq // 2, 1, axis=1)
    other = partner(given, "seq", 2)
    total = kept.astype(jnp.float32) + other.astype(jnp.float32)
    return (total.reshape(total.shape[3:]), other)


def doc_numbers(positions, starts):
    return jnp.sum((starts[:, None, :] <= positions[None, :, None]).astype(jnp.int32), axis=-1)


def norm_kernel(stream_ref, part_ref, gain_ref, out_ref, normed_ref):
    stream = stream_ref[0] + part_ref[0].astype(f32)
    scale = lax.rsqrt(jnp.mean(stream * stream, axis=-1, keepdims=True) + epsilon)
    out_ref[0] = stream
    normed_ref[0] = (stream * scale * gain_ref[...]).astype(jnp.bfloat16)


def norm_specs(stream):
    rows, length, features = stream.shape
    block = min(128, length)
    tile = pl.BlockSpec((1, block, features), lambda i, j: (i, j, 0))
    return ((rows, length // block), tile, pl.BlockSpec((1, features), lambda i, j: (0, 0)))


def norm_forward(stream, part, gain):
    grid, tile, line = norm_specs(stream)
    return pl.pallas_call(
        norm_kernel,
        grid=grid,
        in_specs=[tile, tile, line],
        out_specs=[tile, tile],
        out_shape=[
            jax.ShapeDtypeStruct(stream.shape, f32),
            jax.ShapeDtypeStruct(stream.shape, jnp.bfloat16),
        ],
        cost_estimate=cost(2),
    )(stream, part, gain[None])


def norm_back_kernel(stream_ref, grad_ref, part_ref, gain_ref, out_ref, low_ref):
    stream = stream_ref[0]
    scale = lax.rsqrt(jnp.mean(stream * stream, axis=-1, keepdims=True) + epsilon)
    unit = stream * scale
    scaled = part_ref[0].astype(f32) * gain_ref[...]
    mean = jnp.mean(scaled * unit, axis=-1, keepdims=True)
    grad = grad_ref[0] + scale * (scaled - unit * mean)
    out_ref[0] = grad
    low_ref[0] = grad.astype(jnp.bfloat16)


def norm_backward(stream, grad, part, gain):
    grid, tile, line = norm_specs(stream)
    return pl.pallas_call(
        norm_back_kernel,
        grid=grid,
        in_specs=[tile, tile, tile, line],
        out_specs=[tile, tile],
        out_shape=[
            jax.ShapeDtypeStruct(stream.shape, f32),
            jax.ShapeDtypeStruct(stream.shape, jnp.bfloat16),
        ],
        cost_estimate=cost(2),
    )(stream, grad, part, gain[None])


def gain_share(partial_value, normed, gain):
    product = partial_value.astype(jnp.float32) * normed.astype(jnp.float32)
    return jnp.sum(product, axis=(0, 1)) / gain


def silu_slope(value):
    logistic = jax.nn.sigmoid(value)
    return logistic * (1.0 + value * (1.0 - logistic))


TB = 128
UNROLL = 128
UNROLL_BACK = 64
VM = 48 * 1024 * 1024

def cost(microseconds):
    return pl.CostEstimate(
        flops=int(microseconds * 1e9), bytes_accessed=int(microseconds * 3e6), transcendentals=0
    )


def params():
    return pltpu.CompilerParams(vmem_limit_bytes=VM, dimension_semantics=("arbitrary",))

def turned(ref, b, base, tb):
    return pltpu.roll(ref[b], lax.rem(tb - base, tb), axis=1)

def ends_kernel(step_ref, push_ref, write_ref, rate_ref, end_ref):
    rows, tb = step_ref.shape[0], step_ref.shape[1]
    @pl.when(pl.program_id(0) == 0)
    def _():
        end_ref[...] = jnp.zeros_like(end_ref)
    def group(j, held):
        base = pl.multiple_of(j * UNROLL, UNROLL)
        held = list(held)
        for b in range(rows):
            steps = step_ref[b, pl.ds(base, UNROLL), :]
            pushes = push_ref[b, pl.ds(base, UNROLL), :]
            writes = turned(write_ref, b, base, tb)
            for k in range(UNROLL):
                factor = jnp.exp2(steps[k:k+1] * rate_ref[...])
                held[b] = factor * held[b] + writes[:, k:k+1] * pushes[k:k+1]
        return tuple(held)
    held = lax.fori_loop(0, tb // UNROLL, group, tuple(end_ref[b] for b in range(rows)))
    for b in range(rows):
        end_ref[b] = held[b]

def scan_ends(step, push, write, rate):
    rows, length, chans = step.shape
    states = rate.shape[0]
    tb = min(TB, length)
    big = pl.BlockSpec((rows, tb, chans), lambda i: (0, i, 0))
    thin = pl.BlockSpec((rows, states, tb), lambda i: (0, 0, i))
    return pl.pallas_call(ends_kernel, grid=(length // tb,),
        in_specs=[big, big, thin, pl.BlockSpec((states, chans), lambda i: (0, 0))],
        out_specs=pl.BlockSpec((rows, states, chans), lambda i: (0, 0, 0)),
        out_shape=jax.ShapeDtypeStruct((rows, states, chans), f32),
        cost_estimate=cost(12), compiler_params=params())(step, push, write, rate)

def picker(tb):
    row = lax.broadcasted_iota(jnp.int32, (tb, tb * 8), 0)
    column = lax.broadcasted_iota(jnp.int32, (tb, tb * 8), 1)
    inside = (column >= row * 8) & (column < row * 8 + 8)
    return jnp.where(inside, 1.0, 0.0).astype(jnp.bfloat16)


def folded(value):
    return sum(value[i : i + 8] for i in range(0, value.shape[0], 8))


def across(value):
    return sum(value[:, i : i + 128] for i in range(0, value.shape[1], 128))


def mat(left, right, dims):
    return lax.dot_general(left, right, (dims, ((), ())), preferred_element_type=f32)


def outputs_kernel(step_ref, push_ref, write_ref, read_ref, rate_ref, first_ref, out_ref, start_ref, held_ref, part_ref):
    rows, tb = step_ref.shape[0], step_ref.shape[1]
    @pl.when(pl.program_id(0) == 0)
    def _():
        held_ref[...] = first_ref[...]
    start_ref[:, 0] = held_ref[...]
    for b in range(rows):
        def group(j, held):
            base = pl.multiple_of(j * UNROLL, UNROLL)
            steps = step_ref[b, pl.ds(base, UNROLL), :]
            pushes = push_ref[b, pl.ds(base, UNROLL), :]
            writes = turned(write_ref, b, base, tb)
            reads = turned(read_ref, b, base, tb)
            for k in range(UNROLL):
                factor = jnp.exp2(steps[k:k+1] * rate_ref[...])
                held = factor * held + writes[:, k:k+1] * pushes[k:k+1]
                part_ref[pl.ds(pl.multiple_of((base + k) * 8, 8), 8), :] = folded(held * reads[:, k:k+1])
            return held
        held_ref[b] = lax.fori_loop(0, tb // UNROLL, group, held_ref[b])
        high = part_ref[...].astype(jnp.bfloat16)
        low = (part_ref[...] - high.astype(f32)).astype(jnp.bfloat16)
        out_ref[b] = mat(picker(tb), high, ((1,), (0,))) + mat(picker(tb), low, ((1,), (0,)))

def scan_outputs(step, push, write, read, rate, first):
    rows, length, chans = step.shape
    states = rate.shape[0]
    tb = min(TB, length)
    big = pl.BlockSpec((rows, tb, chans), lambda i: (0, i, 0))
    thin = pl.BlockSpec((rows, states, tb), lambda i: (0, 0, i))
    whole = pl.BlockSpec((rows, states, chans), lambda i: (0, 0, 0))
    return pl.pallas_call(outputs_kernel, grid=(length // tb,),
        in_specs=[big, big, thin, thin, pl.BlockSpec((states, chans), lambda i: (0, 0)), whole],
        out_specs=[big, pl.BlockSpec((rows, 1, states, chans), lambda i: (0, i, 0, 0))],
        out_shape=[jax.ShapeDtypeStruct((rows, length, chans), f32),
                   jax.ShapeDtypeStruct((rows, length // tb, states, chans), f32)],
        scratch_shapes=[pltpu.VMEM((rows, states, chans), f32), pltpu.VMEM((tb * 8, chans), f32)],
        cost_estimate=cost(21), compiler_params=params())(step, push, write, read, rate, first)

def tail_kernel(step_ref, grad_ref, read_ref, rate_ref, end_ref):
    rows, tb = step_ref.shape[0], step_ref.shape[1]
    @pl.when(pl.program_id(0) == 0)
    def _():
        end_ref[...] = jnp.zeros_like(end_ref)
    def group(j, held):
        base = pl.multiple_of(tb - UNROLL - j * UNROLL, UNROLL)
        held = list(held)
        for b in range(rows):
            steps = step_ref[b, pl.ds(base, UNROLL), :]
            grads = grad_ref[b, pl.ds(base, UNROLL), :]
            reads = turned(read_ref, b, base, tb)
            for k in range(UNROLL - 1, -1, -1):
                factor = jnp.exp2(steps[k:k+1] * rate_ref[...])
                held[b] = factor * (held[b] + reads[:, k:k+1] * grads[k:k+1])
        return tuple(held)
    held = lax.fori_loop(0, tb // UNROLL, group, tuple(end_ref[b] for b in range(rows)))
    for b in range(rows):
        end_ref[b] = held[b]

def scan_tail(step, grad, read, rate):
    rows, length, chans = step.shape
    states = rate.shape[0]
    tb = min(TB, length)
    n = length // tb
    big = pl.BlockSpec((rows, tb, chans), lambda i: (0, n - 1 - i, 0))
    thin = pl.BlockSpec((rows, states, tb), lambda i: (0, 0, n - 1 - i))
    return pl.pallas_call(tail_kernel, grid=(n,),
        in_specs=[big, big, thin, pl.BlockSpec((states, chans), lambda i: (0, 0))],
        out_specs=pl.BlockSpec((rows, states, chans), lambda i: (0, 0, 0)),
        out_shape=jax.ShapeDtypeStruct((rows, states, chans), f32),
        cost_estimate=cost(12), compiler_params=params())(step, grad, read, rate)

def back_kernel(step_ref, push_ref, grad_ref, write_ref, read_ref, rate_ref, start_ref, later_ref,
                decay_ref, weight_ref, gwrite_ref, gread_ref, grate_ref,
                carry_ref, factor_sc, kept_sc, decay_sc, weight_sc, gwrite_sc, gread_sc):
    rows, tb = step_ref.shape[0], step_ref.shape[1]
    states = rate_ref.shape[0]
    @pl.when(pl.program_id(0) == 0)
    def _():
        carry_ref[...] = later_ref[...]
        grate_ref[...] = jnp.zeros_like(grate_ref)
    for b in range(rows):
        def redo(j, held):
            base = pl.multiple_of(j * UNROLL, UNROLL)
            steps = step_ref[b, pl.ds(base, UNROLL), :]
            pushes = push_ref[b, pl.ds(base, UNROLL), :]
            writes = turned(write_ref, b, base, tb)
            for k in range(UNROLL):
                factor = jnp.exp2(steps[k:k+1] * rate_ref[...])
                kept = factor * held
                factor_sc[base + k] = factor
                kept_sc[base + k] = kept
                held = kept + writes[:, k:k+1] * pushes[k:k+1]
            return held
        lax.fori_loop(0, tb // UNROLL, redo, start_ref[b, 0])
        def group(j, carried):
            carry, total = carried
            base = pl.multiple_of(tb - UNROLL_BACK - j * UNROLL_BACK, UNROLL_BACK)
            steps = step_ref[b, pl.ds(base, UNROLL_BACK), :]
            pushes = push_ref[b, pl.ds(base, UNROLL_BACK), :]
            grads = grad_ref[b, pl.ds(base, UNROLL_BACK), :]
            writes = turned(write_ref, b, base, tb)
            reads = turned(read_ref, b, base, tb)
            for k in range(UNROLL_BACK - 1, -1, -1):
                kept = kept_sc[base + k]
                adjoint = reads[:, k:k+1] * grads[k:k+1] + carry
                carry = factor_sc[base + k] * adjoint
                weighted = adjoint * kept
                total = total + weighted * steps[k:k+1]
                eight = pl.ds(pl.multiple_of((base + k) * 8, 8), 8)
                decay_sc[eight, :] = folded(weighted * rate_ref[...])
                weight_sc[eight, :] = folded(adjoint * writes[:, k:k+1])
                wide = pl.ds(pl.multiple_of((base + k) * states, states), states)
                gwrite_sc[wide, :] = across(adjoint * pushes[k:k+1])
                gread_sc[wide, :] = across(kept * grads[k:k+1])
            return (carry, total)
        carry, total = lax.fori_loop(0, tb // UNROLL_BACK, group, (carry_ref[b], grate_ref[...]))
        grate_ref[...] = total
        carry_ref[b] = carry
        pick = picker(tb)
        decay_ref[b] = mat(pick, decay_sc[...].astype(jnp.bfloat16), ((1,), (0,)))
        weight_ref[b] = mat(pick, weight_sc[...].astype(jnp.bfloat16), ((1,), (0,)))
        ones = jnp.ones((8, 128), jnp.bfloat16)
        gwrite_ref[b] = mat(ones, gwrite_sc[...].astype(jnp.bfloat16), ((1,), (1,)))[:1]
        gread_ref[b] = mat(ones, gread_sc[...].astype(jnp.bfloat16), ((1,), (1,)))[:1]

def scan_back(step, push, grad, write, read, rate, starts, later):
    rows, length, chans = step.shape
    states = rate.shape[0]
    tb = min(TB, length)
    n = length // tb
    big = pl.BlockSpec((rows, tb, chans), lambda i: (0, n - 1 - i, 0))
    thin = pl.BlockSpec((rows, states, tb), lambda i: (0, 0, n - 1 - i))
    line = pl.BlockSpec((rows, 1, tb * states), lambda i: (0, 0, n - 1 - i))
    whole = pl.BlockSpec((rows, states, chans), lambda i: (0, 0, 0))
    flat = pl.BlockSpec((states, chans), lambda i: (0, 0))
    return pl.pallas_call(back_kernel, grid=(n,),
        in_specs=[big, big, big, thin, thin, flat, pl.BlockSpec((rows, 1, states, chans), lambda i: (0, n - 1 - i, 0, 0)), whole],
        out_specs=[big, big, line, line, flat],
        out_shape=[jax.ShapeDtypeStruct((rows, length, chans), f32)] * 2
                 + [jax.ShapeDtypeStruct((rows, 1, length * states), f32)] * 2
                 + [jax.ShapeDtypeStruct((states, chans), f32)],
        scratch_shapes=[pltpu.VMEM((rows, states, chans), f32),
                        pltpu.VMEM((tb, states, chans), f32),
                        pltpu.VMEM((tb, states, chans), f32),
                        pltpu.VMEM((tb * 8, chans), f32),
                        pltpu.VMEM((tb * 8, chans), f32),
                        pltpu.VMEM((tb * states, 128), f32),
                        pltpu.VMEM((tb * states, 128), f32)],
        cost_estimate=cost(46), compiler_params=params())(step, push, grad, write, read, rate, starts, later)


def mixer_forward(normed, weights, same, flags, late):
    (
        mixer_in,
        conv_taps,
        conv_bias,
        state_proj,
        step_proj,
        step_bias,
        decay_log,
        skip_gain,
        mixer_out,
    ) = weights
    both = jnp.einsum("rtd,dce->rtce", normed, mixer_in, preferred_element_type=jnp.float32)
    signal = both[:, :, 0].astype(jnp.bfloat16)
    gate = both[:, :, 1]
    taps = conv_taps.shape[0]
    length = signal.shape[1]
    rows = signal.shape[0]
    tail = from_behind(signal[:, length - (taps - 1) :], "seq", 1)
    widened = jnp.concatenate([tail, signal], axis=1).astype(jnp.float32)
    conv_sum = conv_bias + jnp.zeros_like(gate)
    for tap in range(taps):
        conv_sum = (
            conv_sum + conv_taps[tap] * widened[:, tap : tap + length] * same[:, :, tap : tap + 1]
        )
    inner = jax.nn.silu(conv_sum).astype(jnp.bfloat16)
    source = inner.astype(jnp.float32)
    mixed, hop = channel_total(
        jnp.einsum("rte,ec->rtc", inner, state_proj, preferred_element_type=jnp.float32)
    )
    late = gather_rows(nudged(late, hop))
    rank = step_proj.shape[0]
    states = decay_log.shape[0]
    step_low = mixed[:, :, :rank]
    write_in = mixed[:, :, rank : rank + states].astype(jnp.float32)
    read_out = mixed[:, :, rank + states :].astype(jnp.float32)
    step_raw = (
        jnp.einsum("rtk,ke->rte", step_low, step_proj, preferred_element_type=jnp.float32)
        + step_bias
    )
    step = jax.nn.softplus(step_raw)
    rate = -jnp.exp(decay_log)
    step_far = jnp.where(flags[:, :, None] > 0, FAR, step)
    push = step * source
    write_cols = jnp.swapaxes(write_in, 1, 2)
    read_cols = jnp.swapaxes(read_out, 1, 2)
    ends = scan_ends(step_far, push, write_cols, rate * LOG2E)
    span = jnp.where(jnp.max(flags, axis=1)[:, None] > 0, FAR, jnp.sum(step, axis=1))
    incoming = carried_in(ends, span, rate, "seq", False)
    scanned, firsts = scan_outputs(
        step_far, push, write_cols, read_cols, rate * LOG2E, incoming
    )
    result = scanned + skip_gain * source
    gated = (result * jax.nn.silu(gate)).astype(jnp.bfloat16)
    partial_value = jnp.einsum("rte,ed->rtd", gated, mixer_out, preferred_element_type=jnp.float32)
    cache = (
        normed,
        widened,
        gate,
        conv_sum,
        inner,
        source,
        step_low,
        step_raw,
        step,
        step_far,
        push,
        write_in,
        write_cols,
        read_cols,
        result,
        gated,
        firsts,
        span,
    )
    return (partial_value, cache, late)


def mixer_backward(grad_branch, cache, weights, same, flags, first, branch):
    (
        mixer_in,
        conv_taps,
        conv_bias,
        state_proj,
        step_proj,
        step_bias,
        decay_log,
        skip_gain,
        mixer_out,
    ) = weights
    (
        normed,
        widened,
        gate,
        conv_sum,
        inner,
        source,
        step_low,
        step_raw,
        step,
        step_far,
        push,
        write_in,
        write_cols,
        read_cols,
        result,
        gated,
        firsts,
        span,
    ) = cache
    grad_gated = jnp.einsum(
        "rtd,ed->rte", grad_branch, mixer_out, preferred_element_type=jnp.float32
    )
    grad_mixer_out = jnp.einsum(
        "rtd,rte->de", grad_branch, gated, preferred_element_type=jnp.float32
    )
    first_out = plane_first(grad_mixer_out)
    grad_gated = after(grad_gated, first)
    grad_result = grad_gated * jax.nn.silu(gate)
    grad_gate = grad_gated * result * silu_slope(gate)
    grad_skip = jnp.sum(grad_result * source, axis=(0, 1))
    rate = -jnp.exp(decay_log)
    tail = scan_tail(step_far, grad_result, read_cols, rate * LOG2E)
    second_out = plane_second(*first_out)
    first = [plane_third(held, tail) for held in first]
    first, arrived = ([pair[0] for pair in first], [pair[1] for pair in first])
    later = carried_in(tail, span, rate, "seq", True)
    decays, weights_back, write_back, read_back, grad_rate = scan_back(
        step_far, push, grad_result, write_cols, read_cols, rate * LOG2E, firsts, later
    )
    grad_mixer_out, _ = plane_third(second_out, grad_rate)
    grad_step = decays * (1.0 / LOG2E) + weights_back * source
    grad_source = weights_back * step
    grad_write = write_back.reshape(write_in.shape)
    grad_read = read_back.reshape(write_in.shape) + write_in * jnp.sum(
        push * grad_result, axis=2, keepdims=True
    )
    grad_source = grad_source + skip_gain * grad_result
    grad_step_raw = (grad_step * jax.nn.sigmoid(step_raw)).astype(jnp.bfloat16)
    grad_step_bias = jnp.sum(grad_step_raw.astype(jnp.float32), axis=(0, 1))
    grad_step_proj = jnp.einsum(
        "rtk,rte->ke", step_low, grad_step_raw, preferred_element_type=jnp.float32
    )
    grad_low = jnp.einsum(
        "rte,ke->rtk", grad_step_raw, step_proj, preferred_element_type=jnp.float32
    )
    grad_mixed, _ = channel_total(
        jnp.concatenate([after(grad_low, arrived, branch), grad_write, grad_read], axis=-1)
    )
    grad_state_proj = jnp.einsum(
        "rte,rtc->ce", inner, grad_mixed, preferred_element_type=jnp.float32
    )
    spread = jnp.einsum("rtc,ec->rte", grad_mixed, state_proj, preferred_element_type=jnp.float32)
    grad_source = grad_source + after(spread, first_out[0])
    grad_conv = grad_source * silu_slope(conv_sum)
    length = grad_conv.shape[1]
    taps = conv_taps.shape[0]
    reach = taps - 1
    terms = [grad_conv * same[:, :, tap : tap + 1] for tap in range(taps)]
    grad_taps = [
        jnp.sum(widened[:, tap : tap + length] * terms[tap], axis=(0, 1)) for tap in range(taps)
    ]
    grad_conv_bias = jnp.sum(grad_conv, axis=(0, 1))
    heads = [conv_taps[tap] * terms[tap][:, :reach] for tap in range(taps)]
    head = sum(
        jnp.pad(heads[tap][:, : reach - tap], ((0, 0), (tap, 0), (0, 0))) for tap in range(reach)
    )
    returned = from_behind(head, "seq", -1)
    grad_signal = jnp.pad(returned, ((0, 0), (length - reach, 0), (0, 0)))
    for tap in range(taps):
        shift = reach - tap
        grad_signal = grad_signal + conv_taps[tap] * jnp.pad(
            terms[tap][:, shift:], ((0, 0), (0, shift), (0, 0))
        )
    grad_both = jnp.stack([grad_signal, grad_gate], axis=2).astype(jnp.bfloat16)
    grad_mixer_in = jnp.einsum(
        "rtd,rtce->dce", normed, grad_both, preferred_element_type=jnp.float32
    )
    grad_normed = jnp.einsum(
        "rtce,dce->rtd", grad_both, mixer_in, preferred_element_type=jnp.float32
    )
    small = (
        jnp.stack(grad_taps),
        grad_conv_bias[None],
        grad_state_proj,
        grad_step_proj,
        grad_step_bias[None],
        grad_rate * rate,
        grad_skip[None],
    )
    return (grad_normed, grad_mixer_in, grad_mixer_out, small, first, second_out)


def dense_forward(normed, dense_in, dense_out):
    both = jnp.einsum(
        "rtd,dcf->rtcf", normed, dense_in, preferred_element_type=jnp.float32
    ).astype(jnp.bfloat16)
    gate = both[:, :, 0]
    upper = both[:, :, 1]
    hidden = jax.nn.silu(gate.astype(jnp.float32)) * upper.astype(jnp.float32)
    hidden = hidden.astype(jnp.bfloat16)
    partial_value = jnp.einsum("rtf,fd->rtd", hidden, dense_out, preferred_element_type=jnp.float32)
    return (partial_value, (normed, gate, upper, hidden))


def dense_backward(grad_branch, cache, dense_in, dense_out, event=()):
    normed, gate, upper, hidden = cache
    gate, upper = (gate.astype(jnp.float32), upper.astype(jnp.float32))
    grad_hidden = jnp.einsum(
        "rtd,fd->rtf", grad_branch, dense_out, preferred_element_type=jnp.float32
    )
    grad_hidden = after(grad_hidden, event)
    grad_gate = grad_hidden * upper * silu_slope(gate)
    grad_upper = grad_hidden * jax.nn.silu(gate)
    grad_both = jnp.stack([grad_gate, grad_upper], axis=2).astype(jnp.bfloat16)
    grad_normed = jnp.einsum(
        "rtcf,dcf->rtd", grad_both, dense_in, preferred_element_type=jnp.float32
    )
    grad_dense_out = jnp.einsum(
        "rtd,rtf->df", grad_branch, hidden, preferred_element_type=jnp.float32
    )
    grad_dense_in = jnp.einsum(
        "rtd,rtcf->dcf", normed, grad_both, preferred_element_type=jnp.float32
    )
    return (grad_normed, [plane_first(grad_dense_in), plane_first(grad_dense_out)])


def plan_of(length):
    block = min(QBLOCK, length)
    return (block, (WINDOW + block) // block)


def lower_edge(info_ref, row, first, block):
    lane = lax.broadcasted_iota(jnp.int32, (1, block), 1)
    place = info_ref[row, 0] + first + lane
    start = jnp.zeros((1, block), jnp.int32)
    for index in range(1, info_ref.shape[1]):
        entry = info_ref[row, index]
        start = jnp.maximum(start, jnp.where(entry <= place, entry, 0))
    return (jnp.maximum(lane + 1, start - (info_ref[row, 0] + first - WINDOW)), lane)


def piece_mask(low, lane, piece, block, pieces):
    index = piece * block + lax.broadcasted_iota(jnp.int32, (block, block), 0)
    allowed = index >= low
    if piece == pieces - 1:
        allowed = allowed & (index <= lane + WINDOW)
    return allowed


NT = (((1,), (1,)), ((), ()))
TN = (((0,), (0,)), ((), ()))
NN = (((1,), (0,)), ((), ()))


def dot(left, right, dims):
    return lax.dot_general(left, right, dims, preferred_element_type=f32)


def gathered_pieces(refs, wide):
    length = refs[0].shape[1]
    for index, ref in enumerate(refs):
        wide[pl.ds(index * length, length), :] = ref[0]


def attend_kernel(
    pieces, skip, info_ref, query_ref, second_ref, first_ref, own_ref, out_ref, total_ref, wide, held
):
    block = query_ref.shape[1]

    @pl.when(pl.program_id(1) == 0)
    def _():
        gathered_pieces((second_ref, first_ref, own_ref), wide)

    first = pl.multiple_of(pl.program_id(1) * block, block)
    low, lane = lower_edge(info_ref, pl.program_id(0), first, block)
    query = query_ref[0]
    top = jnp.full((1, block), masked_score, f32)
    for piece in range(pieces):
        at = pl.ds(pl.multiple_of(first + skip + piece * block, block), block)
        scores = dot(wide[at, :HDIM], query, NT)
        scores = jnp.where(piece_mask(low, lane, piece, block, pieces), scores, masked_score)
        held[piece] = scores
        top = jnp.maximum(top, jnp.max(scores, axis=0, keepdims=True))
    slope = HDIM ** (-0.5) * LOG2E
    total = jnp.zeros((1, block), f32)
    summed = jnp.zeros((HDIM, block), f32)
    for piece in range(pieces):
        at = pl.ds(pl.multiple_of(first + skip + piece * block, block), block)
        soft = jnp.exp2((held[piece] - top) * slope)
        total = total + jnp.sum(soft, axis=0, keepdims=True)
        summed = summed + dot(wide[at, HDIM:], soft.astype(jnp.bfloat16), TN)
    out_ref[0] = (summed / total).T.astype(jnp.bfloat16)
    total_ref[0] = top * slope + jnp.log2(total)


def head_specs(query, head):
    rows, length = (query.shape[0], query.shape[1])
    block, pieces = plan_of(length)
    halo = pl.BlockSpec((1, length, 2 * HDIM), lambda i, j: (i, 0, 0))
    own = pl.BlockSpec((1, length, 2 * HDIM), lambda i, j: (i, 0, head))
    narrow = pl.BlockSpec((1, block, HDIM), lambda i, j: (i, j, head))
    plain = pl.BlockSpec((1, block, HDIM), lambda i, j: (i, j, 0))
    line = pl.BlockSpec((1, 1, block), lambda i, j: (i, 0, j))
    skip = 2 * length - WINDOW
    return (rows, length, block, pieces, skip, halo, own, narrow, plain, line)


def attend(info, query, seconds, firsts, pairs, head):
    rows, length, block, pieces, skip, halo, own, narrow, plain, line = head_specs(query, head)
    body = lambda *refs: attend_kernel(pieces, skip, *refs)
    return pl.pallas_call(
        body,
        grid=(rows, length // block),
        in_specs=[pl.BlockSpec(memory_space=pltpu.SMEM), narrow, halo, halo, own],
        out_specs=[plain, line],
        out_shape=[
            jax.ShapeDtypeStruct((rows, length, HDIM), jnp.bfloat16),
            jax.ShapeDtypeStruct((rows, 1, length), f32),
        ],
        scratch_shapes=[
            pltpu.VMEM((3 * length, 2 * HDIM), jnp.bfloat16),
            pltpu.VMEM((pieces, block, block), f32),
        ],
        cost_estimate=cost(7),
        compiler_params=pltpu.CompilerParams(vmem_limit_bytes=VM),
    )(info, query, seconds, firsts, pairs)


def attend_back_kernel(
    pieces, skip, info_ref, query_ref, grad_ref, second_ref, first_ref, own_ref, total_ref, done_ref,
    gquery_ref, gsecond_ref, gfirst_ref, gown_ref, wide, gkeys, gvalues,
):
    block, length = (query_ref.shape[1], own_ref.shape[1])
    first = pl.multiple_of(pl.program_id(1) * block, block)
    low, lane = lower_edge(info_ref, pl.program_id(0), first, block)

    @pl.when(pl.program_id(1) == 0)
    def _():
        gathered_pieces((second_ref, first_ref, own_ref), wide)
        gkeys[...] = jnp.zeros_like(gkeys)
        gvalues[...] = jnp.zeros_like(gvalues)

    query, grad = (query_ref[0], grad_ref[0])
    total = total_ref[0]
    both = grad.astype(f32) * done_ref[0].astype(f32)
    delta = lax.dot_general(
        jnp.ones((8, HDIM), f32), both, NT, precision=lax.Precision.HIGHEST
    )[:1]
    slope = HDIM ** (-0.5) * LOG2E
    summed = jnp.zeros((HDIM, block), f32)
    for piece in range(pieces):
        at = pl.ds(pl.multiple_of(first + skip + piece * block, block), block)
        keys = wide[at, :HDIM]
        scores = dot(keys, query, NT)
        allowed = piece_mask(low, lane, piece, block, pieces)
        soft = jnp.exp2(jnp.where(allowed, scores * slope - total, masked_score))
        gvalues[at, :] += dot(soft.astype(jnp.bfloat16), grad, NN)
        spread = soft * (dot(wide[at, HDIM:], grad, NT) - delta)
        spread = spread.astype(jnp.bfloat16)
        gkeys[at, :] += dot(spread, query, NN)
        summed = summed + dot(keys, spread, TN)
    gquery_ref[0] = (summed * HDIM ** (-0.5)).T.astype(jnp.bfloat16)

    @pl.when(pl.program_id(1) == pl.num_programs(1) - 1)
    def _():
        for index, ref in enumerate((gsecond_ref, gfirst_ref, gown_ref)):
            at = pl.ds(index * length, length)
            ref[0, :, :HDIM] = (gkeys[at, :] * HDIM ** (-0.5)).astype(ref.dtype)
            ref[0, :, HDIM:] = gvalues[at, :].astype(ref.dtype)


def attend_back(info, query, grad, seconds, firsts, pairs, total, attended, head):
    rows, length, block, pieces, skip, halo, own, narrow, plain, line = head_specs(query, head)
    body = lambda *refs: attend_back_kernel(pieces, skip, *refs)
    double = (rows, length, 2 * HDIM)
    return pl.pallas_call(
        body,
        grid=(rows, length // block),
        in_specs=[
            pl.BlockSpec(memory_space=pltpu.SMEM),
            narrow,
            narrow,
            halo,
            halo,
            own,
            line,
            narrow,
        ],
        out_specs=[plain, halo, halo, halo],
        out_shape=[
            jax.ShapeDtypeStruct((rows, length, HDIM), jnp.bfloat16),
            jax.ShapeDtypeStruct(double, f32),
            jax.ShapeDtypeStruct(double, jnp.bfloat16),
            jax.ShapeDtypeStruct(double, f32),
        ],
        scratch_shapes=[
            pltpu.VMEM((3 * length, 2 * HDIM), jnp.bfloat16),
            pltpu.VMEM((3 * length, HDIM), f32),
            pltpu.VMEM((3 * length, HDIM), f32),
        ],
        cost_estimate=cost(12),
        compiler_params=pltpu.CompilerParams(vmem_limit_bytes=VM),
    )(info, query, grad, seconds, firsts, pairs, total, attended)


def by_head(attend_in):
    features, heads = (attend_in.shape[0], attend_in.shape[2] // HDIM)
    split = attend_in.reshape(features, 3, heads, HDIM)
    pairs = jnp.swapaxes(split[:, 1:], 1, 2).reshape(features, 2 * heads * HDIM)
    return (attend_in[:, 0], pairs)


def attention_forward(normed, attend_in, attend_out, info):
    heads = attend_in.shape[2] // HDIM
    weight_query, weight_pairs = by_head(attend_in)
    pairs = rowwise(
        jnp.einsum(
            "rtd,dh->rth", normed, weight_pairs, preferred_element_type=jnp.float32
        ).astype(jnp.bfloat16)
    )
    query = rowwise(
        jnp.einsum(
            "rtd,dh->rth", normed, weight_query, preferred_element_type=jnp.float32
        ).astype(jnp.bfloat16)
    )
    odd = lax.axis_index("seq") % 2 == 1
    halos, results = ([], [])
    for head in range(heads):
        own = rowwise(pairs[:, :, 2 * head * HDIM : 2 * (head + 1) * HDIM])
        seconds = rowwise(from_behind(own, "seq", 2))
        firsts = rowwise(partner(rowwise(jnp.where(odd, seconds, own)), "seq", 1))
        halos.append((seconds, firsts))
        results.append(attend(info, query, seconds, firsts, pairs, head))
    attended = rowwise(jnp.concatenate([result[0] for result in results], axis=2))
    totals = [result[1] for result in results]
    partial_value = jnp.einsum(
        "rth,hd->rtd", attended, attend_out, preferred_element_type=jnp.float32
    )
    return (partial_value, (normed, query, pairs, halos, attended, totals, weight_query, weight_pairs))


def attention_backward(grad_branch, cache, attend_in, attend_out, info, event):
    normed, query, own_pairs, halos, attended, totals, weight_query, weight_pairs = cache
    rows, length = (query.shape[0], query.shape[1])
    heads = query.shape[2] // HDIM
    grad_attended = jnp.einsum(
        "rtd,hd->rth", grad_branch, attend_out, preferred_element_type=jnp.float32
    )
    grad_attended = rowwise(after(grad_attended, event).astype(jnp.bfloat16))
    grad_attend_out = jnp.einsum(
        "rtd,rth->dh", grad_branch, attended, preferred_element_type=jnp.float32
    )
    odd = lax.axis_index("seq") % 2 == 1
    queries, pairs, marks = ([], [], [[], []])
    for head in range(heads):
        grad_query, second, given, own = attend_back(
            after(info, marks[head]),
            query,
            grad_attended,
            *halos[head],
            own_pairs,
            totals[head],
            attended,
            head,
        )
        queries.append(grad_query)
        given = rowwise(partner(given, "seq", 1)).astype(jnp.float32)
        sent = rowwise((second + jnp.where(odd, given, 0.0)).astype(jnp.bfloat16))
        marks.append(sent)
        back = rowwise(from_behind(sent, "seq", -2))
        pairs.append((own + jnp.where(odd, 0.0, given) + back.astype(jnp.float32)).astype(jnp.bfloat16))
    grad_projected = rowwise(jnp.concatenate(queries + pairs, axis=2))
    grad_weight = jnp.einsum(
        "rtd,rth->dh", normed, grad_projected, preferred_element_type=jnp.float32
    )
    flat = jnp.concatenate([weight_query, weight_pairs], axis=1)
    grad_normed = jnp.einsum(
        "rth,dh->rtd", grad_projected, flat, preferred_element_type=jnp.float32
    )
    return (grad_normed, [plane_first(grad_weight), plane_first(grad_attend_out)])


def in_order(grad_weight, heads):
    features = grad_weight.shape[0]
    query = grad_weight[:, : heads * HDIM].reshape(features, 1, heads, HDIM)
    pairs = grad_weight[:, heads * HDIM :].reshape(features, heads, 2, HDIM)
    both = jnp.concatenate([query, jnp.swapaxes(pairs, 1, 2)], axis=1)
    return both.reshape(features, 3, heads * HDIM)


def shards(
    block_in,
    block_grad,
    norm_gains,
    mixer_in,
    conv_taps,
    conv_bias,
    state_proj,
    step_proj,
    step_bias,
    decay_log,
    skip_gain,
    mixer_out,
    first_in,
    first_out,
    attend_in,
    attend_out,
    second_in,
    second_out,
    row_counts,
    doc_starts,
    row_mask,
):
    local_len = block_in.shape[1]
    length = local_len * lax.axis_size("tp")
    anchor = lax.axis_index("seq") * length
    positions = anchor + jnp.arange(length, dtype=jnp.int32)
    own_place = anchor + lax.axis_index("tp") * local_len + jnp.arange(local_len, dtype=jnp.int32)
    valid = ((own_place[None, :] < row_counts[:, None]) & (row_mask[:, None] == 1)).astype(
        jnp.float32
    )[:, :, None]
    documents = doc_numbers(positions, doc_starts)
    flags = jnp.any(doc_starts[:, None, :] == positions[None, :, None], axis=-1).astype(jnp.float32)
    taps = conv_taps.shape[0]
    same = jnp.stack(
        [
            (
                (positions - (taps - 1 - tap) >= 0)[None, :]
                & (doc_numbers(positions - (taps - 1 - tap), doc_starts) == documents)
            ).astype(jnp.float32)
            for tap in range(taps)
        ],
        axis=-1,
    )
    here = jnp.broadcast_to(anchor, (doc_starts.shape[0], 1)).astype(jnp.int32)
    info = jnp.concatenate([here, doc_starts], axis=1)
    mixer_weights = (
        mixer_in,
        conv_taps,
        conv_bias,
        state_proj,
        step_proj,
        step_bias,
        decay_log,
        skip_gain,
        mixer_out,
    )
    grad_stream = rowwise(block_grad * valid)
    unit = block_in * lax.rsqrt(jnp.mean(block_in * block_in, axis=-1, keepdims=True) + epsilon)
    normed = (unit * norm_gains[0]).astype(jnp.bfloat16)
    gathered = gather_rows(normed)
    partial_value, cache_mix, grad_second = mixer_forward(
        gathered, mixer_weights, same, flags, grad_stream.astype(jnp.bfloat16)
    )
    stream_mix, normed = norm_forward(
        block_in, reduce_rows(partial_value, grad_second), norm_gains[1]
    )
    partial_value, cache_first = dense_forward(gather_rows(normed), first_in, first_out)
    stream_first, normed = norm_forward(stream_mix, reduce_rows(partial_value), norm_gains[2])
    partial_value, cache_attend = attention_forward(
        gather_rows(normed), attend_in, attend_out, info
    )
    stream_attend, normed = norm_forward(stream_first, reduce_rows(partial_value), norm_gains[3])
    partial_out, cache_second = dense_forward(
        gather_rows(normed), second_in, second_out
    )
    partial_out = partial_out.astype(jnp.bfloat16)

    def gain_of(which, low, cache):
        return gain_share(low, cache[0], norm_gains[which])

    grad_normed, firsts = dense_backward(grad_second, cache_second, second_in, second_out)
    low = grad_normed.astype(jnp.bfloat16)
    gain_four = gain_of(3, low, cache_second)
    grad_stream, grad_low = norm_backward(
        stream_attend,
        grad_stream,
        reduce_rows(low),
        after(norm_gains[3], firsts[0][0], firsts[1][0], gain_four, partial_out),
    )
    second = [plane_second(*pair) for pair in firsts]
    gathered = gather_rows(grad_low)
    grad_normed, firsts = attention_backward(
        gathered, cache_attend, attend_in, attend_out, info, second
    )
    low = grad_normed.astype(jnp.bfloat16)
    gain_three = gain_of(2, low, cache_attend)
    second = [plane_third(held, grad_normed)[0] for held in second]
    grad_stream, grad_low = norm_backward(
        stream_first,
        grad_stream,
        reduce_rows(low),
        after(norm_gains[2], firsts[0][0], firsts[1][0], second[0], second[1], gain_three),
    )
    middle = [plane_second(*pair) for pair in firsts]
    grad_normed, firsts = dense_backward(
        gather_rows(grad_low), cache_first, first_in, first_out, middle
    )
    middle = [plane_third(held)[0] for held in middle]
    low = grad_normed.astype(jnp.bfloat16)
    gain_two = gain_of(1, low, cache_first)
    grad_stream, grad_low = norm_backward(
        stream_mix,
        grad_stream,
        reduce_rows(low),
        after(norm_gains[1], firsts[0][0], firsts[1][0], middle[0], middle[1], gain_two),
    )
    firsts = [plane_second(*pair) for pair in firsts]
    gathered = gather_rows(grad_low)
    branch = reduce_rows(partial_out, gathered)
    block_out = (stream_attend + branch.astype(jnp.float32)) * valid
    grad_normed, grad_mixer_in, grad_mixer_out, small, first, second_out = mixer_backward(
        gathered,
        cache_mix,
        mixer_weights,
        same,
        flags,
        firsts,
        branch,
    )
    low = grad_normed.astype(jnp.bfloat16)
    gains = jnp.stack([gain_of(0, low, cache_mix), gain_two, gain_three, gain_four])
    parted = plane_first(grad_mixer_in)
    grad_normed = reduce_rows(low)
    wide = small[0].shape[1]
    small = small + (gains.reshape(-1, wide),)
    counts = [member.shape[0] for member in small]
    packed = after(jnp.concatenate(small), second_out)
    packed = spread_sum(packed, ("seq", "row"), jnp.bfloat16)
    parted = (after(parted[0], packed),) + parted[1:]
    grad_mixer_in, _ = plane_third(plane_second(*parted))
    small, place = ([], 0)
    for count in counts:
        small.append(packed[place : place + count])
        place += count
    gains = spread_sum(small.pop(), ("tp",), jnp.float32).reshape(gains.shape)
    grad_stream, _ = norm_backward(block_in, grad_stream, grad_normed, norm_gains[0])
    middle[0] = in_order(middle[0], attend_in.shape[2] // HDIM)
    pairs = ((grad_mixer_in, grad_mixer_out), first, middle, second)
    flat = [member for pair in pairs for member in (pair[0], pair[1].T)]
    return (
        block_out,
        grad_stream,
        gains,
        flat[0],
        small[0],
        small[1][0],
        small[2].T,
        small[3],
        small[4][0],
        small[5],
        small[6][0],
        flat[1],
        flat[2],
        flat[3],
        flat[4],
        flat[5],
        flat[6],
        flat[7],
    )


def solution(mesh):
    in_specs = (
        P("row", ("seq", "tp"), None),
        P("row", ("seq", "tp"), None),
        P(),
        P(None, None, "tp"),
        P(None, "tp"),
        P("tp"),
        P("tp", None),
        P(None, "tp"),
        P("tp"),
        P(None, "tp"),
        P("tp"),
        P("tp", None),
        P(None, None, "tp"),
        P("tp", None),
        P(None, None, "tp"),
        P("tp", None),
        P(None, None, "tp"),
        P("tp", None),
        P("row"),
        P("row", None),
        P("row"),
    )
    out_specs = (
        P("row", ("seq", "tp"), None),
        P("row", ("seq", "tp"), None),
        P(),
        P(("row", "seq"), None, "tp"),
        P(None, "tp"),
        P("tp"),
        P("tp", None),
        P(None, "tp"),
        P("tp"),
        P(None, "tp"),
        P("tp"),
        P("tp", ("row", "seq")),
        P(("row", "seq"), None, "tp"),
        P("tp", ("row", "seq")),
        P(("row", "seq"), None, "tp"),
        P("tp", ("row", "seq")),
        P(("row", "seq"), None, "tp"),
        P("tp", ("row", "seq")),
    )
    return jax.shard_map(shards, mesh=mesh, in_specs=in_specs, out_specs=out_specs, check_vma=False)
```

```python
import jax
import jax.numpy as jnp
from jax import lax
from jax.experimental import pallas as pl
from jax.experimental.layout import Layout, with_layout_constraint
from jax.experimental.pallas import tpu as pltpu
from jax.sharding import PartitionSpec as P

HDIM = 128
WINDOW = 2048
f32 = jnp.float32
LOG2E = 1.4426950408889634
FAR = 1e30
QBLOCK = 256


epsilon = 1e-05
masked_score = -1e30


def carried_in(state, span, rate, axis, backward):
    both = jnp.concatenate([state, span[:, None, :]], axis=1)
    sign = -1 if backward else 1
    total = jnp.zeros_like(state)
    for by in range(lax.axis_size(axis) - 1, 0, -1):
        piece = from_behind(both, axis, sign * by)
        total = jnp.exp(rate[None] * piece[:, -1:, :]) * total + piece[:, :-1]
    return total


def from_behind(x, axis, by):
    peers = lax.axis_size(axis)
    pairs = [(i, i + by) for i in range(peers) if 0 <= i + by < peers]
    return lax.ppermute(x, axis, pairs)


def gather_rows(local):
    return lax.all_gather(local, "tp", axis=1, tiled=True)


def reduce_rows(partial_value, event=()):
    low = partial_value.astype(jnp.bfloat16)
    if jax.tree.leaves(event):
        low = nudged(low, event)
    return lax.psum_scatter(low, "tp", scatter_dimension=1, tiled=True)


def nudged(value, *events):
    corner = lax.slice(value, (0,) * value.ndim, (1,) * value.ndim)
    return lax.dynamic_update_slice(value, after(corner, *events), (0,) * value.ndim)


def after(value, *events):
    marks = [event[(0,) * event.ndim].astype(jnp.float32) for event in jax.tree.leaves(events)]
    if not marks:
        return value
    return value + (sum(marks) * 0.0).astype(value.dtype)


def rowwise(value):
    return with_layout_constraint(value, Layout(tuple(range(value.ndim))))


def spread_sum(value, axes, kind):
    for axis in axes:
        flip = 1
        while flip < lax.axis_size(axis):
            other = partner(value.astype(kind), axis, flip)
            value = value + other.astype(value.dtype)
            flip *= 2
    return value


def partner(x, axis, flip):
    return lax.ppermute(x, axis, [(i, i ^ flip) for i in range(lax.axis_size(axis))])


def channel_total(partial_value):
    low = partial_value.astype(jnp.bfloat16).astype(jnp.float32)
    flip, hops = (1, [])
    while flip < lax.axis_size("tp"):
        hops.append(partner(low.astype(jnp.bfloat16), "tp", flip))
        low = (low + hops[-1].astype(jnp.float32)).astype(jnp.bfloat16).astype(jnp.float32)
        flip *= 2
    return (low.astype(jnp.bfloat16), hops[0])


def plane_first(grad):
    if lax.axis_size("row") != 2:
        return (grad.astype(jnp.bfloat16),)
    held = grad.reshape((2, 2, 2, grad.shape[0] // 8) + grad.shape[1:])
    place = lax.axis_index("seq") % 2
    given = lax.dynamic_slice_in_dim(held, 1 - place, 1, axis=2).astype(jnp.bfloat16)
    kept = lax.dynamic_slice_in_dim(held, place, 1, axis=2).astype(jnp.bfloat16)
    return (given, kept)


def joined(given, kept, name, flip):
    other = partner(given, name, flip).astype(jnp.float32)
    return kept.astype(jnp.float32) + other


def plane_second(given, kept=None):
    if kept is None:
        return lax.psum_scatter(given, ("row", "seq"), scatter_dimension=0, tiled=True)
    row = lax.axis_index("row")
    held = joined(given, kept, "seq", 1).astype(jnp.bfloat16)
    given = lax.dynamic_slice_in_dim(held, 1 - row, 1, axis=0)
    held = joined(given, lax.dynamic_slice_in_dim(held, row, 1, axis=0), "row", 1)
    return held.astype(jnp.bfloat16)


def plane_third(held, event=()):
    if lax.axis_size("row") != 2:
        return (held.astype(jnp.float32), held)
    seq = lax.axis_index("seq")
    given = after(lax.dynamic_slice_in_dim(held, 1 - seq // 2, 1, axis=1), event)
    kept = lax.dynamic_slice_in_dim(held, seq // 2, 1, axis=1)
    other = partner(given, "seq", 2)
    total = kept.astype(jnp.float32) + other.astype(jnp.float32)
    return (total.reshape(total.shape[3:]), other)


def plane_halves(given, kept=None):
    if kept is None:
        return plane_second(given).astype(jnp.float32)
    row, half = (lax.axis_index("row"), lax.axis_index("seq") // 2)
    held = joined(given, kept, "seq", 1).astype(jnp.bfloat16)
    results = []
    for index in range(2):
        part = held[..., index, :]
        hops = [(0, row, "row", 1), (1, half, "seq", 2)]
        for axis, place, name, flip in hops if index == 0 else hops[::-1]:
            given = lax.dynamic_slice_in_dim(part, 1 - place, 1, axis=axis)
            part = lax.dynamic_slice_in_dim(part, place, 1, axis=axis)
            part = joined(given.astype(jnp.bfloat16), part, name, flip)
        results.append(part.reshape(part.shape[3:]))
    return jnp.stack(results, axis=1)


def doc_numbers(positions, starts):
    return jnp.sum((starts[:, None, :] <= positions[None, :, None]).astype(jnp.int32), axis=-1)


def norm_kernel(stream_ref, part_ref, gain_ref, out_ref, normed_ref):
    stream = stream_ref[0] + part_ref[0].astype(f32)
    scale = lax.rsqrt(jnp.mean(stream * stream, axis=-1, keepdims=True) + epsilon)
    out_ref[0] = stream
    normed_ref[0] = (stream * scale * gain_ref[...]).astype(jnp.bfloat16)


def norm_specs(stream):
    rows, length, features = stream.shape
    block = min(128, length)
    tile = pl.BlockSpec((1, block, features), lambda i, j: (i, j, 0))
    return ((rows, length // block), tile, pl.BlockSpec((1, features), lambda i, j: (0, 0)))


def norm_forward(stream, part, gain):
    grid, tile, line = norm_specs(stream)
    return pl.pallas_call(
        norm_kernel,
        grid=grid,
        in_specs=[tile, tile, line],
        out_specs=[tile, tile],
        out_shape=[
            jax.ShapeDtypeStruct(stream.shape, f32),
            jax.ShapeDtypeStruct(stream.shape, jnp.bfloat16),
        ],
        cost_estimate=cost(2),
    )(stream, part, gain[None])


def norm_back_kernel(stream_ref, grad_ref, part_ref, gain_ref, out_ref, low_ref):
    stream = stream_ref[0]
    scale = lax.rsqrt(jnp.mean(stream * stream, axis=-1, keepdims=True) + epsilon)
    unit = stream * scale
    scaled = part_ref[0].astype(f32) * gain_ref[...]
    mean = jnp.mean(scaled * unit, axis=-1, keepdims=True)
    grad = grad_ref[0] + scale * (scaled - unit * mean)
    out_ref[0] = grad
    low_ref[0] = grad.astype(jnp.bfloat16)


def norm_backward(stream, grad, part, gain):
    grid, tile, line = norm_specs(stream)
    return pl.pallas_call(
        norm_back_kernel,
        grid=grid,
        in_specs=[tile, tile, tile, line],
        out_specs=[tile, tile],
        out_shape=[
            jax.ShapeDtypeStruct(stream.shape, f32),
            jax.ShapeDtypeStruct(stream.shape, jnp.bfloat16),
        ],
        cost_estimate=cost(2),
    )(stream, grad, part, gain[None])


def gain_share(partial_value, normed, gain):
    product = partial_value.astype(jnp.float32) * normed.astype(jnp.float32)
    return jnp.sum(product, axis=(0, 1)) / gain


def silu_slope(value):
    logistic = jax.nn.sigmoid(value)
    return logistic * (1.0 + value * (1.0 - logistic))


TB = 128
UNROLL = 128
UNROLL_BACK = 64
VM = 48 * 1024 * 1024

def cost(microseconds):
    return pl.CostEstimate(
        flops=int(microseconds * 1e9), bytes_accessed=int(microseconds * 3e6), transcendentals=0
    )


def params():
    return pltpu.CompilerParams(vmem_limit_bytes=VM, dimension_semantics=("arbitrary",))

def turned(ref, b, base, tb):
    return pltpu.roll(ref[b], lax.rem(tb - base, tb), axis=1)

def ends_kernel(step_ref, push_ref, write_ref, rate_ref, end_ref):
    rows, tb = step_ref.shape[0], step_ref.shape[1]
    @pl.when(pl.program_id(0) == 0)
    def _():
        end_ref[...] = jnp.zeros_like(end_ref)
    def group(j, held):
        base = pl.multiple_of(j * UNROLL, UNROLL)
        held = list(held)
        for b in range(rows):
            steps = step_ref[b, pl.ds(base, UNROLL), :]
            pushes = push_ref[b, pl.ds(base, UNROLL), :]
            writes = turned(write_ref, b, base, tb)
            for k in range(UNROLL):
                factor = jnp.exp2(steps[k:k+1] * rate_ref[...])
                held[b] = factor * held[b] + writes[:, k:k+1] * pushes[k:k+1]
        return tuple(held)
    held = lax.fori_loop(0, tb // UNROLL, group, tuple(end_ref[b] for b in range(rows)))
    for b in range(rows):
        end_ref[b] = held[b]

def scan_ends(step, push, write, rate):
    rows, length, chans = step.shape
    states = rate.shape[0]
    tb = min(TB, length)
    big = pl.BlockSpec((rows, tb, chans), lambda i: (0, i, 0))
    thin = pl.BlockSpec((rows, states, tb), lambda i: (0, 0, i))
    return pl.pallas_call(ends_kernel, grid=(length // tb,),
        in_specs=[big, big, thin, pl.BlockSpec((states, chans), lambda i: (0, 0))],
        out_specs=pl.BlockSpec((rows, states, chans), lambda i: (0, 0, 0)),
        out_shape=jax.ShapeDtypeStruct((rows, states, chans), f32),
        cost_estimate=cost(12), compiler_params=params())(step, push, write, rate)

def picker(tb):
    row = lax.broadcasted_iota(jnp.int32, (tb, tb * 8), 0)
    column = lax.broadcasted_iota(jnp.int32, (tb, tb * 8), 1)
    inside = (column >= row * 8) & (column < row * 8 + 8)
    return jnp.where(inside, 1.0, 0.0).astype(jnp.bfloat16)


def folded(value):
    return sum(value[i : i + 8] for i in range(0, value.shape[0], 8))


def across(value):
    return sum(value[:, i : i + 128] for i in range(0, value.shape[1], 128))


def mat(left, right, dims):
    return lax.dot_general(left, right, (dims, ((), ())), preferred_element_type=f32)


def outputs_kernel(step_ref, push_ref, write_ref, read_ref, rate_ref, first_ref, out_ref, start_ref, held_ref, part_ref):
    rows, tb = step_ref.shape[0], step_ref.shape[1]
    @pl.when(pl.program_id(0) == 0)
    def _():
        held_ref[...] = first_ref[...]
    start_ref[:, 0] = held_ref[...]
    for b in range(rows):
        def group(j, held):
            base = pl.multiple_of(j * UNROLL, UNROLL)
            steps = step_ref[b, pl.ds(base, UNROLL), :]
            pushes = push_ref[b, pl.ds(base, UNROLL), :]
            writes = turned(write_ref, b, base, tb)
            reads = turned(read_ref, b, base, tb)
            for k in range(UNROLL):
                factor = jnp.exp2(steps[k:k+1] * rate_ref[...])
                held = factor * held + writes[:, k:k+1] * pushes[k:k+1]
                part_ref[pl.ds(pl.multiple_of((base + k) * 8, 8), 8), :] = folded(held * reads[:, k:k+1])
            return held
        held_ref[b] = lax.fori_loop(0, tb // UNROLL, group, held_ref[b])
        high = part_ref[...].astype(jnp.bfloat16)
        low = (part_ref[...] - high.astype(f32)).astype(jnp.bfloat16)
        out_ref[b] = mat(picker(tb), high, ((1,), (0,))) + mat(picker(tb), low, ((1,), (0,)))

def scan_outputs(step, push, write, read, rate, first):
    rows, length, chans = step.shape
    states = rate.shape[0]
    tb = min(TB, length)
    big = pl.BlockSpec((rows, tb, chans), lambda i: (0, i, 0))
    thin = pl.BlockSpec((rows, states, tb), lambda i: (0, 0, i))
    whole = pl.BlockSpec((rows, states, chans), lambda i: (0, 0, 0))
    return pl.pallas_call(outputs_kernel, grid=(length // tb,),
        in_specs=[big, big, thin, thin, pl.BlockSpec((states, chans), lambda i: (0, 0)), whole],
        out_specs=[big, pl.BlockSpec((rows, 1, states, chans), lambda i: (0, i, 0, 0))],
        out_shape=[jax.ShapeDtypeStruct((rows, length, chans), f32),
                   jax.ShapeDtypeStruct((rows, length // tb, states, chans), f32)],
        scratch_shapes=[pltpu.VMEM((rows, states, chans), f32), pltpu.VMEM((tb * 8, chans), f32)],
        cost_estimate=cost(21), compiler_params=params())(step, push, write, read, rate, first)

def tail_kernel(step_ref, grad_ref, read_ref, rate_ref, end_ref):
    rows, tb = step_ref.shape[0], step_ref.shape[1]
    @pl.when(pl.program_id(0) == 0)
    def _():
        end_ref[...] = jnp.zeros_like(end_ref)
    def group(j, held):
        base = pl.multiple_of(tb - UNROLL - j * UNROLL, UNROLL)
        held = list(held)
        for b in range(rows):
            steps = step_ref[b, pl.ds(base, UNROLL), :]
            grads = grad_ref[b, pl.ds(base, UNROLL), :]
            reads = turned(read_ref, b, base, tb)
            for k in range(UNROLL - 1, -1, -1):
                factor = jnp.exp2(steps[k:k+1] * rate_ref[...])
                held[b] = factor * (held[b] + reads[:, k:k+1] * grads[k:k+1])
        return tuple(held)
    held = lax.fori_loop(0, tb // UNROLL, group, tuple(end_ref[b] for b in range(rows)))
    for b in range(rows):
        end_ref[b] = held[b]

def scan_tail(step, grad, read, rate):
    rows, length, chans = step.shape
    states = rate.shape[0]
    tb = min(TB, length)
    n = length // tb
    big = pl.BlockSpec((rows, tb, chans), lambda i: (0, n - 1 - i, 0))
    thin = pl.BlockSpec((rows, states, tb), lambda i: (0, 0, n - 1 - i))
    return pl.pallas_call(tail_kernel, grid=(n,),
        in_specs=[big, big, thin, pl.BlockSpec((states, chans), lambda i: (0, 0))],
        out_specs=pl.BlockSpec((rows, states, chans), lambda i: (0, 0, 0)),
        out_shape=jax.ShapeDtypeStruct((rows, states, chans), f32),
        cost_estimate=cost(12), compiler_params=params())(step, grad, read, rate)

def back_kernel(step_ref, push_ref, grad_ref, write_ref, read_ref, rate_ref, start_ref, later_ref,
                decay_ref, weight_ref, gwrite_ref, gread_ref, grate_ref,
                carry_ref, factor_sc, kept_sc, decay_sc, weight_sc, gwrite_sc, gread_sc):
    rows, tb = step_ref.shape[0], step_ref.shape[1]
    states = rate_ref.shape[0]
    @pl.when(pl.program_id(0) == 0)
    def _():
        carry_ref[...] = later_ref[...]
        grate_ref[...] = jnp.zeros_like(grate_ref)
    for b in range(rows):
        def redo(j, held):
            base = pl.multiple_of(j * UNROLL, UNROLL)
            steps = step_ref[b, pl.ds(base, UNROLL), :]
            pushes = push_ref[b, pl.ds(base, UNROLL), :]
            writes = turned(write_ref, b, base, tb)
            for k in range(UNROLL):
                factor = jnp.exp2(steps[k:k+1] * rate_ref[...])
                kept = factor * held
                factor_sc[base + k] = factor
                kept_sc[base + k] = kept
                held = kept + writes[:, k:k+1] * pushes[k:k+1]
            return held
        lax.fori_loop(0, tb // UNROLL, redo, start_ref[b, 0])
        def group(j, carried):
            carry, total = carried
            base = pl.multiple_of(tb - UNROLL_BACK - j * UNROLL_BACK, UNROLL_BACK)
            steps = step_ref[b, pl.ds(base, UNROLL_BACK), :]
            pushes = push_ref[b, pl.ds(base, UNROLL_BACK), :]
            grads = grad_ref[b, pl.ds(base, UNROLL_BACK), :]
            writes = turned(write_ref, b, base, tb)
            reads = turned(read_ref, b, base, tb)
            for k in range(UNROLL_BACK - 1, -1, -1):
                kept = kept_sc[base + k]
                adjoint = reads[:, k:k+1] * grads[k:k+1] + carry
                carry = factor_sc[base + k] * adjoint
                weighted = adjoint * kept
                total = total + weighted * steps[k:k+1]
                eight = pl.ds(pl.multiple_of((base + k) * 8, 8), 8)
                decay_sc[eight, :] = folded(weighted * rate_ref[...])
                weight_sc[eight, :] = folded(adjoint * writes[:, k:k+1])
                wide = pl.ds(pl.multiple_of((base + k) * states, states), states)
                gwrite_sc[wide, :] = across(adjoint * pushes[k:k+1])
                gread_sc[wide, :] = across(kept * grads[k:k+1])
            return (carry, total)
        carry, total = lax.fori_loop(0, tb // UNROLL_BACK, group, (carry_ref[b], grate_ref[...]))
        grate_ref[...] = total
        carry_ref[b] = carry
        pick = picker(tb)
        decay_ref[b] = mat(pick, decay_sc[...].astype(jnp.bfloat16), ((1,), (0,)))
        weight_ref[b] = mat(pick, weight_sc[...].astype(jnp.bfloat16), ((1,), (0,)))
        ones = jnp.ones((8, 128), jnp.bfloat16)
        gwrite_ref[b] = mat(ones, gwrite_sc[...].astype(jnp.bfloat16), ((1,), (1,)))[:1]
        gread_ref[b] = mat(ones, gread_sc[...].astype(jnp.bfloat16), ((1,), (1,)))[:1]

def scan_back(step, push, grad, write, read, rate, starts, later):
    rows, length, chans = step.shape
    states = rate.shape[0]
    tb = min(TB, length)
    n = length // tb
    big = pl.BlockSpec((rows, tb, chans), lambda i: (0, n - 1 - i, 0))
    thin = pl.BlockSpec((rows, states, tb), lambda i: (0, 0, n - 1 - i))
    line = pl.BlockSpec((rows, 1, tb * states), lambda i: (0, 0, n - 1 - i))
    whole = pl.BlockSpec((rows, states, chans), lambda i: (0, 0, 0))
    flat = pl.BlockSpec((states, chans), lambda i: (0, 0))
    return pl.pallas_call(back_kernel, grid=(n,),
        in_specs=[big, big, big, thin, thin, flat, pl.BlockSpec((rows, 1, states, chans), lambda i: (0, n - 1 - i, 0, 0)), whole],
        out_specs=[big, big, line, line, flat],
        out_shape=[jax.ShapeDtypeStruct((rows, length, chans), f32)] * 2
                 + [jax.ShapeDtypeStruct((rows, 1, length * states), f32)] * 2
                 + [jax.ShapeDtypeStruct((states, chans), f32)],
        scratch_shapes=[pltpu.VMEM((rows, states, chans), f32),
                        pltpu.VMEM((tb, states, chans), f32),
                        pltpu.VMEM((tb, states, chans), f32),
                        pltpu.VMEM((tb * 8, chans), f32),
                        pltpu.VMEM((tb * 8, chans), f32),
                        pltpu.VMEM((tb * states, 128), f32),
                        pltpu.VMEM((tb * states, 128), f32)],
        cost_estimate=cost(46), compiler_params=params())(step, push, grad, write, read, rate, starts, later)


def mixer_forward(normed, weights, same, flags, late):
    (
        mixer_in,
        conv_taps,
        conv_bias,
        state_proj,
        step_proj,
        step_bias,
        decay_log,
        skip_gain,
        mixer_out,
    ) = weights
    both = jnp.einsum("rtd,dce->rtce", normed, mixer_in, preferred_element_type=jnp.float32)
    signal = both[:, :, 0].astype(jnp.bfloat16)
    gate = both[:, :, 1]
    taps = conv_taps.shape[0]
    length = signal.shape[1]
    rows = signal.shape[0]
    tail = from_behind(signal[:, length - (taps - 1) :], "seq", 1)
    widened = jnp.concatenate([tail, signal], axis=1).astype(jnp.float32)
    conv_sum = conv_bias + jnp.zeros_like(gate)
    for tap in range(taps):
        conv_sum = (
            conv_sum + conv_taps[tap] * widened[:, tap : tap + length] * same[:, :, tap : tap + 1]
        )
    inner = jax.nn.silu(conv_sum).astype(jnp.bfloat16)
    source = inner.astype(jnp.float32)
    mixed, hop = channel_total(
        jnp.einsum("rte,ec->rtc", inner, state_proj, preferred_element_type=jnp.float32)
    )
    late = gather_rows(nudged(late, hop))
    rank = step_proj.shape[0]
    states = decay_log.shape[0]
    step_low = mixed[:, :, :rank]
    write_in = mixed[:, :, rank : rank + states].astype(jnp.float32)
    read_out = mixed[:, :, rank + states :].astype(jnp.float32)
    step_raw = (
        jnp.einsum("rtk,ke->rte", step_low, step_proj, preferred_element_type=jnp.float32)
        + step_bias
    )
    step = jax.nn.softplus(step_raw)
    rate = -jnp.exp(decay_log)
    step_far = jnp.where(flags[:, :, None] > 0, FAR, step)
    push = step * source
    write_cols = jnp.swapaxes(write_in, 1, 2)
    read_cols = jnp.swapaxes(read_out, 1, 2)
    ends = scan_ends(step_far, push, write_cols, rate * LOG2E)
    span = jnp.where(jnp.max(flags, axis=1)[:, None] > 0, FAR, jnp.sum(step, axis=1))
    incoming = carried_in(ends, span, rate, "seq", False)
    scanned, firsts = scan_outputs(
        step_far, push, write_cols, read_cols, rate * LOG2E, incoming
    )
    result = scanned + skip_gain * source
    gated = (result * jax.nn.silu(gate)).astype(jnp.bfloat16)
    partial_value = jnp.einsum("rte,ed->rtd", gated, mixer_out, preferred_element_type=jnp.float32)
    cache = (
        normed,
        widened,
        gate,
        conv_sum,
        inner,
        source,
        step_low,
        step_raw,
        step,
        step_far,
        push,
        write_in,
        write_cols,
        read_cols,
        result,
        gated,
        firsts,
        span,
    )
    return (partial_value, cache, late)


def mixer_backward(grad_branch, cache, weights, same, flags, first, branch):
    (
        mixer_in,
        conv_taps,
        conv_bias,
        state_proj,
        step_proj,
        step_bias,
        decay_log,
        skip_gain,
        mixer_out,
    ) = weights
    (
        normed,
        widened,
        gate,
        conv_sum,
        inner,
        source,
        step_low,
        step_raw,
        step,
        step_far,
        push,
        write_in,
        write_cols,
        read_cols,
        result,
        gated,
        firsts,
        span,
    ) = cache
    grad_gated = jnp.einsum(
        "rtd,ed->rte", grad_branch, mixer_out, preferred_element_type=jnp.float32
    )
    grad_mixer_out = jnp.einsum(
        "rtd,rte->de", grad_branch, gated, preferred_element_type=jnp.float32
    )
    first_out = plane_first(grad_mixer_out)
    grad_gated = after(grad_gated, first)
    grad_result = grad_gated * jax.nn.silu(gate)
    grad_gate = grad_gated * result * silu_slope(gate)
    grad_skip = jnp.sum(grad_result * source, axis=(0, 1))
    rate = -jnp.exp(decay_log)
    tail = scan_tail(step_far, grad_result, read_cols, rate * LOG2E)
    second_out = plane_second(*first_out)
    first = [plane_third(held, tail) for held in first]
    first, arrived = ([pair[0] for pair in first], [pair[1] for pair in first])
    later = carried_in(tail, span, rate, "seq", True)
    decays, weights_back, write_back, read_back, grad_rate = scan_back(
        step_far, push, grad_result, write_cols, read_cols, rate * LOG2E, firsts, later
    )
    grad_mixer_out, _ = plane_third(second_out, grad_rate)
    grad_step = decays * (1.0 / LOG2E) + weights_back * source
    grad_source = weights_back * step
    grad_write = write_back.reshape(write_in.shape)
    grad_read = read_back.reshape(write_in.shape) + write_in * jnp.sum(
        push * grad_result, axis=2, keepdims=True
    )
    grad_source = grad_source + skip_gain * grad_result
    grad_step_raw = (grad_step * jax.nn.sigmoid(step_raw)).astype(jnp.bfloat16)
    grad_step_bias = jnp.sum(grad_step_raw.astype(jnp.float32), axis=(0, 1))
    grad_step_proj = jnp.einsum(
        "rtk,rte->ke", step_low, grad_step_raw, preferred_element_type=jnp.float32
    )
    grad_low = jnp.einsum(
        "rte,ke->rtk", grad_step_raw, step_proj, preferred_element_type=jnp.float32
    )
    grad_mixed, _ = channel_total(
        jnp.concatenate([after(grad_low, arrived, branch), grad_write, grad_read], axis=-1)
    )
    grad_state_proj = jnp.einsum(
        "rte,rtc->ce", inner, grad_mixed, preferred_element_type=jnp.float32
    )
    spread = jnp.einsum("rtc,ec->rte", grad_mixed, state_proj, preferred_element_type=jnp.float32)
    grad_source = grad_source + after(spread, first_out[0])
    grad_conv = grad_source * silu_slope(conv_sum)
    length = grad_conv.shape[1]
    taps = conv_taps.shape[0]
    reach = taps - 1
    terms = [grad_conv * same[:, :, tap : tap + 1] for tap in range(taps)]
    grad_taps = [
        jnp.sum(widened[:, tap : tap + length] * terms[tap], axis=(0, 1)) for tap in range(taps)
    ]
    grad_conv_bias = jnp.sum(grad_conv, axis=(0, 1))
    heads = [conv_taps[tap] * terms[tap][:, :reach] for tap in range(taps)]
    head = sum(
        jnp.pad(heads[tap][:, : reach - tap], ((0, 0), (tap, 0), (0, 0))) for tap in range(reach)
    )
    returned = from_behind(head, "seq", -1)
    grad_signal = jnp.pad(returned, ((0, 0), (length - reach, 0), (0, 0)))
    for tap in range(taps):
        shift = reach - tap
        grad_signal = grad_signal + conv_taps[tap] * jnp.pad(
            terms[tap][:, shift:], ((0, 0), (0, shift), (0, 0))
        )
    grad_both = jnp.stack([grad_signal, grad_gate], axis=2).astype(jnp.bfloat16)
    grad_mixer_in = jnp.einsum(
        "rtd,rtce->dce", normed, grad_both, preferred_element_type=jnp.float32
    )
    grad_normed = jnp.einsum(
        "rtce,dce->rtd", grad_both, mixer_in, preferred_element_type=jnp.float32
    )
    small = (
        jnp.stack(grad_taps),
        grad_conv_bias[None],
        grad_state_proj,
        grad_step_proj,
        grad_step_bias[None],
        grad_rate * rate,
        grad_skip[None],
    )
    return (grad_normed, grad_mixer_in, grad_mixer_out, small, first, second_out)


def dense_forward(normed, dense_in, dense_out):
    both = jnp.einsum(
        "rtd,dcf->rtcf", normed, dense_in, preferred_element_type=jnp.float32
    ).astype(jnp.bfloat16)
    gate = both[:, :, 0]
    upper = both[:, :, 1]
    hidden = jax.nn.silu(gate.astype(jnp.float32)) * upper.astype(jnp.float32)
    hidden = hidden.astype(jnp.bfloat16)
    partial_value = jnp.einsum("rtf,fd->rtd", hidden, dense_out, preferred_element_type=jnp.float32)
    return (partial_value, (normed, gate, upper, hidden))


def dense_backward(grad_branch, cache, dense_in, dense_out, event=()):
    normed, gate, upper, hidden = cache
    gate, upper = (gate.astype(jnp.float32), upper.astype(jnp.float32))
    grad_hidden = jnp.einsum(
        "rtd,fd->rtf", grad_branch, dense_out, preferred_element_type=jnp.float32
    )
    grad_hidden = after(grad_hidden, event)
    grad_gate = grad_hidden * upper * silu_slope(gate)
    grad_upper = grad_hidden * jax.nn.silu(gate)
    grad_both = jnp.stack([grad_gate, grad_upper], axis=2).astype(jnp.bfloat16)
    grad_normed = jnp.einsum(
        "rtcf,dcf->rtd", grad_both, dense_in, preferred_element_type=jnp.float32
    )
    grad_dense_out = jnp.einsum(
        "rtd,rtf->df", grad_branch, hidden, preferred_element_type=jnp.float32
    )
    grad_dense_in = jnp.einsum(
        "rtd,rtcf->dcf", normed, grad_both, preferred_element_type=jnp.float32
    )
    return (grad_normed, [plane_first(grad_dense_in), plane_first(grad_dense_out)])


def plan_of(length):
    block = min(QBLOCK, length)
    return (block, (WINDOW + block) // block)


def lower_edge(info_ref, row, first, block):
    lane = lax.broadcasted_iota(jnp.int32, (1, block), 1)
    place = info_ref[row, 0] + first + lane
    start = jnp.zeros((1, block), jnp.int32)
    for index in range(1, info_ref.shape[1]):
        entry = info_ref[row, index]
        start = jnp.maximum(start, jnp.where(entry <= place, entry, 0))
    return (jnp.maximum(lane + 1, start - (info_ref[row, 0] + first - WINDOW)), lane)


def piece_mask(low, lane, piece, block, pieces):
    index = piece * block + lax.broadcasted_iota(jnp.int32, (block, block), 0)
    allowed = index >= low
    if piece == pieces - 1:
        allowed = allowed & (index <= lane + WINDOW)
    return allowed


NT = (((1,), (1,)), ((), ()))
TN = (((0,), (0,)), ((), ()))
NN = (((1,), (0,)), ((), ()))


def dot(left, right, dims):
    return lax.dot_general(left, right, dims, preferred_element_type=f32)


def gathered_pieces(refs, wide):
    length = refs[0].shape[1]
    for index, ref in enumerate(refs):
        wide[pl.ds(index * length, length), :] = ref[0]


def attend_kernel(
    pieces, skip, info_ref, query_ref, second_ref, first_ref, own_ref, out_ref, total_ref, wide, held
):
    block = query_ref.shape[1]

    @pl.when(pl.program_id(1) == 0)
    def _():
        gathered_pieces((second_ref, first_ref, own_ref), wide)

    first = pl.multiple_of(pl.program_id(1) * block, block)
    low, lane = lower_edge(info_ref, pl.program_id(0), first, block)
    query = query_ref[0]
    top = jnp.full((1, block), masked_score, f32)
    for piece in range(pieces):
        at = pl.ds(pl.multiple_of(first + skip + piece * block, block), block)
        scores = dot(wide[at, :HDIM], query, NT)
        scores = jnp.where(piece_mask(low, lane, piece, block, pieces), scores, masked_score)
        held[piece] = scores
        top = jnp.maximum(top, jnp.max(scores, axis=0, keepdims=True))
    slope = HDIM ** (-0.5) * LOG2E
    total = jnp.zeros((1, block), f32)
    summed = jnp.zeros((HDIM, block), f32)
    for piece in range(pieces):
        at = pl.ds(pl.multiple_of(first + skip + piece * block, block), block)
        soft = jnp.exp2((held[piece] - top) * slope)
        total = total + jnp.sum(soft, axis=0, keepdims=True)
        summed = summed + dot(wide[at, HDIM:], soft.astype(jnp.bfloat16), TN)
    out_ref[0] = (summed / total).T.astype(jnp.bfloat16)
    total_ref[0] = top * slope + jnp.log2(total)


def head_specs(query, head):
    rows, length = (query.shape[0], query.shape[1])
    block, pieces = plan_of(length)
    halo = pl.BlockSpec((1, length, 2 * HDIM), lambda i, j: (i, 0, 0))
    own = pl.BlockSpec((1, length, 2 * HDIM), lambda i, j: (i, 0, head))
    narrow = pl.BlockSpec((1, block, HDIM), lambda i, j: (i, j, head))
    plain = pl.BlockSpec((1, block, HDIM), lambda i, j: (i, j, 0))
    line = pl.BlockSpec((1, 1, block), lambda i, j: (i, 0, j))
    skip = 2 * length - WINDOW
    return (rows, length, block, pieces, skip, halo, own, narrow, plain, line)


def attend(info, query, seconds, firsts, pairs, head):
    rows, length, block, pieces, skip, halo, own, narrow, plain, line = head_specs(query, head)
    body = lambda *refs: attend_kernel(pieces, skip, *refs)
    return pl.pallas_call(
        body,
        grid=(rows, length // block),
        in_specs=[pl.BlockSpec(memory_space=pltpu.SMEM), narrow, halo, halo, own],
        out_specs=[plain, line],
        out_shape=[
            jax.ShapeDtypeStruct((rows, length, HDIM), jnp.bfloat16),
            jax.ShapeDtypeStruct((rows, 1, length), f32),
        ],
        scratch_shapes=[
            pltpu.VMEM((3 * length, 2 * HDIM), jnp.bfloat16),
            pltpu.VMEM((pieces, block, block), f32),
        ],
        cost_estimate=cost(7),
        compiler_params=pltpu.CompilerParams(vmem_limit_bytes=VM),
    )(info, query, seconds, firsts, pairs)


def attend_back_kernel(
    pieces, skip, info_ref, query_ref, grad_ref, second_ref, first_ref, own_ref, total_ref, done_ref,
    gquery_ref, gsecond_ref, gfirst_ref, gown_ref, wide, gkeys, gvalues,
):
    block, length = (query_ref.shape[1], own_ref.shape[1])
    first = pl.multiple_of(pl.program_id(1) * block, block)
    low, lane = lower_edge(info_ref, pl.program_id(0), first, block)

    @pl.when(pl.program_id(1) == 0)
    def _():
        gathered_pieces((second_ref, first_ref, own_ref), wide)
        gkeys[...] = jnp.zeros_like(gkeys)
        gvalues[...] = jnp.zeros_like(gvalues)

    query, grad = (query_ref[0], grad_ref[0])
    total = total_ref[0]
    both = grad.astype(f32) * done_ref[0].astype(f32)
    delta = lax.dot_general(
        jnp.ones((8, HDIM), f32), both, NT, precision=lax.Precision.HIGHEST
    )[:1]
    slope = HDIM ** (-0.5) * LOG2E
    summed = jnp.zeros((HDIM, block), f32)
    for piece in range(pieces):
        at = pl.ds(pl.multiple_of(first + skip + piece * block, block), block)
        keys = wide[at, :HDIM]
        scores = dot(keys, query, NT)
        allowed = piece_mask(low, lane, piece, block, pieces)
        soft = jnp.exp2(jnp.where(allowed, scores * slope - total, masked_score))
        gvalues[at, :] += dot(soft.astype(jnp.bfloat16), grad, NN)
        spread = soft * (dot(wide[at, HDIM:], grad, NT) - delta)
        spread = spread.astype(jnp.bfloat16)
        gkeys[at, :] += dot(spread, query, NN)
        summed = summed + dot(keys, spread, TN)
    gquery_ref[0] = (summed * HDIM ** (-0.5)).T.astype(jnp.bfloat16)

    @pl.when(pl.program_id(1) == pl.num_programs(1) - 1)
    def _():
        for index, ref in enumerate((gsecond_ref, gfirst_ref, gown_ref)):
            at = pl.ds(index * length, length)
            ref[0, :, :HDIM] = (gkeys[at, :] * HDIM ** (-0.5)).astype(ref.dtype)
            ref[0, :, HDIM:] = gvalues[at, :].astype(ref.dtype)


def attend_back(info, query, grad, seconds, firsts, pairs, total, attended, head):
    rows, length, block, pieces, skip, halo, own, narrow, plain, line = head_specs(query, head)
    body = lambda *refs: attend_back_kernel(pieces, skip, *refs)
    double = (rows, length, 2 * HDIM)
    return pl.pallas_call(
        body,
        grid=(rows, length // block),
        in_specs=[
            pl.BlockSpec(memory_space=pltpu.SMEM),
            narrow,
            narrow,
            halo,
            halo,
            own,
            line,
            narrow,
        ],
        out_specs=[plain, halo, halo, halo],
        out_shape=[
            jax.ShapeDtypeStruct((rows, length, HDIM), jnp.bfloat16),
            jax.ShapeDtypeStruct(double, f32),
            jax.ShapeDtypeStruct(double, jnp.bfloat16),
            jax.ShapeDtypeStruct(double, f32),
        ],
        scratch_shapes=[
            pltpu.VMEM((3 * length, 2 * HDIM), jnp.bfloat16),
            pltpu.VMEM((3 * length, HDIM), f32),
            pltpu.VMEM((3 * length, HDIM), f32),
        ],
        cost_estimate=cost(12),
        compiler_params=pltpu.CompilerParams(vmem_limit_bytes=VM),
    )(info, query, grad, seconds, firsts, pairs, total, attended)


def by_head(attend_in):
    features, heads = (attend_in.shape[0], attend_in.shape[2] // HDIM)
    split = attend_in.reshape(features, 3, heads, HDIM)
    pairs = jnp.swapaxes(split[:, 1:], 1, 2).reshape(features, 2 * heads * HDIM)
    return (attend_in[:, 0], pairs)


def attention_forward(normed, attend_in, attend_out, info):
    heads = attend_in.shape[2] // HDIM
    weight_query, weight_pairs = by_head(attend_in)
    pairs = rowwise(
        jnp.einsum(
            "rtd,dh->rth", normed, weight_pairs, preferred_element_type=jnp.float32
        ).astype(jnp.bfloat16)
    )
    query = rowwise(
        jnp.einsum(
            "rtd,dh->rth", normed, weight_query, preferred_element_type=jnp.float32
        ).astype(jnp.bfloat16)
    )
    odd = lax.axis_index("seq") % 2 == 1
    halos, results, mark = ([], [], ())
    for head in range(heads):
        own = rowwise(pairs[:, :, 2 * head * HDIM : 2 * (head + 1) * HDIM])
        seconds = rowwise(from_behind(own, "seq", 2))
        handed = rowwise(jnp.where(odd, after(seconds, mark), own))
        firsts = rowwise(partner(handed, "seq", 1))
        halos.append((seconds, firsts))
        results.append(attend(info, query, seconds, firsts, pairs, head))
        mark = results[-1][0]
    attended = rowwise(jnp.concatenate([result[0] for result in results], axis=2))
    totals = [result[1] for result in results]
    partial_value = jnp.einsum(
        "rth,hd->rtd", attended, attend_out, preferred_element_type=jnp.float32
    )
    return (partial_value, (normed, query, pairs, halos, attended, totals, weight_query, weight_pairs))


def attention_backward(grad_branch, cache, attend_in, attend_out, info, event):
    normed, query, own_pairs, halos, attended, totals, weight_query, weight_pairs = cache
    rows, length = (query.shape[0], query.shape[1])
    heads = query.shape[2] // HDIM
    grad_attended = jnp.einsum(
        "rtd,hd->rth", grad_branch, attend_out, preferred_element_type=jnp.float32
    )
    grad_attended = rowwise(after(grad_attended, event).astype(jnp.bfloat16))
    grad_attend_out = jnp.einsum(
        "rtd,rth->dh", grad_branch, attended, preferred_element_type=jnp.float32
    )
    odd = lax.axis_index("seq") % 2 == 1
    queries, pairs, marks = ([], [], [[], []])
    for head in range(heads):
        grad_query, second, given, own = attend_back(
            after(info, marks[head]),
            query,
            grad_attended,
            *halos[head],
            own_pairs,
            totals[head],
            attended,
            head,
        )
        queries.append(grad_query)
        given = rowwise(partner(given, "seq", 1)).astype(jnp.float32)
        sent = rowwise((second + jnp.where(odd, given, 0.0)).astype(jnp.bfloat16))
        marks.append(sent)
        back = rowwise(from_behind(sent, "seq", -2))
        pairs.append((own + jnp.where(odd, 0.0, given) + back.astype(jnp.float32)).astype(jnp.bfloat16))
    grad_projected = rowwise(jnp.concatenate(queries + pairs, axis=2))
    grad_weight = jnp.einsum(
        "rtd,rth->dh", normed, grad_projected, preferred_element_type=jnp.float32
    )
    flat = jnp.concatenate([weight_query, weight_pairs], axis=1)
    grad_normed = jnp.einsum(
        "rth,dh->rtd", grad_projected, flat, preferred_element_type=jnp.float32
    )
    return (grad_normed, [plane_first(grad_weight), plane_first(grad_attend_out)])


def in_order(grad_weight, heads):
    features = grad_weight.shape[0]
    query = grad_weight[:, : heads * HDIM].reshape(features, 1, heads, HDIM)
    pairs = grad_weight[:, heads * HDIM :].reshape(features, heads, 2, HDIM)
    both = jnp.concatenate([query, jnp.swapaxes(pairs, 1, 2)], axis=1)
    return both.reshape(features, 3, heads * HDIM)


def shards(
    block_in,
    block_grad,
    norm_gains,
    mixer_in,
    conv_taps,
    conv_bias,
    state_proj,
    step_proj,
    step_bias,
    decay_log,
    skip_gain,
    mixer_out,
    first_in,
    first_out,
    attend_in,
    attend_out,
    second_in,
    second_out,
    row_counts,
    doc_starts,
    row_mask,
):
    local_len = block_in.shape[1]
    length = local_len * lax.axis_size("tp")
    anchor = lax.axis_index("seq") * length
    positions = anchor + jnp.arange(length, dtype=jnp.int32)
    own_place = anchor + lax.axis_index("tp") * local_len + jnp.arange(local_len, dtype=jnp.int32)
    valid = ((own_place[None, :] < row_counts[:, None]) & (row_mask[:, None] == 1)).astype(
        jnp.float32
    )[:, :, None]
    documents = doc_numbers(positions, doc_starts)
    flags = jnp.any(doc_starts[:, None, :] == positions[None, :, None], axis=-1).astype(jnp.float32)
    taps = conv_taps.shape[0]
    same = jnp.stack(
        [
            (
                (positions - (taps - 1 - tap) >= 0)[None, :]
                & (doc_numbers(positions - (taps - 1 - tap), doc_starts) == documents)
            ).astype(jnp.float32)
            for tap in range(taps)
        ],
        axis=-1,
    )
    here = jnp.broadcast_to(anchor, (doc_starts.shape[0], 1)).astype(jnp.int32)
    info = jnp.concatenate([here, doc_starts], axis=1)
    mixer_weights = (
        mixer_in,
        conv_taps,
        conv_bias,
        state_proj,
        step_proj,
        step_bias,
        decay_log,
        skip_gain,
        mixer_out,
    )
    grad_stream = rowwise(block_grad * valid)
    unit = block_in * lax.rsqrt(jnp.mean(block_in * block_in, axis=-1, keepdims=True) + epsilon)
    normed = (unit * norm_gains[0]).astype(jnp.bfloat16)
    gathered = gather_rows(normed)
    partial_value, cache_mix, grad_second = mixer_forward(
        gathered, mixer_weights, same, flags, grad_stream.astype(jnp.bfloat16)
    )
    stream_mix, normed = norm_forward(
        block_in, reduce_rows(partial_value, grad_second), norm_gains[1]
    )
    partial_value, cache_first = dense_forward(gather_rows(normed), first_in, first_out)
    stream_first, normed = norm_forward(stream_mix, reduce_rows(partial_value), norm_gains[2])
    partial_value, cache_attend = attention_forward(
        gather_rows(normed), attend_in, attend_out, info
    )
    stream_attend, normed = norm_forward(stream_first, reduce_rows(partial_value), norm_gains[3])
    partial_out, cache_second = dense_forward(
        gather_rows(normed), second_in, second_out
    )
    partial_out = partial_out.astype(jnp.bfloat16)

    def gain_of(which, low, cache):
        return gain_share(low, cache[0], norm_gains[which])

    grad_normed, firsts = dense_backward(grad_second, cache_second, second_in, second_out)
    low = grad_normed.astype(jnp.bfloat16)
    gain_four = gain_of(3, low, cache_second)
    grad_stream, grad_low = norm_backward(
        stream_attend,
        grad_stream,
        reduce_rows(low),
        after(norm_gains[3], firsts[0][0], firsts[1][0], gain_four, partial_out),
    )
    second = [plane_second(*pair) for pair in firsts]
    gathered = gather_rows(grad_low)
    grad_normed, firsts = attention_backward(
        gathered, cache_attend, attend_in, attend_out, info, second
    )
    low = grad_normed.astype(jnp.bfloat16)
    gain_three = gain_of(2, low, cache_attend)
    second = [plane_third(held, grad_normed)[0] for held in second]
    grad_stream, grad_low = norm_backward(
        stream_first,
        grad_stream,
        reduce_rows(low),
        after(norm_gains[2], firsts[0][0], firsts[1][0], second[0], second[1], gain_three),
    )
    middle = [plane_second(*pair) for pair in firsts]
    grad_normed, firsts = dense_backward(
        gather_rows(grad_low), cache_first, first_in, first_out, middle
    )
    middle = [plane_third(held)[0] for held in middle]
    low = grad_normed.astype(jnp.bfloat16)
    gain_two = gain_of(1, low, cache_first)
    grad_stream, grad_low = norm_backward(
        stream_mix,
        grad_stream,
        reduce_rows(low),
        after(norm_gains[1], firsts[0][0], firsts[1][0], middle[0], middle[1], gain_two),
    )
    firsts = [plane_second(*pair) for pair in firsts]
    gathered = gather_rows(grad_low)
    branch = reduce_rows(partial_out, gathered)
    block_out = (stream_attend + branch.astype(jnp.float32)) * valid
    grad_normed, grad_mixer_in, grad_mixer_out, small, first, second_out = mixer_backward(
        gathered,
        cache_mix,
        mixer_weights,
        same,
        flags,
        firsts,
        branch,
    )
    low = grad_normed.astype(jnp.bfloat16)
    gains = jnp.stack([gain_of(0, low, cache_mix), gain_two, gain_three, gain_four])
    parted = plane_first(grad_mixer_in)
    grad_normed = reduce_rows(low)
    wide = small[0].shape[1]
    small = small + (gains.reshape(-1, wide),)
    counts = [member.shape[0] for member in small]
    packed = after(jnp.concatenate(small), second_out)
    packed = spread_sum(packed, ("seq", "row"), jnp.bfloat16)
    parted = (after(parted[0], packed),) + parted[1:]
    grad_mixer_in = plane_halves(*parted)
    small, place = ([], 0)
    for count in counts:
        small.append(packed[place : place + count])
        place += count
    gains = spread_sum(small.pop(), ("tp",), jnp.float32).reshape(gains.shape)
    grad_stream, _ = norm_backward(block_in, grad_stream, grad_normed, norm_gains[0])
    middle[0] = in_order(middle[0], attend_in.shape[2] // HDIM)
    pairs = ((grad_mixer_in, grad_mixer_out), first, middle, second)
    flat = [member for pair in pairs for member in (pair[0], pair[1].T)]
    return (
        block_out,
        grad_stream,
        gains,
        flat[0],
        small[0],
        small[1][0],
        small[2].T,
        small[3],
        small[4][0],
        small[5],
        small[6][0],
        flat[1],
        flat[2],
        flat[3],
        flat[4],
        flat[5],
        flat[6],
        flat[7],
    )


def solution(mesh):
    in_specs = (
        P("row", ("seq", "tp"), None),
        P("row", ("seq", "tp"), None),
        P(),
        P(None, None, "tp"),
        P(None, "tp"),
        P("tp"),
        P("tp", None),
        P(None, "tp"),
        P("tp"),
        P(None, "tp"),
        P("tp"),
        P("tp", None),
        P(None, None, "tp"),
        P("tp", None),
        P(None, None, "tp"),
        P("tp", None),
        P(None, None, "tp"),
        P("tp", None),
        P("row"),
        P("row", None),
        P("row"),
    )
    out_specs = (
        P("row", ("seq", "tp"), None),
        P("row", ("seq", "tp"), None),
        P(),
        P(("row", "seq"), None, "tp"),
        P(None, "tp"),
        P("tp"),
        P("tp", None),
        P(None, "tp"),
        P("tp"),
        P(None, "tp"),
        P("tp"),
        P("tp", ("row", "seq")),
        P(("row", "seq"), None, "tp"),
        P("tp", ("row", "seq")),
        P(("row", "seq"), None, "tp"),
        P("tp", ("row", "seq")),
        P(("row", "seq"), None, "tp"),
        P("tp", ("row", "seq")),
    )
    return jax.shard_map(shards, mesh=mesh, in_specs=in_specs, out_specs=out_specs, check_vma=False)
```
